128 devices in a mesh: blk: 16 (over z, y), tok: 8 (over x, core).
Axes of the slice: x: 4, y: 4, z: 4, core: 2. Of those that a mesh axis runs over, the one named last changes fastest.
Arguments:
- inputs: bfloat16 [2048, 8, 2048], P('blk', 'tok'), may hold values from -6 to 6
- resets: int32 [2048, 8], P(None, 'tok'), may hold values from 0 to 1, as said below
- gain_rec: float32 [2048], replicated, may hold values from 0.5 to 1.5
- w_branch: bfloat16 [2048, 2560], P('tok', 'blk'), may hold values from -0.125 to 0.125
- w_gelu: bfloat16 [2048, 2560], P('tok', 'blk'), may hold values from -0.125 to 0.125
- conv_weight: float32 [4, 2560], P(None, 'blk'), may hold values from -3 to 3
- conv_bias: float32 [2560], P('blk'), may hold values from -1.5 to 1.5
- gate_a_weight: bfloat16 [16, 160, 160], P('blk'), may hold values from -0.5 to 0.5
- gate_a_bias: float32 [2560], P('blk'), may hold values from -2.5 to 2.5
- gate_x_weight: bfloat16 [16, 160, 160], P('blk'), may hold values from -0.5 to 0.5
- gate_x_bias: float32 [2560], P('blk'), may hold values from -2.5 to 2.5
- decay_param: float32 [2560], P('blk'), may hold values from 3.5 to 9
- w_out: bfloat16 [2048, 2560], P('tok', 'blk'), may hold values from -0.3125 to 0.3125
- gain_mlp: float32 [2048], replicated, may hold values from 0.5 to 1.5
- w_gate: bfloat16 [2048, 6144], P('tok', 'blk'), may hold values from -0.125 to 0.125
- w_up: bfloat16 [2048, 6144], P('tok', 'blk'), may hold values from -0.125 to 0.125
- w_down: bfloat16 [2048, 6144], P('tok', 'blk'), may hold values from -0.15625 to 0.15625
- cotangent: bfloat16 [2048, 8, 2048], P('blk', 'tok'), may hold values from -6 to 6
Outputs:
- output: bfloat16 [2048, 8, 2048], P('blk', 'tok')
- grad_inputs: float32 [2048, 8, 2048], P('blk', 'tok')
- grad_gain_rec: float32 [2048], replicated
- grad_w_branch: float32 [2048, 2560], P('tok', 'blk')
- grad_w_gelu: float32 [2048, 2560], P('tok', 'blk')
- grad_conv_weight: float32 [4, 2560], P(None, 'blk')
- grad_conv_bias: float32 [2560], P('blk')
- grad_gate_a_weight: float32 [16, 160, 160], P('blk')
- grad_gate_a_bias: float32 [2560], P('blk')
- grad_gate_x_weight: float32 [16, 160, 160], P('blk')
- grad_gate_x_bias: float32 [2560], P('blk')
- grad_decay_param: float32 [2560], P('blk')
- grad_w_out: float32 [2048, 2560], P('tok', 'blk')
- grad_gain_mlp: float32 [2048], replicated
- grad_w_gate: float32 [2048, 6144], P('tok', 'blk')
- grad_w_up: float32 [2048, 6144], P('tok', 'blk')
- grad_w_down: float32 [2048, 6144], P('tok', 'blk')
The draws below stay inside these ranges and needn't reach their ends.
Inputs may be any that keep to these rules, and one draw needn't show every extreme that they name: `resets`: position 0 of every sequence is 1. Among the 1 sequence held by one index of tok, one has no 1 at positions 128 to 1919.
All inputs are finite; a program needn't handle non-finite values.
Results may differ from the reference program's by a relative error of at most 0.028.
Values may be sent and summed in bfloat16 or wider, within the bound.
A program may use at most 256 MiB of HBM per device.

```python
import jax
import jax.numpy as jnp
from jax import lax

D = 2048
R = 2560
F = 6144
H = 16
CONV = 4
LENGTH = 2048
SEQS = 1
NSEQ = 8
TOK_SHARD = 128
BW = 160


def draw_resets(key, part):
    key = jax.random.fold_in(key, 11)
    pick_key, flag_key = jax.random.split(key)
    chosen = jax.random.randint(pick_key, (NSEQ // SEQS,), 0, SEQS)
    sequence = jnp.arange(NSEQ)
    long_seq = sequence % SEQS == chosen[sequence // SEQS]
    position = jnp.arange(LENGTH)[:, None]
    at_edge = (position < TOK_SHARD) | (position >= LENGTH - TOK_SHARD)
    level = jnp.where(long_seq[None, :], jnp.where(at_edge, 256, 0), max(8192 // LENGTH, 1))
    draws = jax.random.randint(flag_key, (LENGTH, NSEQ), 0, 1024)
    flags = (draws < level) | (position == 0)
    return flags.astype(jnp.int32)


def draw_decay_param(key, part):
    key = jax.random.fold_in(key, 23)
    return jax.random.uniform(key, (R,), jnp.float32, 3.5, 9.0)


def level_of(own_key, shape, cuts, least, high):
    level = 1.0
    for dim, shards_of in cuts:
        steps = jax.random.uniform(jax.random.fold_in(jax.random.fold_in(own_key, 6), dim), (shards_of,), jnp.float32, least / len(cuts), high / len(cuts))
        level = level * jnp.repeat(jnp.exp(steps), shape[dim] // shards_of).reshape((-1,) + (1,) * (len(shape) - 1 - dim))
    return level


def gaussian(key, extent, scale, limit, shards=(), kind=jnp.bfloat16):
    drawn = scale * jax.random.normal(key, extent, jnp.float32)
    if shards:
        drawn = drawn * level_of(key, extent, shards, -0.22, 0.18)
    return jnp.clip(drawn, -limit, limit).astype(kind)


def setup_inputs(seed: int = 0) -> dict:
    key_list = jax.random.split(jax.random.key(seed), 19)
    return {
        "inputs": gaussian(key_list[0], (LENGTH, NSEQ, D), 1.0, 6.0, ((0, 16), (1, 8))),
        "resets": draw_resets(jax.random.fold_in(key_list[18], 71), 0),
        "gain_rec": jnp.clip(1.0 + 0.1 * jax.random.normal(key_list[2], (D,), jnp.float32), 0.5, 1.5),
        "w_branch": gaussian(key_list[3], (D, R), D ** -0.5, 0.125, ((0, 8), (1, 16))),
        "w_gelu": gaussian(key_list[4], (D, R), D ** -0.5, 0.125, ((0, 8), (1, 16))),
        "conv_weight": gaussian(key_list[5], (CONV, R), 0.5, 3.0, ((1, 16),), jnp.float32),
        "conv_bias": gaussian(key_list[6], (R,), 0.3, 1.5, ((0, 16),), jnp.float32),
        "gate_a_weight": gaussian(key_list[7], (H, BW, BW), BW ** -0.5, 0.5, ((0, 16),)),
        "gate_a_bias": gaussian(key_list[8], (R,), 0.5, 2.5, ((0, 16),), jnp.float32),
        "gate_x_weight": gaussian(key_list[9], (H, BW, BW), BW ** -0.5, 0.5, ((0, 16),)),
        "gate_x_bias": gaussian(key_list[10], (R,), 0.5, 2.5, ((0, 16),), jnp.float32),
        "decay_param": draw_decay_param(jax.random.fold_in(key_list[18], 71), 0),
        "w_out": gaussian(key_list[12], (D, R), (R // 8) ** -0.5, 0.3125, ((0, 8), (1, 16))),
        "gain_mlp": jnp.clip(1.0 + 0.1 * jax.random.normal(key_list[13], (D,), jnp.float32), 0.5, 1.5),
        "w_gate": gaussian(key_list[14], (D, F), D ** -0.5, 0.125, ((0, 8), (1, 16))),
        "w_up": gaussian(key_list[15], (D, F), D ** -0.5, 0.125, ((0, 8), (1, 16))),
        "w_down": gaussian(key_list[16], (D, F), (F // 4) ** -0.5, 0.15625, ((0, 8), (1, 16))),
        "cotangent": gaussian(key_list[17], (LENGTH, NSEQ, D), 1.0, 6.0, ((0, 16), (1, 8))),
    }


EPSILON = 1e-06
PRECISE = lax.Precision.HIGHEST

@jax.custom_vjp
def low(v):
    return lax.optimization_barrier(v.astype(jnp.bfloat16)).astype(jnp.float32)

@jax.custom_vjp
def low_back(v):
    return v

def low_keep(v):
    return (low(v), None)

def low_pass(kept, grad):
    return (grad,)

def back_keep(v):
    return (v, None)

def back_low(kept, grad):
    return (low(grad),)
low.defvjp(low_keep, low_pass)
low_back.defvjp(back_keep, back_low)

def matmul_full(left, right):
    return jnp.dot(left, right, precision=PRECISE)

def matmul_back(left, right):
    return lax.dot_general(left, right, (((1,), (1,)), ((), ())), precision=PRECISE)

def rms_scale(values, gain_vector):
    return values * lax.rsqrt(lax.optimization_barrier(jnp.mean(values * values, axis=-1, keepdims=True)) + EPSILON) * gain_vector

def causal_conv(branch, conv_weight, conv_bias, document):
    length = branch.shape[0]
    total = conv_bias + conv_weight[0] * branch
    for offset in range(1, conv_weight.shape[0]):
        moved = jnp.pad(branch[:length - offset], ((offset, 0), (0, 0), (0, 0)))
        moved_doc = jnp.pad(document[:length - offset], ((offset, 0), (0, 0)), constant_values=-1)
        same_doc = (moved_doc == document).astype(branch.dtype)[:, :, None]
        total = total + conv_weight[offset] * moved * same_doc
    return total

def block_mix(values, weight):
    length, seq_count, channels = values.shape
    blocks, block_size, _ = weight.shape
    split_up = values.reshape(length, seq_count, blocks, block_size)
    mixed_out = jnp.einsum('lshi,hij->lshj', split_up, weight, precision=PRECISE)
    return mixed_out.reshape(length, seq_count, channels)

def recurrence(conv_out, pre_rate, pre_admit, rate_bias, admit_bias, decay_param, resets):
    rate_gate = jax.nn.sigmoid(pre_rate + rate_bias)
    admit_gate = jax.nn.sigmoid(pre_admit + admit_bias)
    log_decay = -8.0 * rate_gate * jax.nn.softplus(-decay_param)
    restart = (resets == 1)[:, :, None]
    decay_rate = jnp.where(restart, 0.0, jnp.exp(log_decay))
    scaling = jnp.where(restart, 1.0, jnp.sqrt(-jnp.expm1(2.0 * log_decay)))
    driven = scaling * admit_gate * conv_out

    def combine(earlier, later):
        return (earlier[0] * later[0], later[0] * earlier[1] + later[1])
    return lax.associative_scan(combine, (decay_rate, driven), axis=0)[1]

def layer(values, resets, params):
    gain_rec, w_branch, w_gelu, conv_weight, conv_bias, gate_a_weight, gate_a_bias, gate_x_weight, gate_x_bias, decay_param, w_out, gain_mlp, w_gate, w_up, w_down = params
    length, seq_count, model_width = values.shape
    flat = values.reshape(length * seq_count, model_width)
    normed = low(rms_scale(flat, gain_rec))
    branch = low_back(matmul_full(normed, w_branch))
    gelu_pre = low_back(matmul_full(normed, w_gelu))
    document = jnp.cumsum(resets, axis=0).astype(jnp.int32)
    conv_out = causal_conv(branch.reshape(length, seq_count, -1), conv_weight, conv_bias, document)
    conv_low = low(conv_out)
    pre_rate = low_back(block_mix(conv_low, gate_a_weight))
    pre_admit = low_back(block_mix(conv_low, gate_x_weight))
    states = recurrence(conv_out, pre_rate, pre_admit, gate_a_bias, gate_x_bias, decay_param, resets)
    gated = low(states.reshape(length * seq_count, -1) * jax.nn.gelu(gelu_pre))
    mixed_rows = flat + low_back(matmul_back(gated, w_out))
    normed_mlp = low(rms_scale(mixed_rows, gain_mlp))
    gate_pre = low_back(matmul_full(normed_mlp, w_gate))
    up_pre = low_back(matmul_full(normed_mlp, w_up))
    hidden = low(jax.nn.gelu(gate_pre) * up_pre)
    result = mixed_rows + low_back(matmul_back(hidden, w_down))
    return result.reshape(length, seq_count, model_width)

def reference(inputs, resets, gain_rec, w_branch, w_gelu, conv_weight, conv_bias, gate_a_weight, gate_a_bias, gate_x_weight, gate_x_bias, decay_param, w_out, gain_mlp, w_gate, w_up, w_down, cotangent):
    params = tuple((argument.astype(jnp.float32) for argument in (gain_rec, w_branch, w_gelu, conv_weight, conv_bias, gate_a_weight, gate_a_bias, gate_x_weight, gate_x_bias, decay_param, w_out, gain_mlp, w_gate, w_up, w_down)))
    length, seq_total, model_width = inputs.shape
    groups = seq_total // 2

    def regroup(array):
        return jnp.moveaxis(array.reshape((length, groups, 2) + array.shape[2:]), 1, 0)
    values_all = regroup(inputs.astype(jnp.float32))
    resets_all = regroup(resets)
    cotangent_all = regroup(cotangent.astype(jnp.float32))

    def one_group(totals, pieces):
        values, reset_piece, cot_piece = pieces
        result, pullback = jax.vjp(lambda weights, token_rows: layer(token_rows, reset_piece, weights), params, values)
        weight_grads, grad_rows = pullback(cot_piece)
        return (jax.tree.map(jnp.add, totals, weight_grads), (result, grad_rows))
    zero_grads = jax.tree.map(jnp.zeros_like, params)
    totals, (results, grad_rows) = lax.scan(one_group, zero_grads, (values_all, resets_all, cotangent_all))

    def ungroup(array):
        return jnp.moveaxis(array, 0, 1).reshape(length, seq_total, model_width)
    return (ungroup(results).astype(jnp.bfloat16), ungroup(grad_rows), totals[0], totals[1], totals[2], totals[3], totals[4], totals[5], totals[6], totals[7], totals[8], totals[9], totals[10], totals[11], totals[12], totals[13], totals[14])
```

```python
import functools
import math

import jax
import jax.numpy as jnp
from jax import lax
from jax.experimental import pallas as pl
from jax.experimental.pallas import tpu as pltpu
from jax.sharding import Mesh
from jax.sharding import PartitionSpec as P

EPSILON = 1e-06
MESH = pl.DeviceIdType.MESH
AXES = ("z", "y", "x", "core")
GELU_A = math.sqrt(2.0 / math.pi)
GELU_B = 0.044715
F32 = jnp.float32
BF16 = jnp.bfloat16


def dot_nn(left, right):
    return lax.dot_general(left, right, (((1,), (0,)), ((), ())), preferred_element_type=F32)


def dot_nt(left, right):
    return lax.dot_general(left, right, (((1,), (1,)), ((), ())), preferred_element_type=F32)


def dot_tn(left, right):
    return lax.dot_general(left, right, (((0,), (0,)), ((), ())), preferred_element_type=F32)


def gelu_parts(v):
    t = jnp.tanh(GELU_A * (v + GELU_B * v * v * v))
    return 0.5 * v * (1.0 + t), t


def gelu_slope(v, t):
    return 0.5 * (1.0 + t) + 0.5 * v * (1.0 - t * t) * (GELU_A * (1.0 + 3.0 * GELU_B * v * v))


def one_minus_exp(v):
    series = 1.0 + v * (1.0 / 9.0)
    for order in (8.0, 7.0, 6.0, 5.0, 4.0, 3.0, 2.0):
        series = 1.0 + v * (1.0 / order) * series
    return jnp.where(v > -0.5, -v * series, 1.0 - jnp.exp(v))


def around(axis, size, step):
    return {axis: lax.rem(lax.axis_index(axis) + (step + size), size)}


ROWS = 32
LANES = 128


def put(ref, here, value):
    for c in range(ref.shape[0]):
        ref[c, here, :] = value[:, c * LANES : (c + 1) * LANES]


def take(ref, here):
    return jnp.concatenate([ref[c, here, :] for c in range(ref.shape[0])], axis=1)


def forward_kernel(
    z_size,
    branch_in,
    gelu_in,
    masks,
    gate_a,
    gate_x,
    params,
    branch_out,
    conv_out,
    rate_out,
    admit_out,
    states_out,
    gated_out,
    enter_out,
    low,
    decay,
    local,
    product,
    totals,
    halo_sems,
    total_send,
    total_recv,
):
    rows, channels = branch_in.shape
    seg = rows // 8
    z = lax.axis_index("z")
    barrier = pltpu.get_barrier_semaphore()
    for step in range(1, z_size):
        pl.semaphore_signal(barrier, inc=1, device_id=around("z", z_size, step), device_id_type=MESH)
    pl.semaphore_wait(barrier, z_size - 1)
    halo = pltpu.make_async_remote_copy(
        src_ref=branch_in.at[pl.ds(rows - 8, 8)],
        dst_ref=branch_out.at[pl.ds(0, 8)],
        send_sem=halo_sems.at[0],
        recv_sem=halo_sems.at[1],
        device_id=around("z", z_size, 1),
        device_id_type=MESH,
    )
    halo.start()

    def move(i, carry):
        at = pl.multiple_of(i * ROWS, ROWS)
        branch_out[pl.ds(at + 8, ROWS), :] = branch_in[pl.ds(at, ROWS), :]
        return carry

    lax.fori_loop(0, rows // ROWS, move, 0)
    halo.wait()

    def conv(i, carry):
        at = pl.multiple_of(i * ROWS, ROWS)
        window = branch_out[pl.ds(at, ROWS + 8), :]
        mask = masks[pl.ds(at, ROWS), :]
        total = params[4:5, :] + params[0:1, :] * window[8:, :]
        for k in range(1, 4):
            total = total + params[k : k + 1, :] * window[8 - k : 8 - k + ROWS, :] * mask[:, k : k + 1]
        conv_out[pl.ds(at, ROWS), :] = total
        low[pl.ds(at, ROWS), :] = total.astype(BF16)
        return carry

    lax.fori_loop(0, rows // ROWS, conv, 0)

    def gates(i, carry):
        at = pl.multiple_of(i * 128, 128)
        rate_out[pl.ds(at, 128), :] = dot_nn(low[pl.ds(at, 128), :], gate_a[...])
        admit_out[pl.ds(at, 128), :] = dot_nn(low[pl.ds(at, 128), :], gate_x[...])
        return carry

    lax.fori_loop(0, rows // 128, gates, 0)

    def point(i, carry):
        at = pl.multiple_of(i * ROWS, ROWS)
        here = pl.ds(at, ROWS)
        restart = masks[here, 0:1] > 0.5
        rate = jax.nn.sigmoid(rate_out[here, :] + params[5:6, :])
        admit = jax.nn.sigmoid(admit_out[here, :] + params[6:7, :])
        log_decay = -8.0 * rate * params[8:9, :]
        scaling = jnp.where(restart, 1.0, jnp.sqrt(one_minus_exp(2.0 * log_decay)))
        rate_out[here, :] = rate
        admit_out[here, :] = admit
        put(decay, here, jnp.where(restart, 0.0, jnp.exp(log_decay)))
        put(local, here, scaling * admit * conv_out[here, :])
        return carry

    lax.fori_loop(0, rows // ROWS, point, 0)

    def scan(j, carry):
        state, prod = carry
        here = pl.ds(j, 8, stride=seg)
        rate = take(decay, here)
        state = rate * state + take(local, here)
        prod = prod * rate
        put(local, here, state)
        put(product, here, prod)
        return state, prod

    state, prod = lax.fori_loop(
        0, seg, scan, (jnp.zeros((8, channels), F32), jnp.ones((8, channels), F32))
    )

    def segments(entering):
        found = [entering]
        for s in range(8):
            found.append(prod[s : s + 1, :] * found[-1] + state[s : s + 1, :])
        return found

    whole = prod[0:1, :]
    for s in range(1, 8):
        whole = whole * prod[s : s + 1, :]
    totals[0, 0:1, :] = whole
    totals[0, 1:2, :] = segments(jnp.zeros((1, channels), F32))[-1]
    copies = []
    for step in range(1, z_size):
        copy = pltpu.make_async_remote_copy(
            src_ref=totals.at[0],
            dst_ref=totals.at[step],
            send_sem=total_send.at[step],
            recv_sem=total_recv.at[step],
            device_id=around("z", z_size, step),
            device_id_type=MESH,
        )
        copy.start()
        copies.append(copy)
    for copy in copies:
        copy.wait()
    entering = jnp.zeros((1, channels), F32)
    for step in range(z_size - 1, 0, -1):
        later = totals[step, 0:1, :] * entering + totals[step, 1:2, :]
        entering = jnp.where(z - step >= 0, later, entering)
    enter_out[...] = jnp.broadcast_to(entering, (8, channels))
    found = segments(entering)
    for s in range(8):
        base = s * seg

        def fix(i, carry):
            at = pl.multiple_of(base + i * ROWS, ROWS)
            here = pl.ds(at, ROWS)
            states = take(local, here) + take(product, here) * found[s]
            states_out[here, :] = states
            gated_out[here, :] = (states * gelu_parts(gelu_in[here, :])[0]).astype(BF16)
            return carry

        lax.fori_loop(0, seg // ROWS, fix, 0)


def backward_kernel(
    z_size,
    g_gated,
    gelu_in,
    branch_in,
    conv_in,
    rate_in,
    admit_in,
    states_in,
    enter_in,
    masks,
    gate_a,
    gate_x,
    params,
    g_gelu_out,
    g_branch_out,
    rate_low,
    admit_low,
    conv_low,
    small_out,
    decay,
    local,
    product,
    conv_grad,
    totals,
    halo_sems,
    total_send,
    total_recv,
):
    rows, channels = g_gated.shape
    seg = rows // 8
    z = lax.axis_index("z")
    barrier = pltpu.get_barrier_semaphore()
    for step in range(1, z_size):
        pl.semaphore_signal(barrier, inc=1, device_id=around("z", z_size, step), device_id_type=MESH)
    pl.semaphore_wait(barrier, z_size - 1)

    def point(i, carry):
        at = pl.multiple_of(i * ROWS, ROWS)
        here = pl.ds(at, ROWS)
        restart = masks[here, 0:1] > 0.5
        grads = g_gated[here, :]
        value, tang = gelu_parts(gelu_in[here, :])
        g_gelu_out[here, :] = (grads * states_in[here, :] * gelu_slope(gelu_in[here, :], tang)).astype(BF16)
        put(local, here, grads * value)
        put(decay, here, jnp.where(restart, 0.0, jnp.exp(-8.0 * rate_in[here, :] * params[8:9, :])))
        return carry

    lax.fori_loop(0, rows // ROWS, point, 0)

    def scan(i, carry):
        j = seg - 1 - i
        coming, prod = carry
        here = pl.ds(j, 8, stride=seg)
        rate = take(decay, here)
        total = take(local, here) + coming
        put(local, here, total)
        put(product, here, prod)
        return rate * total, prod * rate

    coming, prod = lax.fori_loop(
        0, seg, scan, (jnp.zeros((8, channels), F32), jnp.ones((8, channels), F32))
    )

    def segments(entering):
        found = [None] * 8 + [entering]
        for s in range(7, -1, -1):
            found[s] = prod[s : s + 1, :] * found[s + 1] + coming[s : s + 1, :]
        return found

    whole = prod[0:1, :]
    for s in range(1, 8):
        whole = whole * prod[s : s + 1, :]
    totals[0, 0:1, :] = whole
    totals[0, 1:2, :] = segments(jnp.zeros((1, channels), F32))[0]
    copies = []
    for step in range(1, z_size):
        copy = pltpu.make_async_remote_copy(
            src_ref=totals.at[0],
            dst_ref=totals.at[step],
            send_sem=total_send.at[step],
            recv_sem=total_recv.at[step],
            device_id=around("z", z_size, -step),
            device_id_type=MESH,
        )
        copy.start()
        copies.append(copy)
    for copy in copies:
        copy.wait()
    entering = jnp.zeros((1, channels), F32)
    for step in range(z_size - 1, 0, -1):
        later = totals[step, 0:1, :] * entering + totals[step, 1:2, :]
        entering = jnp.where(z + step < z_size, later, entering)
    found = segments(entering)
    sums = (jnp.zeros((1, channels), F32),) * 3
    for s in range(8):
        base = s * seg
        before_first = enter_in[0:1, :] if s == 0 else states_in[base - 1 : base, :]

        def fix(i, carry):
            rate_sum, admit_sum, decay_sum, before_block = carry
            at = pl.multiple_of(base + i * ROWS, ROWS)
            here = pl.ds(at, ROWS)
            running = masks[here, 0:1] < 0.5
            states = states_in[here, :]
            before = jnp.concatenate([before_block, states[: ROWS - 1, :]], axis=0)
            carried = take(local, here) + take(product, here) * found[s + 1]
            rate = rate_in[here, :]
            admit = admit_in[here, :]
            conv = conv_in[here, :]
            spread = take(decay, here)
            scaling = jnp.where(running, jnp.sqrt(one_minus_exp(-16.0 * rate * params[8:9, :])), 1.0)
            driven = admit * conv
            g_log = jnp.where(
                running, carried * (before * spread - driven * spread * spread / scaling), 0.0
            )
            g_rate = g_log * (-8.0 * params[8:9, :]) * rate * (1.0 - rate)
            scaled = carried * scaling * admit
            g_admit = scaled * conv * (1.0 - admit)
            rate_low[here, :] = g_rate.astype(BF16)
            admit_low[here, :] = g_admit.astype(BF16)
            conv_low[here, :] = conv.astype(BF16)
            conv_grad[here, :] = scaled
            return (
                rate_sum + jnp.sum(g_rate, axis=0, keepdims=True),
                admit_sum + jnp.sum(g_admit, axis=0, keepdims=True),
                decay_sum + jnp.sum(g_log * rate, axis=0, keepdims=True),
                states[ROWS - 1 :, :],
            )

        result = lax.fori_loop(0, seg // ROWS, fix, sums + (before_first,))
        sums = result[:3]

    def gates(i, carry):
        at = pl.multiple_of(i * 128, 128)
        here = pl.ds(at, 128)
        conv_grad[here, :] = (
            conv_grad[here, :]
            + dot_nt(rate_low[here, :], gate_a[...])
            + dot_nt(admit_low[here, :], gate_x[...])
        )
        return carry

    lax.fori_loop(0, rows // 128, gates, 0)
    halo = pltpu.make_async_remote_copy(
        src_ref=conv_grad.at[pl.ds(0, 8)],
        dst_ref=conv_grad.at[pl.ds(rows, 8)],
        send_sem=halo_sems.at[0],
        recv_sem=halo_sems.at[1],
        device_id=around("z", z_size, -1),
        device_id_type=MESH,
    )
    halo.start()
    halo.wait()

    def conv(i, carry):
        at = pl.multiple_of(i * ROWS, ROWS)
        grads = conv_grad[pl.ds(at, ROWS + 8), :]
        mask = masks[pl.ds(at, ROWS + 8), :]
        window = branch_in[pl.ds(at, ROWS + 8), :]
        own = grads[:ROWS, :]
        total = params[0:1, :] * own
        new = [carry[0] + jnp.sum(own * window[8:, :], axis=0, keepdims=True)]
        for k in range(1, 4):
            held = grads * mask[:, k : k + 1]
            total = total + params[k : k + 1, :] * held[k : k + ROWS, :]
            new.append(
                carry[k] + jnp.sum(held[:ROWS, :] * window[8 - k : 8 - k + ROWS, :], axis=0, keepdims=True)
            )
        new.append(carry[4] + jnp.sum(own, axis=0, keepdims=True))
        g_branch_out[pl.ds(at, ROWS), :] = total.astype(BF16)
        return tuple(new)

    taps = lax.fori_loop(0, rows // ROWS, conv, (jnp.zeros((1, channels), F32),) * 5)
    for k in range(5):
        small_out[k : k + 1, :] = taps[k]
    small_out[5:6, :] = sums[0]
    small_out[6:7, :] = sums[1]
    small_out[7:8, :] = sums[2] * 8.0 * params[9:10, :]


def placed(step):
    return ((step % 4) * 2 + step // 4) * 256


class Links:
    def __init__(self, send, recv):
        self.send, self.recv, self.used = send, recv, 0

    def start(self, src, dst, axis, step):
        size = lax.axis_size(axis)
        copy = pltpu.make_async_remote_copy(
            src_ref=src,
            dst_ref=dst,
            send_sem=self.send.at[self.used],
            recv_sem=self.recv.at[self.used],
            device_id=around(axis, size, step),
            device_id_type=MESH,
        )
        self.used += 1
        copy.start()
        return copy

    def local(self, src, dst):
        copy = pltpu.make_async_copy(src, dst, self.send.at[self.used])
        self.used += 1
        copy.start()
        return copy


def greet(reach):
    barrier = pltpu.get_barrier_semaphore()
    total = 0
    for axis, steps in reach:
        for step in steps:
            pl.semaphore_signal(
                barrier, inc=1, device_id=around(axis, lax.axis_size(axis), step), device_id_type=MESH
            )
            total += 1
    pl.semaphore_wait(barrier, total)


EVERYONE = (("y", (1, 2, 3)), ("x", (1, 2, 3)), ("z", (1, 2, 3)), ("core", (1,)))


def run(*tasks):
    waiting = list(tasks)
    while waiting:
        for task in list(waiting):
            try:
                next(task)
            except StopIteration:
                waiting.remove(task)


def gather_weight(links, own, full):
    z, x, core = lax.axis_index("z"), lax.axis_index("x"), lax.axis_index("core")
    rows = own.shape[0]
    half = rows // 2
    mine = pl.ds(pl.multiple_of((core * 4 + x) * 256, 256), 256)
    ours = pl.ds(pl.multiple_of(core * 1024, 1024), 1024)
    top, low = pl.ds(0, half), pl.ds(half, rows - half)
    sent = []
    here = links.local(own, full.at[z, :, mine])
    first_a = [links.start(own.at[top], full.at[z, top, mine], "x", s) for s in (1, 3, 2)]
    first_b = [links.start(own.at[low], full.at[z, low, mine], "z", s) for s in (1, 3, 2)]
    sent += first_a + first_b
    yield
    here.wait()
    for copy in first_a:
        copy.wait_recv()
    block = full.at[z, top, ours]
    second_a = [links.start(block, block, "z", s) for s in (1, -1)]
    for copy in first_b:
        copy.wait_recv()
    block = full.at[:, low, mine]
    second_b = [links.start(block, block, "x", s) for s in (1, -1)]
    sent += second_a + second_b
    yield
    relays = []
    for way in (0, 1):
        step = 1 if way == 0 else -1
        origin = lax.rem(z - step + 4, 4)
        second_a[way].wait_recv()
        half_lanes = pl.ds(pl.multiple_of(core * 1024 + way * 512, 512), 512)
        block = full.at[origin, top, half_lanes]
        relays.append(links.start(block, block, "z", step))
        origin = lax.rem(x - step + 4, 4)
        second_b[way].wait_recv()
        lanes = pl.ds(pl.multiple_of((core * 4 + origin) * 256, 256), 256)
        block = full.at[pl.ds(2 * way, 2), low, lanes]
        relays.append(links.start(block, block, "x", step))
    sent += relays
    yield
    for copy in relays:
        copy.wait_recv()
    block = full.at[:, :, ours]
    last = links.start(block, block, "core", 1)
    sent.append(last)
    yield
    last.wait_recv()
    for copy in sent:
        copy.wait_send()


GATHER_SEMS = 16


def gather_rows(links, seq):
    y = lax.axis_index("y")
    own = seq.at[y]
    first = [links.start(own, own, "y", s) for s in (1, -1)]
    yield
    relays = []
    for way in (0, 1):
        step = 1 if way == 0 else -1
        first[way].wait_recv()
        block = seq.at[lax.rem(y - step + 4, 4), :, pl.ds(way * 1024, 1024)]
        relays.append(links.start(block, block, "y", step))
    yield
    for copy in relays:
        copy.wait_recv()
    for copy in first + relays:
        copy.wait_send()


def add_rows(out, terms, dtype=None):
    count = out.shape[0] // 16

    def body(i, carry):
        here = pl.ds(pl.multiple_of(i * 16, 16), 16)
        total = terms[0][here, :].astype(F32)
        for term in terms[1:]:
            total = total + term[here, :].astype(F32)
        out[here, :] = total.astype(out.dtype)
        return carry

    lax.fori_loop(0, count, body, 0)


def scatter_rows(links, part, far, near, out):
    y = lax.axis_index("y")
    across = part.at[lax.rem(y + 2, 4)]
    first = [
        links.start(across.at[:, pl.ds(way * 1024, 1024)], far.at[way], "y", 1 - 2 * way) for way in (0, 1)
    ]
    yield
    second = []
    for way in (0, 1):
        step = 1 - 2 * way
        first[way].wait_recv()
        chunk = part.at[lax.rem(y + step + 4, 4)]
        lanes = pl.ds(way * 1024, 1024)
        add_rows(chunk.at[:, lanes], [chunk.at[:, lanes], far.at[way]])
        second.append(links.start(chunk, near.at[way], "y", step))
    yield
    for copy in second:
        copy.wait_recv()
    add_rows(out, [part.at[y], near.at[0], near.at[1]])
    for copy in first + second:
        copy.wait_send()


def scatter_weight(links, part, own, mate, heavy_a, heavy_b, light_a, light_b, out):
    z, x, core = lax.axis_index("z"), lax.axis_index("x"), lax.axis_index("core")
    rows = part.shape[1]
    half = rows // 2
    top, low = pl.ds(0, half), pl.ds(half, rows - half)
    theirs = pl.ds(pl.multiple_of((1 - core) * 1024, 1024), 1024)
    ours = pl.ds(pl.multiple_of(core * 1024, 1024), 1024)
    here = links.local(part.at[:, :, ours], own)
    across = links.start(part.at[:, :, theirs], mate, "core", 1)
    yield
    here.wait()
    across.wait_recv()
    for block in range(4):
        add_rows(own.at[block], [own.at[block], mate.at[block]])
    first_a, first_b = [], []
    for i, step in enumerate((1, 3, 2)):
        to_z = lax.rem(z + step, 4)
        first_a.append(links.start(own.at[to_z, top, :], heavy_a.at[i], "z", step))
        to_x = pl.ds(pl.multiple_of(lax.rem(x + step, 4) * 256, 256), 256)
        first_b.append(links.start(own.at[:, low, to_x], heavy_b.at[i], "x", step))
    yield
    for copy in first_a:
        copy.wait_recv()
    mine_a = own.at[z, top, :]
    add_rows(mine_a, [mine_a] + [heavy_a.at[i] for i in range(3)])
    second = []
    for i, step in enumerate((1, 3, 2)):
        to_x = pl.ds(pl.multiple_of(lax.rem(x + step, 4) * 256, 256), 256)
        second.append(links.start(own.at[z, top, to_x], light_a.at[i], "x", step))
    for copy in first_b:
        copy.wait_recv()
    my_x = pl.ds(pl.multiple_of(x * 256, 256), 256)
    for block in range(4):
        mine_b = own.at[block, low, my_x]
        add_rows(mine_b, [mine_b] + [heavy_b.at[i, block] for i in range(3)])
    for i, step in enumerate((1, 3, 2)):
        to_z = lax.rem(z + step, 4)
        second.append(links.start(own.at[to_z, low, my_x], light_b.at[i], "z", step))
    yield
    for copy in second:
        copy.wait_recv()
    add_rows(out.at[top], [own.at[z, top, my_x]] + [light_a.at[i] for i in range(3)])
    add_rows(out.at[low], [own.at[z, low, my_x]] + [light_b.at[i] for i in range(3)])
    for copy in [across] + first_a + first_b + second:
        copy.wait_send()


SCATTER_SEMS = 16


def scatter_scratch(rows):
    half = rows // 2
    return [
        pltpu.VMEM((4, rows, 1024), BF16),
        pltpu.VMEM((4, rows, 1024), BF16),
        pltpu.VMEM((3, half, 1024), BF16),
        pltpu.VMEM((3, 4, half, 256), BF16),
        pltpu.VMEM((3, half, 256), BF16),
        pltpu.VMEM((3, half, 256), BF16),
    ]


def sum_everywhere(links, slots, axis):
    size = lax.axis_size(axis)
    own = slots.at[lax.axis_index(axis)]
    copies = [links.start(own, own, axis, s) for s in range(1, size)]
    yield
    for copy in copies:
        copy.wait_recv()
    for copy in copies:
        copy.wait_send()


STRIP = 16


def placed_rows(ref, here):
    return jnp.concatenate([ref[here, pl.ds(placed(p), 256)] for p in range(8)], axis=1)


def restore_rows(ref, here, value):
    for p in range(8):
        ref[here, pl.ds(placed(p), 256)] = value[:, p * 256 : (p + 1) * 256]


def strips(count, body, carry=0):
    def step(i, carry):
        return body(pl.ds(pl.multiple_of(i * STRIP, STRIP), STRIP), carry)

    return lax.fori_loop(0, count // STRIP, step, carry)


def inverse_rms(values):
    return lax.rsqrt(jnp.mean(values * values, axis=-1, keepdims=True) + EPSILON)


def norm_back(grads, values, scale, gain):
    held = grads * gain
    return scale * held - values * (scale * scale * scale) * jnp.mean(held * values, axis=-1, keepdims=True)


def first_kernel(widths, x_in, gain, weights, seq, branch, gelu, out, normed, send, recv):
    links = Links(send, recv)
    y = lax.axis_index("y")
    greet(EVERYONE)
    tasks, at = [], 0
    for full, width in zip((branch, gelu, out), widths):
        tasks.append(gather_weight(links, weights.at[pl.ds(at, width)], full))
        at += width

    def rows():
        gains = placed_rows(gain, slice(None))

        def body(here, carry):
            values = placed_rows(x_in, here).astype(F32)
            normed[here, :] = (values * inverse_rms(values) * gains).astype(BF16)
            return carry

        strips(x_in.shape[0], body)
        copy = links.local(normed, seq.at[y])
        copy.wait()
        yield from gather_rows(links, seq)

    run(*tasks, rows())


def middle_kernel(
    widths, skip, part, x_in, cot, gain, weights, mixed, seq_mlp, seq_grad, gate, up, down,
    far, near, normed, cot_placed, send, recv,
):
    links = Links(send, recv)
    y = lax.axis_index("y")
    count = x_in.shape[0]
    greet(EVERYONE)
    tasks, at = [], skip
    for full, width in zip((gate, up, down), widths):
        tasks.append(gather_weight(links, weights.at[pl.ds(at, width)], full))
        at += width

    def rows():
        yield from scatter_rows(links, part, far, near, mixed)
        gains = placed_rows(gain, slice(None))

        def body(here, carry):
            values = placed_rows(x_in, here).astype(F32) + mixed[here, :]
            mixed[here, :] = values
            normed[here, :] = (values * inverse_rms(values) * gains).astype(BF16)
            cot_placed[here, :] = placed_rows(cot, here)
            return carry

        strips(count, body)
        own_mlp = links.local(normed, seq_mlp.at[y])
        own_grad = links.local(cot_placed, seq_grad.at[y])
        own_mlp.wait()
        yield from gather_rows(links, seq_mlp)
        own_grad.wait()
        yield from gather_rows(links, seq_grad)

    run(rows(), *tasks)


def third_kernel(
    part_out, part_back, grad_gate, grad_up, grad_down, mixed, cot, gain,
    output, g_mixed, seq_mixed, gate_out, up_out, down_out, gain_out,
    far, near, total, low, far_out, near_out, *rest,
):
    send, recv = rest[-2:]
    links = Links(send, recv)
    y = lax.axis_index("y")
    count, model = mixed.shape
    greet(EVERYONE)
    tasks = []
    for i, (part, out) in enumerate(
        ((grad_down, down_out), (grad_gate, gate_out), (grad_up, up_out))
    ):
        tasks.append(scatter_weight(links, part, *rest[6 * i : 6 * i + 6], out))

    def rows():
        yield from scatter_rows(links, part_back, far, near, total)
        gains = placed_rows(gain, slice(None))

        def body(here, carry):
            values = mixed[here, :]
            back = total[here, :]
            scale = inverse_rms(values)
            grads = placed_rows(cot, here).astype(F32) + norm_back(back, values, scale, gains)
            g_mixed[here, :] = grads
            low[here, :] = grads.astype(BF16)
            return carry + jnp.sum(back * values * scale, axis=0, keepdims=True)

        sums = strips(count, body, jnp.zeros((1, model), F32))
        restore_rows(gain_out, slice(None), jnp.broadcast_to(sums, (8, model)))
        copy = links.local(low, seq_mixed.at[y])
        copy.wait()
        yield from gather_rows(links, seq_mixed)
        yield from scatter_rows(links, part_out, far_out, near_out, total)

        def last(here, carry):
            restore_rows(output, here, (mixed[here, :] + total[here, :]).astype(BF16))
            return carry

        strips(count, last)

    run(rows(), *tasks)


def fourth_kernel(
    part, grad_branch, grad_gelu, grad_out, g_mixed, x_in, gain, gain_mlp, small,
    g_inputs, branch_out, gelu_out, out_out, small_out, gain_out,
    far, near, total, small_z, small_x, small_core, gain_slots, *rest,
):
    send, recv = rest[-2:]
    links = Links(send, recv)
    count, model = g_mixed.shape
    greet(EVERYONE)
    tasks = []
    for i, (weight, out) in enumerate(
        ((grad_branch, branch_out), (grad_gelu, gelu_out), (grad_out, out_out))
    ):
        tasks.append(scatter_weight(links, weight, *rest[6 * i : 6 * i + 6], out))
    z, x, core = lax.axis_index("z"), lax.axis_index("x"), lax.axis_index("core")

    def smalls():
        copies = []
        for i, step in enumerate((1, 3, 2)):
            copies.append(links.start(small.at[lax.rem(z + step, 4)], small_z.at[i], "z", step))
        yield
        for copy in copies:
            copy.wait_recv()
        add_rows(small_x.at[x], [small.at[z]] + [small_z.at[i] for i in range(3)])
        yield from sum_everywhere(links, small_x, "x")
        add_rows(small_core.at[core], [small_x.at[i] for i in range(4)])
        yield from sum_everywhere(links, small_core, "core")
        add_rows(small_out, [small_core.at[0], small_core.at[1]])
        for copy in copies:
            copy.wait_send()

    def rows():
        yield from scatter_rows(links, part, far, near, total)
        gains = placed_rows(gain, slice(None))

        def body(here, carry):
            values = placed_rows(x_in, here).astype(F32)
            back = total[here, :]
            scale = inverse_rms(values)
            grads = g_mixed[here, :] + norm_back(back, values, scale, gains)
            restore_rows(g_inputs, here, grads)
            return carry + jnp.sum(back * values * scale, axis=0, keepdims=True)

        sums = strips(count, body, jnp.zeros((1, model), F32))
        restore_rows(gain_out, slice(0, 1), sums)
        gain_out[1:2, :] = gain_mlp[0:1, :]
        gain_out[2:8, :] = jnp.zeros((6, model), F32)
        for n, axis in enumerate(("y", "z", "x", "core")):
            size = lax.axis_size(axis)
            slots = gain_slots.at[n]
            slots[lax.axis_index(axis)] = gain_out[...]
            yield from sum_everywhere(links, slots.at[pl.ds(0, size)], axis)
            total_now = slots[0]
            for i in range(1, size):
                total_now = total_now + slots[i]
            gain_out[...] = total_now

    run(rows(), smalls(), *tasks)


def any_space(count):
    return [pl.BlockSpec(memory_space=pl.ANY)] * count


def vmem(count):
    return [pl.BlockSpec(memory_space=pltpu.VMEM)] * count


def shape(dims, dtype):
    return jax.ShapeDtypeStruct(dims, dtype)


def sems(count):
    return [pltpu.SemaphoreType.DMA((count,)), pltpu.SemaphoreType.DMA((count,))]


def options(number, mib=56):
    return pltpu.CompilerParams(
        collective_id=number, has_side_effects=True, vmem_limit_bytes=mib * 2**20
    )


def call_first(x_in, gain, weights, widths):
    count, model = x_in.shape
    return pl.pallas_call(
        functools.partial(first_kernel, widths),
        out_shape=[shape((4, count, model), BF16)] + [shape((4, w, model), BF16) for w in widths],
        in_specs=vmem(2) + any_space(1),
        out_specs=any_space(4),
        scratch_shapes=[pltpu.VMEM((count, model), BF16)] + sems(3 * GATHER_SEMS + 8),
        compiler_params=options(3),
    )(x_in, gain, weights)


def call_middle(part, x_in, cot, gain, weights, widths, skip):
    count, model = x_in.shape
    seq = shape((4, count, model), BF16)
    return pl.pallas_call(
        functools.partial(middle_kernel, widths, skip),
        out_shape=[shape((count, model), F32), seq, seq] + [shape((4, w, model), BF16) for w in widths],
        in_specs=vmem(4) + any_space(1),
        out_specs=vmem(1) + any_space(5),
        scratch_shapes=[
            pltpu.VMEM((2, count, model // 2), BF16),
            pltpu.VMEM((2, count, model), BF16),
            pltpu.VMEM((count, model), BF16),
            pltpu.VMEM((count, model), BF16),
        ]
        + sems(3 * GATHER_SEMS + 16),
        compiler_params=options(4),
    )(part, x_in, cot, gain, weights)


def call_third(part_out, part_back, grad_gate, grad_up, grad_down, mixed, cot, gain):
    count, model = mixed.shape
    width = grad_gate.shape[1]
    final = shape((width, 256), F32)
    return pl.pallas_call(
        third_kernel,
        out_shape=[
            shape((count, model), BF16),
            shape((count, model), F32),
            shape((4, count, model), BF16),
            final,
            final,
            final,
            shape((8, model), F32),
        ],
        in_specs=vmem(2) + any_space(3) + vmem(3),
        out_specs=vmem(2) + any_space(1) + vmem(4),
        scratch_shapes=[
            pltpu.VMEM((2, count, model // 2), BF16),
            pltpu.VMEM((2, count, model), BF16),
            pltpu.VMEM((count, model), F32),
            pltpu.VMEM((count, model), BF16),
            pltpu.VMEM((2, count, model // 2), BF16),
            pltpu.VMEM((2, count, model), BF16),
        ]
        + scatter_scratch(width) * 3
        + sems(3 * SCATTER_SEMS + 16),
        compiler_params=options(5),
    )(part_out, part_back, grad_gate, grad_up, grad_down, mixed, cot, gain)


def call_fourth(part, grad_branch, grad_gelu, grad_out, g_mixed, x_in, gain, gain_mlp, small):
    count, model = g_mixed.shape
    width = grad_out.shape[1]
    final = shape((width, 256), F32)
    packed = small.shape[1:]
    return pl.pallas_call(
        fourth_kernel,
        out_shape=[
            shape((count, model), F32),
            final,
            final,
            final,
            shape(packed, F32),
            shape((8, model), F32),
        ],
        in_specs=vmem(1) + any_space(3) + vmem(5),
        out_specs=vmem(6),
        scratch_shapes=[
            pltpu.VMEM((2, count, model // 2), BF16),
            pltpu.VMEM((2, count, model), BF16),
            pltpu.VMEM((count, model), F32),
            pltpu.VMEM((3,) + packed, BF16),
            pltpu.VMEM((4,) + packed, BF16),
            pltpu.VMEM((2,) + packed, BF16),
            pltpu.VMEM((4, 4, 8, model), F32),
        ]
        + scatter_scratch(width) * 3
        + sems(3 * SCATTER_SEMS + 32),
        compiler_params=options(6),
    )(part, grad_branch, grad_gelu, grad_out, g_mixed, x_in, gain, gain_mlp, small)


def recurrence_forward(branch, gelu_pre, masks, gate_a, gate_x, params):
    z_size = lax.axis_size("z")
    rows, channels = branch.shape
    wide = jax.ShapeDtypeStruct((rows, channels), F32)
    return pl.pallas_call(
        functools.partial(forward_kernel, z_size),
        out_shape=[
            jax.ShapeDtypeStruct((rows + 8, channels), F32),
            wide,
            wide,
            wide,
            wide,
            jax.ShapeDtypeStruct((rows, channels), BF16),
            jax.ShapeDtypeStruct((8, channels), F32),
        ],
        in_specs=vmem(6),
        out_specs=vmem(7),
        scratch_shapes=[
            pltpu.VMEM((rows, channels), BF16),
            pltpu.VMEM((channels // LANES, rows, LANES), F32),
            pltpu.VMEM((channels // LANES, rows, LANES), F32),
            pltpu.VMEM((channels // LANES, rows, LANES), F32),
            pltpu.VMEM((z_size, 8, channels), F32),
            pltpu.SemaphoreType.DMA((2,)),
            pltpu.SemaphoreType.DMA((z_size,)),
            pltpu.SemaphoreType.DMA((z_size,)),
        ],
        compiler_params=pltpu.CompilerParams(
            collective_id=1, has_side_effects=True, vmem_limit_bytes=48 * 2**20
        ),
    )(branch, gelu_pre, masks, gate_a, gate_x, params)


def recurrence_backward(g_gated, gelu_pre, branch, conv, rate, admit, states, enter, masks, gate_a, gate_x, params):
    z_size = lax.axis_size("z")
    rows, channels = g_gated.shape
    low = jax.ShapeDtypeStruct((rows, channels), BF16)
    return pl.pallas_call(
        functools.partial(backward_kernel, z_size),
        out_shape=[low, low, low, low, low, jax.ShapeDtypeStruct((8, channels), F32)],
        in_specs=vmem(12),
        out_specs=vmem(6),
        scratch_shapes=[
            pltpu.VMEM((channels // LANES, rows, LANES), F32),
            pltpu.VMEM((channels // LANES, rows, LANES), F32),
            pltpu.VMEM((channels // LANES, rows, LANES), F32),
            pltpu.VMEM((rows + 8, channels), F32),
            pltpu.VMEM((z_size, 8, channels), F32),
            pltpu.SemaphoreType.DMA((2,)),
            pltpu.SemaphoreType.DMA((z_size,)),
            pltpu.SemaphoreType.DMA((z_size,)),
        ],
        compiler_params=pltpu.CompilerParams(
            collective_id=2, has_side_effects=True, vmem_limit_bytes=48 * 2**20
        ),
    )(g_gated, gelu_pre, branch, conv, rate, admit, states, enter, masks, gate_a, gate_x, params)


def block_diagonal(blocks):
    count, size, _ = blocks.shape
    spread = blocks[:, :, None, :] * jnp.eye(count, dtype=blocks.dtype)[:, None, :, None]
    return spread.reshape(count * size, count * size)


def diagonal_blocks(square, count):
    size = square.shape[0] // count
    return jnp.stack([square[i * size : (i + 1) * size, i * size : (i + 1) * size] for i in range(count)])


def on_device(
    inputs,
    resets,
    gain_rec,
    w_branch,
    w_gelu,
    conv_weight,
    conv_bias,
    gate_a_weight,
    gate_a_bias,
    gate_x_weight,
    gate_x_bias,
    decay_param,
    w_out,
    gain_mlp,
    w_gate,
    w_up,
    w_down,
    cotangent,
):
    shard, _, model = inputs.shape
    z_size, y_size = lax.axis_size("z"), lax.axis_size("y")
    z = lax.axis_index("z")
    rows = shard * y_size
    length = resets.shape[0]
    flags = jnp.pad(resets.reshape(length).astype(F32), (8, 8), constant_values=1.0)
    window = lax.dynamic_slice(flags, (z * rows,), (rows + 16,))
    keep = 1.0 - window
    first = keep[8:]
    second = first * keep[7:-1]
    third = second * keep[6:-2]
    masks = jnp.stack([window[8:], first, second, third] + [jnp.zeros_like(first)] * 4, axis=1)

    vectors = jnp.concatenate(
        [conv_weight, jnp.stack([conv_bias, gate_a_bias, gate_x_bias, decay_param])], axis=0
    )
    vectors = lax.all_gather(vectors, "z", axis=0).transpose(1, 0, 2).reshape(8, -1)
    soft = jax.nn.softplus(-vectors[7:8])
    slope = jax.nn.sigmoid(-vectors[7:8])
    params = jnp.concatenate([vectors, soft, slope, jnp.zeros((6, vectors.shape[1]), F32)], axis=0)
    gates = lax.all_gather(jnp.concatenate([gate_a_weight, gate_x_weight]), "z", axis=0)
    gate_a = block_diagonal(gates[:, 0])
    gate_x = block_diagonal(gates[:, 1])

    rec, mlp = w_branch.shape[1], w_gate.shape[1]
    weights = jnp.concatenate([w_branch, w_gelu, w_out, w_gate, w_up, w_down], axis=1).T
    gain_rec = gain_rec.reshape(1, model)
    gain_mlp = gain_mlp.reshape(1, model)

    def whole(parts):
        return parts.reshape(-1, parts.shape[-1])

    def split(full):
        return full.astype(BF16).reshape(y_size, -1, model)

    flat = inputs.reshape(shard, model)
    cot = cotangent.reshape(shard, model)
    seq_normed, full_branch, full_gelu, full_out = map(
        whole, call_first(flat, gain_rec, weights, (rec,) * 3)
    )
    branch = dot_nt(seq_normed, full_branch)
    gelu_pre = dot_nt(seq_normed, full_gelu)
    branch_held, conv, rate, admit, states, gated, enter = recurrence_forward(
        branch, gelu_pre, masks, gate_a, gate_x, params
    )
    mixed, seq_mlp, seq_grad, full_gate, full_up, full_down = map(
        whole,
        call_middle(
            split(dot_nn(gated, full_out)), flat, cot, gain_mlp, weights, (mlp,) * 3, 3 * rec
        ),
    )
    gate_pre = dot_nt(seq_mlp, full_gate)
    up_pre = dot_nt(seq_mlp, full_up)
    gate_value, gate_tang = gelu_parts(gate_pre)
    hidden = (gate_value * up_pre).astype(BF16)
    g_hidden = dot_nt(seq_grad, full_down)
    g_gate = (g_hidden * up_pre * gelu_slope(gate_pre, gate_tang)).astype(BF16)
    g_up = (g_hidden * gate_value).astype(BF16)
    part_out = split(dot_nn(hidden, full_down))
    part_back = split(dot_nn(g_gate, full_gate) + dot_nn(g_up, full_up))
    output, g_mixed, seq_mixed, grad_gate, grad_up, grad_down, gain_part = call_third(
        part_out,
        part_back,
        split(dot_tn(g_gate, seq_mlp)),
        split(dot_tn(g_up, seq_mlp)),
        split(dot_tn(hidden, seq_grad)),
        mixed,
        cot,
        gain_mlp,
    )
    seq_mixed = whole(seq_mixed)
    g_gated = dot_nt(seq_mixed, full_out)
    g_gelu, g_branch, rate_low, admit_low, conv_low, small = recurrence_backward(
        g_gated, gelu_pre, branch_held, conv, rate, admit, states, enter, masks, gate_a, gate_x, params
    )
    blocks_a = diagonal_blocks(dot_tn(conv_low, rate_low), z_size).reshape(z_size, -1)
    blocks_x = diagonal_blocks(dot_tn(conv_low, admit_low), z_size).reshape(z_size, -1)
    vectors_back = small.reshape(8, z_size, rec).transpose(1, 0, 2).reshape(z_size, -1)
    packed = jnp.concatenate([blocks_a, blocks_x, vectors_back], axis=1).astype(BF16)
    packed = jnp.pad(packed, ((0, 0), (0, -packed.shape[1] % 4096))).reshape(z_size, -1, 256)
    g_inputs, grad_branch, grad_gelu, grad_out, packed, gains = call_fourth(
        split(dot_nn(g_branch, full_branch) + dot_nn(g_gelu, full_gelu)),
        split(dot_tn(g_branch, seq_normed)),
        split(dot_tn(g_gelu, seq_normed)),
        split(dot_tn(gated, seq_mixed)),
        g_mixed,
        flat,
        gain_rec,
        gain_part,
        packed,
    )
    packed = packed.reshape(-1)
    block = rec * rec
    vector = packed[2 * block : 2 * block + 8 * rec].reshape(8, rec)
    return (
        output.reshape(shard, 1, model),
        g_inputs.reshape(shard, 1, model),
        gains[0],
        grad_branch.T,
        grad_gelu.T,
        vector[:4],
        vector[4],
        packed[:block].reshape(1, rec, rec),
        vector[5],
        packed[block : 2 * block].reshape(1, rec, rec),
        vector[6],
        vector[7],
        grad_out.T,
        gains[1],
        grad_gate.T,
        grad_up.T,
        grad_down.T,
    )


def solution(mesh):
    sizes = {"blk": mesh.shape["blk"], "tok": mesh.shape["tok"]}
    side = math.isqrt(sizes["blk"])
    grid = Mesh(mesh.devices.reshape(side, side, sizes["tok"] // 2, 2), AXES)
    blk, tok = ("z", "y"), ("x", "core")
    in_specs = (
        P(blk, tok, None),
        P(None, tok),
        P(),
        P(tok, blk),
        P(tok, blk),
        P(None, blk),
        P(blk),
        P(blk, None, None),
        P(blk),
        P(blk, None, None),
        P(blk),
        P(blk),
        P(tok, blk),
        P(),
        P(tok, blk),
        P(tok, blk),
        P(tok, blk),
        P(blk, tok, None),
    )
    out_specs = (
        P(blk, tok, None),
        P(blk, tok, None),
        P(),
        P(tok, blk),
        P(tok, blk),
        P(None, blk),
        P(blk),
        P(blk, None, None),
        P(blk),
        P(blk, None, None),
        P(blk),
        P(blk),
        P(tok, blk),
        P(),
        P(tok, blk),
        P(tok, blk),
        P(tok, blk),
    )
    return jax.shard_map(
        on_device, mesh=grid, in_specs=in_specs, out_specs=out_specs, check_vma=False
    )
```

```python
import functools
import math

import jax
import jax.numpy as jnp
from jax import lax
from jax.experimental import pallas as pl
from jax.experimental.pallas import tpu as pltpu
from jax.sharding import Mesh
from jax.sharding import PartitionSpec as P

EPSILON = 1e-06
MESH = pl.DeviceIdType.MESH
AXES = ("z", "y", "x", "core")
GELU_A = math.sqrt(2.0 / math.pi)
GELU_B = 0.044715
F32 = jnp.float32
BF16 = jnp.bfloat16
RING = 4
CHUNK = 128
STEPS = CHUNK // 8
LEAD = 24


def dot_nn(left, right):
    return lax.dot_general(left, right, (((1,), (0,)), ((), ())), preferred_element_type=F32)


def dot_nt(left, right):
    return lax.dot_general(left, right, (((1,), (1,)), ((), ())), preferred_element_type=F32)


def dot_tn(left, right):
    return lax.dot_general(left, right, (((0,), (0,)), ((), ())), preferred_element_type=F32)


def gelu_parts(v):
    t = jnp.tanh(GELU_A * (v + GELU_B * v * v * v))
    return 0.5 * v * (1.0 + t), t


def gelu_slope(v, t):
    return 0.5 * (1.0 + t) + 0.5 * v * (1.0 - t * t) * (GELU_A * (1.0 + 3.0 * GELU_B * v * v))


def one_minus_exp(v):
    series = 1.0 + v * (1.0 / 9.0)
    for order in (8.0, 7.0, 6.0, 5.0, 4.0, 3.0, 2.0):
        series = 1.0 + v * (1.0 / order) * series
    return jnp.where(v > -0.5, -v * series, 1.0 - jnp.exp(v))


def inverse_rms(values):
    return lax.rsqrt(jnp.mean(values * values, axis=-1, keepdims=True) + EPSILON)


def norm_back(grads, values, scale, gain):
    held = grads * gain
    return scale * held - values * (scale * scale * scale) * jnp.mean(held * values, axis=-1, keepdims=True)


def around(axis, size, step):
    return {axis: lax.rem(lax.axis_index(axis) + (step + size), size)}


def turned(index, step):
    return lax.rem(index + (step + RING), RING)


class Links:
    def __init__(self, send, recv):
        self.send, self.recv, self.used = send, recv, 0

    def start(self, src, dst, axis, step):
        copy = pltpu.make_async_remote_copy(
            src_ref=src,
            dst_ref=dst,
            send_sem=self.send.at[self.used],
            recv_sem=self.recv.at[self.used],
            device_id=around(axis, lax.axis_size(axis), step),
            device_id_type=MESH,
        )
        self.used += 1
        copy.start()
        return copy

    def local(self, src, dst):
        copy = pltpu.make_async_copy(src, dst, self.send.at[self.used])
        self.used += 1
        copy.start()
        return copy


def greet():
    barrier = pltpu.get_barrier_semaphore()
    total = 0
    for axis in AXES:
        size = lax.axis_size(axis)
        for step in range(1, size):
            pl.semaphore_signal(barrier, inc=1, device_id=around(axis, size, step), device_id_type=MESH)
            total += 1
    pl.semaphore_wait(barrier, total)


class Task:
    def __init__(self, stages):
        self.stages = stages

    def step(self):
        next(self.stages, None)

    def finish(self):
        for _ in self.stages:
            pass


def strips(count, body, carry=0, size=16):
    def step(i, carry):
        return body(pl.ds(pl.multiple_of(i * size, size), size), carry)

    return lax.fori_loop(0, count // size, step, carry)


def add_rows(out, terms):
    def body(here, carry):
        total = terms[0][here, :].astype(F32)
        for term in terms[1:]:
            total = total + term[here, :].astype(F32)
        out[here, :] = total.astype(out.dtype)
        return carry

    strips(out.shape[0], body)


def gather_weight(links, own, full):
    z, x, core = lax.axis_index("z"), lax.axis_index("x"), lax.axis_index("core")
    rows = own.shape[0]
    half = rows // 2
    mine = pl.ds(pl.multiple_of((core * 4 + x) * 256, 256), 256)
    ours = pl.ds(pl.multiple_of(core * 1024, 1024), 1024)
    top, low = pl.ds(0, half), pl.ds(half, rows - half)
    here = links.local(own, full.at[z, :, mine])
    first_a = [links.start(own.at[top], full.at[z, top, mine], "x", s) for s in (1, 3, 2)]
    first_b = [links.start(own.at[low], full.at[z, low, mine], "z", s) for s in (1, 3, 2)]
    yield
    here.wait()
    for copy in first_a:
        copy.wait_recv()
    block = full.at[z, top, ours]
    second_a = [links.start(block, block, "z", s) for s in (1, -1)]
    for copy in first_b:
        copy.wait_recv()
    block = full.at[:, low, mine]
    second_b = [links.start(block, block, "x", s) for s in (1, -1)]
    yield
    relays = []
    for way in (0, 1):
        step = 1 - 2 * way
        second_a[way].wait_recv()
        lanes = pl.ds(pl.multiple_of(core * 1024 + way * 512, 512), 512)
        block = full.at[turned(z, -step), top, lanes]
        relays.append(links.start(block, block, "z", step))
        second_b[way].wait_recv()
        lanes = pl.ds(pl.multiple_of((core * 4 + turned(x, -step)) * 256, 256), 256)
        block = full.at[pl.ds(2 * way, 2), low, lanes]
        relays.append(links.start(block, block, "x", step))
    yield
    for copy in relays:
        copy.wait_recv()
    block = full.at[:, :, ours]
    last = links.start(block, block, "core", 1)
    yield
    last.wait_recv()
    for copy in first_a + first_b + second_a + second_b + relays + [last]:
        copy.wait_send()


def gather_rows(links, seq):
    y = lax.axis_index("y")
    own = seq.at[y]
    first = [links.start(own, own, "y", s) for s in (1, -1)]
    yield
    relays = []
    for way in (0, 1):
        step = 1 - 2 * way
        first[way].wait_recv()
        block = seq.at[turned(y, -step), :, pl.ds(way * 1024, 1024)]
        relays.append(links.start(block, block, "y", step))
    yield
    for copy in relays:
        copy.wait_recv()
    for copy in first + relays:
        copy.wait_send()


def scatter_rows(links, produce, part, far, near, out):
    y = lax.axis_index("y")
    across = turned(y, 2)
    produce(across)
    first = [
        links.start(part.at[across, :, pl.ds(way * 1024, 1024)], far.at[way], "y", 1 - 2 * way)
        for way in (0, 1)
    ]
    for step in (1, -1):
        produce(turned(y, step))
    yield
    second = []
    for way in (0, 1):
        step = 1 - 2 * way
        first[way].wait_recv()
        chunk = part.at[turned(y, step)]
        half = chunk.at[:, pl.ds(way * 1024, 1024)]
        add_rows(half, [half, far.at[way]])
        second.append(links.start(chunk, near.at[way], "y", step))
    produce(y)
    yield
    for copy in second:
        copy.wait_recv()
    add_rows(out, [part.at[y], near.at[0], near.at[1]])
    for copy in first + second:
        copy.wait_send()


ROW_SCRATCH = [pltpu.VMEM((2, CHUNK, 1024), BF16), pltpu.VMEM((2, CHUNK, 2048), BF16)]


def scatter_weight(links, part, mate, far_a, near_a, far_b, near_b, light_a, light_b, out):
    z, x, core = lax.axis_index("z"), lax.axis_index("x"), lax.axis_index("core")
    rows = part.shape[1]
    half = rows // 2
    top, low = pl.ds(0, half), pl.ds(half, rows - half)
    ours = pl.ds(pl.multiple_of(core * 1024, 1024), 1024)

    def lanes(place):
        return pl.ds(pl.multiple_of(core * 1024 + place * 256, 256), 256)

    theirs = part.at[:, :, pl.ds(pl.multiple_of((1 - core) * 1024, 1024), 1024)]
    across = links.start(theirs, mate, "core", 1)
    yield
    across.wait_recv()
    for block in range(4):
        held = part.at[block, :, ours]
        add_rows(held, [held, mate.at[block]])
    first = []
    for way in (0, 1):
        step = 1 - 2 * way
        half_lanes = pl.ds(pl.multiple_of(core * 1024 + way * 512, 512), 512)
        first.append(links.start(part.at[turned(z, 2), top, half_lanes], far_a.at[way], "z", step))
        block = part.at[pl.ds(2 * way, 2), low, lanes(turned(x, 2))]
        first.append(links.start(block, far_b.at[way], "x", step))
    yield
    second = []
    for way in (0, 1):
        step = 1 - 2 * way
        first[2 * way].wait_recv()
        half_lanes = pl.ds(pl.multiple_of(core * 1024 + way * 512, 512), 512)
        held = part.at[turned(z, step), top, half_lanes]
        add_rows(held, [held, far_a.at[way]])
        second.append(links.start(part.at[turned(z, step), top, ours], near_a.at[way], "z", step))
        first[2 * way + 1].wait_recv()
        for i in range(2):
            held = part.at[2 * way + i, low, lanes(turned(x, step))]
            add_rows(held, [held, far_b.at[way, i]])
        second.append(links.start(part.at[:, low, lanes(turned(x, step))], near_b.at[way], "x", step))
    yield
    for way in (0, 1):
        second[2 * way].wait_recv()
    held = part.at[z, top, ours]
    add_rows(held, [held, near_a.at[0], near_a.at[1]])
    third = []
    for i, step in enumerate((1, 3, 2)):
        third.append(links.start(part.at[z, top, lanes(turned(x, step))], light_a.at[i], "x", step))
    for way in (0, 1):
        second[2 * way + 1].wait_recv()
    for block in range(4):
        held = part.at[block, low, lanes(x)]
        add_rows(held, [held, near_b.at[0, block], near_b.at[1, block]])
    for i, step in enumerate((1, 3, 2)):
        third.append(links.start(part.at[turned(z, step), low, lanes(x)], light_b.at[i], "z", step))
    yield
    for copy in third:
        copy.wait_recv()
    add_rows(out.at[top], [part.at[z, top, lanes(x)]] + [light_a.at[i] for i in range(3)])
    add_rows(out.at[low], [part.at[z, low, lanes(x)]] + [light_b.at[i] for i in range(3)])
    for copy in [across] + first + second + third:
        copy.wait_send()


def scatter_scratch(rows):
    half = rows // 2
    return [
        pltpu.VMEM((4, rows, 1024), BF16),
        pltpu.VMEM((2, half, 512), BF16),
        pltpu.VMEM((2, half, 1024), BF16),
        pltpu.VMEM((2, 2, half, 256), BF16),
        pltpu.VMEM((2, 4, half, 256), BF16),
        pltpu.VMEM((3, half, 256), BF16),
        pltpu.VMEM((3, half, 256), BF16),
    ]


SCATTER_REFS = 7


def sum_everywhere(links, slots, axis):
    size = lax.axis_size(axis)
    own = slots.at[lax.axis_index(axis)]
    copies = [links.start(own, own, axis, s) for s in range(1, size)]
    yield
    for copy in copies:
        copy.wait_recv()
    for copy in copies:
        copy.wait_send()


def any_space(count):
    return [pl.BlockSpec(memory_space=pl.ANY)] * count


def vmem(count):
    return [pl.BlockSpec(memory_space=pltpu.VMEM)] * count


def shape(dims, dtype):
    return jax.ShapeDtypeStruct(dims, dtype)


def sems(count):
    return [pltpu.SemaphoreType.DMA((count,)), pltpu.SemaphoreType.DMA((count,))]


def options(number, mib=60):
    return pltpu.CompilerParams(
        collective_id=number, has_side_effects=True, vmem_limit_bytes=mib * 2**20
    )


def spots(q, at, size):
    return pl.ds(pl.multiple_of(q * CHUNK + at, 8), size)


def flat2(ref):
    value = ref[...]
    return value.reshape(value.shape[0] * value.shape[1], value.shape[2])


def column(i, j, low, high, shift):
    row = lax.broadcasted_iota(jnp.int32, (i, j), 0)
    col = lax.broadcasted_iota(jnp.int32, (i, j), 1)
    hit = (col == row + shift) & (row >= low) & (row < high)
    return jnp.where(hit, 1.0, 0.0).astype(BF16)


def gather_small(links, vectors, gate_pack, vector_slots, gate_slots, params, gate_a, gate_x):
    z, core = lax.axis_index("z"), lax.axis_index("core")
    width = gate_pack.shape[0]
    half = width // 2
    part = pl.ds(pl.multiple_of(core * half, 16), half)
    here = [
        links.local(vectors, vector_slots.at[z]),
        links.local(gate_pack.at[part], gate_slots.at[z, part]),
    ]
    sent = []
    for step in (1, 3, 2):
        sent.append(links.start(vectors, vector_slots.at[z], "z", step))
        sent.append(links.start(gate_pack.at[part], gate_slots.at[z, part], "z", step))
    yield
    for copy in here:
        copy.wait()
    for copy in sent:
        copy.wait_recv()
    block = gate_slots.at[:, part]
    last = links.start(block, block, "core", 1)
    found = vector_slots[0] + vector_slots[1] + vector_slots[2] + vector_slots[3]
    params[8:16, :] = jnp.zeros_like(found)
    params[0:8, :] = found
    minus = -found[7:8, :]
    params[8:9, :] = jnp.maximum(minus, 0.0) + jnp.log1p(jnp.exp(-jnp.abs(minus)))
    params[9:10, :] = jax.nn.sigmoid(minus)
    yield
    last.wait_recv()
    channels = gate_a.shape[1]
    for place in range(RING):
        rows = pl.ds(place * width, width)
        packed = gate_slots[place]
        size = packed.shape[1]
        pick = column(size, channels, 0, width, place * width)
        gate_a[rows, :] = dot_nn(packed, pick).astype(BF16)
        pick = column(size, channels, width, 2 * width, place * width - width)
        gate_x[rows, :] = dot_nn(packed, pick).astype(BF16)
    for copy in sent + [last]:
        copy.wait_send()


def fill_lead(buf, halo, tiles):
    count = tiles * 8
    for q in range(RING):
        for i in range(tiles):
            at = buf.shape[1] - count + i * 8
            tile = buf[q, pl.ds(at, 8), :]
            before = halo[i * 8 + 7 : i * 8 + 8, :] if q == 0 else buf[q - 1, pl.ds(at + 7, 1), :]
            buf[q, pl.ds(i * 8, 8), :] = jnp.concatenate([before, tile[:7, :]], axis=0)


def fill_tail(buf, halo, tiles):
    for q in range(RING):
        for i in range(tiles):
            tile = buf[q, pl.ds(i * 8, 8), :]
            after = halo[i * 8 : i * 8 + 1, :] if q == RING - 1 else buf[q + 1, pl.ds(i * 8, 1), :]
            buf[q, pl.ds(CHUNK + i * 8, 8), :] = jnp.concatenate([tile[1:, :], after], axis=0)


def conv_gates(branch, masks, params, gate_a, gate_x, conv, low, rate, admit, decay, scaling, local):
    for q in range(RING):

        def taps(here, carry):
            at = here.start
            mask = masks[q, here, :]
            total = params[4:5, :] + params[0:1, :] * branch[q, pl.ds(pl.multiple_of(at + LEAD, 8), 32), :]
            for k in range(1, 4):
                moved = branch[q, pl.ds(pl.multiple_of(at + LEAD - 8 * k, 8), 32), :]
                total = total + params[k : k + 1, :] * (moved * mask[:, k : k + 1])
            conv[spots(q, at, 32), :] = total
            low[spots(q, at, 32), :] = total.astype(BF16)
            return carry

        strips(CHUNK, taps, size=32)
    rate[...] = dot_nn(low[...], gate_a[...])
    admit[...] = dot_nn(low[...], gate_x[...])
    for q in range(RING):

        def point(here, carry):
            spot = spots(q, here.start, 32)
            restart = masks[q, here, 0:1] > 0.5
            rated = jax.nn.sigmoid(rate[spot, :] + params[5:6, :])
            admitted = jax.nn.sigmoid(admit[spot, :] + params[6:7, :])
            log_decay = -8.0 * rated * params[8:9, :]
            scaled = jnp.where(restart, 1.0, jnp.sqrt(one_minus_exp(2.0 * log_decay)))
            rate[spot, :] = rated
            admit[spot, :] = admitted
            decay[spot, :] = jnp.where(restart, 0.0, jnp.exp(log_decay))
            scaling[spot, :] = scaled
            local[spot, :] = scaled * admitted * conv[spot, :]
            return carry

        strips(CHUNK, point, size=32)


def scan_start(channels):
    return (jnp.zeros((8, channels), F32), jnp.ones((8, channels), F32)) * RING


def scan_forward(decay, local, product):
    def step(j, carry):
        kept = []
        for q in range(RING):
            here = spots(q, j * 8, 8)
            rated = decay[here, :]
            state = rated * carry[2 * q] + local[here, :]
            prod = rated * carry[2 * q + 1]
            local[here, :] = state
            product[here, :] = prod
            kept += [state, prod]
        return tuple(kept)

    return lax.fori_loop(0, STEPS, step, scan_start(local.shape[1]))


def scan_backward(decay, local, product):
    def step(i, carry):
        kept = []
        for q in range(RING):
            here = spots(q, (STEPS - 1 - i) * 8, 8)
            rated = decay[here, :]
            total = local[here, :] + carry[2 * q]
            local[here, :] = total
            product[here, :] = carry[2 * q + 1]
            kept += [rated * total, rated * carry[2 * q + 1]]
        return tuple(kept)

    return lax.fori_loop(0, STEPS, step, scan_start(local.shape[1]))


def join_segments(ends, heads, totals, order):
    channels = totals.shape[2]
    prod, state = jnp.ones((1, channels), F32), jnp.zeros((1, channels), F32)
    for q in order(RING):
        for s in order(8):
            heads[0, q, s : s + 1, :] = prod
            heads[1, q, s : s + 1, :] = state
            rated = ends[2 * q + 1][s : s + 1, :]
            state = rated * state + ends[2 * q][s : s + 1, :]
            prod = rated * prod
    totals[0, 0:1, :] = prod
    totals[0, 1:2, :] = state


def share_totals(links, totals, way):
    return [links.start(totals.at[0], totals.at[step], "z", way * step) for step in range(1, RING)]


def entering_state(copies, totals, way):
    z = lax.axis_index("z")
    for copy in copies:
        copy.wait()
    entering = jnp.zeros((1, totals.shape[2]), F32)
    for step in range(RING - 1, 0, -1):
        later = totals[step, 0:1, :] * entering + totals[step, 1:2, :]
        valid = z - step >= 0 if way > 0 else z + step < RING
        entering = jnp.where(valid, later, entering)
    return entering


def spread_head(heads, q, entering):
    tile = heads[0, q] * entering + heads[1, q]
    return jnp.concatenate([tile] * 4, axis=0)


def kernel_a(
    x_in, cot, gain_rec, gain_mlp, weights, vectors, gate_pack, masks,
    mixed, seq_normed, seq_mlp, seq_grad, pair_out, out_out, gate_out, up_out, down_out,
    branch_out, conv_out, rate_out, admit_out, decay_out, scaling_out, states_out, gelu_out, gated_out,
    params_out, gate_a_out, gate_x_out,
    seq, pair, w_out, branch, gelu_pre, conv, low, rate, admit, decay, scaling, local, product, states, gated,
    params, gate_a, gate_x, vector_slots, gate_slots, halo, totals, heads, part, far, near, normed,
    send, recv,
):
    links = Links(send, recv)
    y = lax.axis_index("y")
    count = x_in.shape[0]
    width = vectors.shape[1] // RING
    hidden = gate_out.shape[1]
    greet()
    small = Task(gather_small(links, vectors, gate_pack, vector_slots, gate_slots, params, gate_a, gate_x))
    first = Task(gather_weight(links, weights.at[pl.ds(0, 2 * width)], pair))
    first.step()
    small.step()

    def norm(here, carry):
        values = x_in[here, :].astype(F32)
        seq[y, here, :] = (values * inverse_rms(values) * gain_rec[...]).astype(BF16)
        return carry

    strips(count, norm)
    rows = Task(gather_rows(links, seq))
    rows.step()
    own_cot = links.local(cot, seq_grad.at[y])
    second = Task(gather_weight(links, weights.at[pl.ds(2 * width, width)], w_out))
    second.step()
    first.step()
    small.step()
    second.step()
    small.finish()
    at = 3 * width
    late = []
    for full in (gate_out, up_out, down_out):
        late.append(Task(gather_weight(links, weights.at[pl.ds(at, hidden)], full)))
        at += hidden
    late[0].step()
    first.step()
    rows.step()
    own_cot.wait()
    cots = Task(gather_rows(links, seq_grad))
    first.step()
    second.step()
    late[0].step()
    rows.finish()
    cots.step()
    first.finish()
    late[1].step()

    normed_rows = flat2(seq)
    whole = pair[:, 0:width, :].reshape(RING * width, normed_rows.shape[1])
    result = dot_nt(normed_rows, whole)
    for q in range(RING):
        branch[q, LEAD:, :] = result[q * CHUNK : (q + 1) * CHUNK, :]
    edge = links.start(branch.at[RING - 1, pl.ds(CHUNK, LEAD)], halo, "z", 1)
    whole = pair[:, width:, :].reshape(RING * width, normed_rows.shape[1])
    gelu_pre[...] = dot_nt(normed_rows, whole)
    second.step()
    edge.wait()
    fill_lead(branch, halo, 3)
    saves = [
        links.local(branch, branch_out),
        links.local(gelu_pre, gelu_out),
        links.local(seq, seq_normed),
        links.local(pair, pair_out),
        links.local(params, params_out),
        links.local(gate_a, gate_a_out),
        links.local(gate_x, gate_x_out),
    ]
    conv_gates(branch, masks, params, gate_a, gate_x, conv, low, rate, admit, decay, scaling, local)
    late[0].step()
    late[1].step()
    ends = scan_forward(decay, local, product)
    join_segments(ends, heads, totals, range)
    copies = share_totals(links, totals, 1)
    saves += [
        links.local(conv, conv_out),
        links.local(rate, rate_out),
        links.local(admit, admit_out),
        links.local(decay, decay_out),
        links.local(scaling, scaling_out),
    ]
    cots.step()
    second.finish()
    late[2].step()
    entering = entering_state(copies, totals, 1)
    for q in range(RING):
        head = spread_head(heads, q, entering)

        def fix(here, carry):
            spot = spots(q, here.start, 32)
            state = local[spot, :] + product[spot, :] * head
            states[q, pl.ds(pl.multiple_of(here.start + 8, 8), 32), :] = state
            gated[spot, :] = (state * gelu_parts(gelu_pre[spot, :])[0]).astype(BF16)
            return carry

        strips(CHUNK, fix, size=32)
    halo[0:8, :] = jnp.broadcast_to(entering, (8, entering.shape[1]))
    fill_lead(states, halo, 1)
    saves += [
        links.local(states, states_out),
        links.local(gated, gated_out),
        links.local(w_out, out_out),
    ]

    def produce(q):
        spot = pl.ds(pl.multiple_of(q * CHUNK, CHUNK), CHUNK)
        part[q] = dot_nn(gated[spot, :], flat2(w_out)).astype(BF16)

    sums = Task(scatter_rows(links, produce, part, far, near, mixed))
    sums.step()
    late[0].step()
    late[1].step()
    late[2].step()
    sums.step()
    late[0].step()
    sums.finish()

    def renorm(here, carry):
        values = x_in[here, :].astype(F32) + mixed[here, :]
        mixed[here, :] = values
        normed[here, :] = (values * inverse_rms(values) * gain_mlp[...]).astype(BF16)
        return carry

    strips(count, renorm)
    links.local(normed, seq_mlp.at[y]).wait()
    rows = Task(gather_rows(links, seq_mlp))
    rows.step()
    late[0].finish()
    late[1].step()
    late[2].step()
    cots.finish()
    rows.step()
    late[1].step()
    late[2].step()
    rows.finish()
    late[1].finish()
    late[2].finish()
    for copy in saves:
        copy.wait()


def kernel_b(
    seq_mlp, seq_grad, w_gate, w_up, w_down, mixed, cot, gain,
    g_mixed, seq_mixed, part_out, gate_grad, up_grad, down_grad, gain_out,
    mlp, grads, gate, up, down, pre_gate, pre_up, pre_hidden, hidden, g_gate, g_up,
    part, outs, total, low, far, near, *rest,
):
    send, recv = rest[-2:]
    links = Links(send, recv)
    y = lax.axis_index("y")
    count, model = mixed.shape
    width = gate.shape[1]
    load_mlp, load_grads = links.local(seq_mlp, mlp), None
    loads = []
    for n in range(RING):
        loads.append([links.local(w_gate.at[n], gate.at[n]), links.local(w_up.at[n], up.at[n])])
        if n == 0:
            load_grads = links.local(seq_grad, grads)
        loads[n].append(links.local(w_down.at[n], down.at[n]))
    greet()
    load_mlp.wait()
    for n in range(RING):
        loads[n][0].wait()
        pre_gate[...] = dot_nt(flat2(mlp), gate[n])
        loads[n][1].wait()
        pre_up[...] = dot_nt(flat2(mlp), up[n])
        if n == 0:
            load_grads.wait()
        loads[n][2].wait()
        pre_hidden[...] = dot_nt(flat2(grads), down[n])
        lanes = pl.ds(n * width, width)

        def point(here, carry):
            gates, ups, backs = pre_gate[here, :], pre_up[here, :], pre_hidden[here, :]
            value, tang = gelu_parts(gates)
            hidden[here, lanes] = (value * ups).astype(BF16)
            g_gate[here, lanes] = (backs * ups * gelu_slope(gates, tang)).astype(BF16)
            g_up[here, lanes] = (backs * value).astype(BF16)
            return carry

        strips(RING * CHUNK, point, size=32)

    def produce(q):
        spot = pl.ds(pl.multiple_of(q * CHUNK, CHUNK), CHUNK)
        result = dot_nn(g_gate[spot, :], flat2(gate)) + dot_nn(g_up[spot, :], flat2(up))
        part[q] = result.astype(BF16)

    def weight_grad(left, right, out):
        def block(n, carry):
            lanes = pl.ds(pl.multiple_of(n * width, 128), width)
            out[n] = dot_tn(left[:, lanes], flat2(right)).astype(BF16)
            return carry

        lax.fori_loop(0, RING, block, 0)

    sums = Task(scatter_rows(links, produce, part, far, near, total))
    sums.step()
    sums.step()

    for q in range(RING):
        outs[q] = dot_nn(hidden[q * CHUNK : (q + 1) * CHUNK, :], flat2(down)).astype(BF16)
    save = links.local(outs, part_out)
    weight_grad(hidden, grads, down)
    downs = Task(scatter_weight(links, down, *rest[:SCATTER_REFS], down_grad))
    downs.step()
    sums.finish()

    def back(here, carry):
        values = mixed[here, :]
        backs = total[here, :]
        scale = inverse_rms(values)
        held = cot[here, :].astype(F32) + norm_back(backs, values, scale, gain[...])
        g_mixed[here, :] = held
        low[here, :] = held.astype(BF16)
        new = backs * values * scale
        return carry + new[:8, :] + new[8:, :]

    acc = strips(count, back, jnp.zeros((8, model), F32))
    gain_out[...] = jnp.broadcast_to(jnp.sum(acc, axis=0, keepdims=True), (8, model))
    links.local(low, seq_mixed.at[y]).wait()
    rows = Task(gather_rows(links, seq_mixed))
    rows.step()
    downs.step()
    weight_grad(g_gate, mlp, gate)
    gates = Task(scatter_weight(links, gate, *rest[SCATTER_REFS : 2 * SCATTER_REFS], gate_grad))
    gates.step()
    downs.step()
    rows.step()
    gates.step()
    weight_grad(g_up, mlp, up)
    ups = Task(scatter_weight(links, up, *rest[2 * SCATTER_REFS : 3 * SCATTER_REFS], up_grad))
    ups.step()
    downs.step()
    gates.step()
    ups.step()
    rows.finish()
    downs.finish()
    gates.step()
    ups.step()
    gates.finish()
    ups.finish()
    save.wait()


def kernel_c(
    seq_mixed, seq_normed, w_pair, w_out, branch_in, conv_in, rate_in, admit_in, decay_in, scaling_in,
    states_in, gelu_in, gated_in, params, gate_a, gate_x, masks, g_mixed, mixed, x_in, gain, gain_part,
    part_out,
    g_inputs, output, pair_grad, out_grad, small_out, gain_out,
    seq, normed, pair, w_o, branch, conv, rate, admit, decay, scaling, states, gelu_pre, gated,
    local, product, g_gelu, rate_low, admit_low, low, g_conv, g_branch, halo, totals, heads,
    squares, pack, pack_mate, pack_z, pack_x, small_rows, gain_slots, gain_acc,
    pair_part, total, far, near, outs, far_out, near_out, *rest,
):
    send, recv = rest[-2:]
    links = Links(send, recv)
    count, model = g_mixed.shape
    width = out_grad.shape[0]
    channels = RING * width
    z, x, core = lax.axis_index("z"), lax.axis_index("x"), lax.axis_index("core")
    load_seq = links.local(seq_mixed, seq)
    load_w = links.local(w_out, w_o)
    load_mid = [links.local(s, d) for s, d in ((gelu_in, gelu_pre), (states_in, states), (decay_in, decay))]
    load_out = links.local(part_out, outs)
    load_late = [
        links.local(s, d)
        for s, d in (
            (seq_normed, normed), (gated_in, gated), (conv_in, conv), (rate_in, rate), (admit_in, admit),
            (scaling_in, scaling), (branch_in, branch), (w_pair, pair),
        )
    ]
    greet()
    load_out.wait()
    out_sums = Task(scatter_rows(links, lambda q: None, outs, far_out, near_out, total))
    out_sums.step()
    load_seq.wait()
    load_w.wait()
    product[...] = dot_nt(flat2(seq), flat2(w_o))
    for copy in load_mid:
        copy.wait()
    out_sums.step()
    for q in range(RING):

        def point(here, carry):
            spot = spots(q, here.start, 32)
            held = product[spot, :]
            pre = gelu_pre[spot, :]
            value, tang = gelu_parts(pre)
            state = states[q, pl.ds(pl.multiple_of(here.start + 8, 8), 32), :]
            g_gelu[spot, :] = (held * state * gelu_slope(pre, tang)).astype(BF16)
            local[spot, :] = held * value
            return carry

        strips(CHUNK, point, size=32)
    ends = scan_backward(decay, local, product)
    join_segments(ends, heads, totals, lambda n: range(n - 1, -1, -1))
    copies = share_totals(links, totals, -1)
    for copy in load_late:
        copy.wait()

    def weight_grad(left, right, out, base):
        for first, size in ((0, 256), (256, 256), (512, 128)):
            result = dot_tn(left[:, first : first + size], right).astype(BF16)
            at = first
            while at < first + size:
                place, row = at // width, at % width
                take = min(width - row, first + size - at)
                out[place, base + row : base + row + take, :] = result[at - first : at - first + take, :]
                at += take

    normed_rows = flat2(normed)
    weight_grad(gated, flat2(seq), w_o, 0)
    part = seq
    outw = Task(scatter_weight(links, w_o, *rest[:SCATTER_REFS], out_grad))
    outw.step()
    weight_grad(g_gelu, normed_rows, pair_part, width)
    entering = entering_state(copies, totals, -1)
    zero = jnp.zeros((8, channels), F32)

    def eights(value):
        return value[0:8, :] + value[8:16, :] + value[16:24, :] + value[24:32, :]

    sums = (zero, zero, zero)
    for q in range(RING):
        head = spread_head(heads, q, entering)

        def fix(here, carry):
            spot = spots(q, here.start, 32)
            running = masks[q, here, 0:1] < 0.5
            before = states[q, here, :]
            carried = local[spot, :] + product[spot, :] * head
            rated, admitted, held = rate[spot, :], admit[spot, :], conv[spot, :]
            spread, scaled = decay[spot, :], scaling[spot, :]
            g_log = jnp.where(
                running, carried * spread * (before - admitted * held * spread / scaled), 0.0
            )
            g_rate = g_log * (-8.0 * params[8:9, :]) * rated * (1.0 - rated)
            driven = carried * scaled * admitted
            g_admit = driven * held * (1.0 - admitted)
            rate_low[spot, :] = g_rate.astype(BF16)
            admit_low[spot, :] = g_admit.astype(BF16)
            low[spot, :] = held.astype(BF16)
            g_conv[q, here, :] = driven
            return carry[0] + eights(g_rate), carry[1] + eights(g_admit), carry[2] + eights(g_log * rated)

        sums = strips(CHUNK, fix, sums, size=32)
    back = dot_nt(rate_low[...], gate_a[...]) + dot_nt(admit_low[...], gate_x[...])
    for q in range(RING):
        g_conv[q, 0:CHUNK, :] = g_conv[q, 0:CHUNK, :] + back[q * CHUNK : (q + 1) * CHUNK, :]
    edge = links.start(g_conv.at[0, pl.ds(0, LEAD)], halo, "z", -1)
    outw.step()
    squares[0] = dot_tn(low[...], rate_low[...]).astype(BF16)
    squares[1] = dot_tn(low[...], admit_low[...]).astype(BF16)
    edge.wait()
    fill_tail(g_conv, halo, 3)
    taps = (zero,) * 5
    for q in range(RING):

        def conv_back(here, carry):
            at = here.start
            own = g_conv[q, here, :]
            total_here = params[0:1, :] * own
            new = [carry[0] + eights(own * branch[q, pl.ds(pl.multiple_of(at + LEAD, 8), 32), :])]
            for k in range(1, 4):
                later = pl.ds(pl.multiple_of(at + 8 * k, 8), 32)
                total_here = total_here + params[k : k + 1, :] * (
                    g_conv[q, later, :] * masks[q, later, k : k + 1]
                )
                moved = branch[q, pl.ds(pl.multiple_of(at + LEAD - 8 * k, 8), 32), :]
                new.append(carry[k] + eights(own * masks[q, here, k : k + 1] * moved))
            new.append(carry[4] + eights(own))
            g_branch[spots(q, at, 32), :] = total_here.astype(BF16)
            return tuple(new)

        taps = strips(CHUNK, conv_back, taps, size=32)
    weight_grad(g_branch, normed_rows, pair_part, 0)
    pairs = Task(scatter_weight(links, pair_part, *rest[SCATTER_REFS : 2 * SCATTER_REFS], pair_grad))
    pairs.step()
    outw.step()
    gain_acc[...] = jnp.zeros((8, model), F32)

    def produce(q):
        spot = pl.ds(pl.multiple_of(q * CHUNK, CHUNK), CHUNK)
        first = pair[:, 0:width, :].reshape(channels, model)
        other = pair[:, width:, :].reshape(channels, model)
        part[q] = (dot_nn(g_branch[spot, :], first) + dot_nn(g_gelu[spot, :], other)).astype(BF16)

        def gather_gain(here, carry):
            new = part[q, here, :].astype(F32) * normed[q, here, :].astype(F32)
            gain_acc[...] = gain_acc[...] + new[:8, :] + new[8:, :]
            return carry

        strips(CHUNK, gather_gain)

    out_sums.finish()

    def last(here, carry):
        output[here, :] = (mixed[here, :] + total[here, :]).astype(BF16)
        return carry

    strips(count, last)
    row_sums = Task(scatter_rows(links, produce, part, far, near, total))
    row_sums.step()

    for i, value in enumerate(taps + sums):
        row = jnp.sum(value, axis=0, keepdims=True)
        small_rows[i : i + 1, :] = row * 8.0 * params[9:10, :] if i == 7 else row
    small_rows[8:16, :] = jnp.zeros((8, channels), F32)
    size = pack.shape[2]
    for place in range(RING):
        pick = column(channels, size, place * width, (place + 1) * width, -place * width)
        rows_here = pl.ds(place * width, width)
        pack[place, 0:width, :] = dot_nn(squares[0, rows_here, :], pick).astype(BF16)
        pack[place, width : 2 * width, :] = dot_nn(squares[1, rows_here, :], pick).astype(BF16)
        pack[place, 2 * width : 2 * width + 16, :] = dot_nn(small_rows[...].astype(BF16), pick).astype(BF16)
        pack[place, 2 * width + 16 :, :] = jnp.zeros((pack.shape[1] - 2 * width - 16, size), BF16)

    def smalls():
        half = pack.shape[1] // 2
        ours = pl.ds(pl.multiple_of(core * half, 16), half)
        theirs = pl.ds(pl.multiple_of((1 - core) * half, 16), half)
        across = links.start(pack.at[:, theirs], pack_mate, "core", 1)
        yield
        across.wait_recv()
        for place in range(RING):
            held = pack.at[place, ours]
            add_rows(held, [held, pack_mate.at[place]])
        sent = [
            links.start(pack.at[turned(z, step), ours], pack_z.at[i], "z", step)
            for i, step in enumerate((1, 3, 2))
        ]
        yield
        for copy in sent:
            copy.wait_recv()
        add_rows(pack_x.at[x], [pack.at[z, ours]] + [pack_z.at[i] for i in range(3)])
        yield from sum_everywhere(links, pack_x, "x")
        add_rows(small_out.at[ours], [pack_x.at[i] for i in range(RING)])
        held = small_out.at[ours]
        final = links.start(held, held, "core", 1)
        yield
        final.wait()
        for copy in [across] + sent:
            copy.wait_send()

    def gains():
        rec = jnp.sum(gain_acc[...], axis=0, keepdims=True) / gain[...]
        quarter = model // 4
        for i in range(4):
            gain_out[i : i + 1, :] = rec[:, i * quarter : (i + 1) * quarter]
            gain_out[4 + i : 5 + i, :] = gain_part[0:1, i * quarter : (i + 1) * quarter]
        for n, axis in enumerate(("y", "z", "x", "core")):
            slots = gain_slots.at[n, pl.ds(0, lax.axis_size(axis))]
            slots[lax.axis_index(axis)] = gain_out[...]
            yield from sum_everywhere(links, slots, axis)
            found = slots[0]
            for i in range(1, lax.axis_size(axis)):
                found = found + slots[i]
            gain_out[...] = found

    small_task = Task(smalls())
    small_task.step()
    pairs.step()
    small_task.step()
    row_sums.step()
    gain_task = Task(gains())
    gain_task.step()
    small_task.step()
    gain_task.step()
    outw.step()
    pairs.step()
    small_task.step()
    gain_task.step()
    outw.finish()
    pairs.step()
    gain_task.step()
    small_task.finish()
    gain_task.finish()
    row_sums.finish()

    def finish(here, carry):
        values = x_in[here, :].astype(F32)
        g_inputs[here, :] = g_mixed[here, :] + norm_back(
            total[here, :], values, inverse_rms(values), gain[...]
        )
        return carry

    strips(count, finish)
    pairs.finish()


def call_a(x_in, cot, gain_rec, gain_mlp, weights, vectors, gate_pack, masks, width, hidden):
    count, model = x_in.shape
    channels = RING * width
    rows = RING * CHUNK
    wide = shape((rows, channels), F32)
    seq = shape((RING, count, model), BF16)
    square = shape((channels, channels), BF16)
    big = shape((RING, hidden, model), BF16)
    lead = (RING, CHUNK + LEAD, channels)
    held = (RING, CHUNK + 8, channels)
    flat = pltpu.VMEM((rows, channels), F32)
    return pl.pallas_call(
        kernel_a,
        out_shape=[
            shape((count, model), F32), seq, seq, seq,
            shape((RING, 2 * width, model), BF16), shape((RING, width, model), BF16), big, big, big,
            shape(lead, F32), wide, wide, wide, wide, wide, shape(held, F32), wide,
            shape((rows, channels), BF16), shape((16, channels), F32), square, square,
        ],
        in_specs=vmem(4) + any_space(1) + vmem(3),
        out_specs=vmem(1) + any_space(20),
        scratch_shapes=[
            pltpu.VMEM((RING, count, model), BF16),
            pltpu.VMEM((RING, 2 * width, model), BF16),
            pltpu.VMEM((RING, width, model), BF16),
            pltpu.VMEM(lead, F32),
            flat, flat,
            pltpu.VMEM((rows, channels), BF16),
            flat, flat, flat, flat, flat, flat,
            pltpu.VMEM(held, F32),
            pltpu.VMEM((rows, channels), BF16),
            pltpu.VMEM((16, channels), F32),
            pltpu.VMEM((channels, channels), BF16),
            pltpu.VMEM((channels, channels), BF16),
            pltpu.VMEM((RING, 8, channels), F32),
            pltpu.VMEM((RING,) + gate_pack.shape, BF16),
            pltpu.VMEM((LEAD, channels), F32),
            pltpu.VMEM((RING, 8, channels), F32),
            pltpu.VMEM((2, RING, 8, channels), F32),
            pltpu.VMEM((RING, count, model), BF16),
        ]
        + ROW_SCRATCH
        + [pltpu.VMEM((count, model), BF16)]
        + sems(160),
        compiler_params=options(1),
    )(x_in, cot, gain_rec, gain_mlp, weights, vectors, gate_pack, masks)


def call_b(seq_mlp, seq_grad, w_gate, w_up, w_down, mixed, cot, gain):
    count, model = mixed.shape
    hidden = w_gate.shape[1]
    rows = RING * CHUNK
    seq = shape((RING, count, model), BF16)
    big = pltpu.VMEM((RING, hidden, model), BF16)
    final = shape((hidden, 256), F32)
    wide = pltpu.VMEM((rows, RING * hidden), BF16)
    pre = pltpu.VMEM((rows, hidden), F32)
    rows_held = pltpu.VMEM((RING, count, model), BF16)
    return pl.pallas_call(
        kernel_b,
        out_shape=[shape((count, model), F32), seq, seq, final, final, final, shape((8, model), F32)],
        in_specs=any_space(5) + vmem(3),
        out_specs=vmem(1) + any_space(2) + vmem(4),
        scratch_shapes=[
            rows_held, rows_held, big, big, big, pre, pre, pre, wide, wide, wide, rows_held, rows_held,
            pltpu.VMEM((count, model), F32),
            pltpu.VMEM((count, model), BF16),
        ]
        + ROW_SCRATCH
        + scatter_scratch(hidden) * 3
        + sems(128),
        compiler_params=options(2, 63),
    )(seq_mlp, seq_grad, w_gate, w_up, w_down, mixed, cot, gain)


def call_c(*args):
    w_pair, masks, g_mixed = args[2], args[16], args[17]
    count, model = g_mixed.shape
    width = w_pair.shape[1] // 2
    channels = RING * width
    rows = RING * CHUNK
    pack = (RING, 2 * width + 32, 256)
    flat = pltpu.VMEM((rows, channels), F32)
    thin = pltpu.VMEM((rows, channels), BF16)
    rows_held = pltpu.VMEM((RING, count, model), BF16)
    lead = pltpu.VMEM((RING, CHUNK + LEAD, channels), F32)
    half = pack[1] // 2
    return pl.pallas_call(
        kernel_c,
        out_shape=[
            shape((count, model), F32),
            shape((count, model), BF16),
            shape((2 * width, 256), F32),
            shape((width, 256), F32),
            shape(pack[1:], BF16),
            shape((8, model // 4), F32),
        ],
        in_specs=any_space(13) + vmem(9) + any_space(1),
        out_specs=vmem(6),
        scratch_shapes=[
            rows_held, rows_held,
            pltpu.VMEM((RING, 2 * width, model), BF16),
            pltpu.VMEM((RING, width, model), BF16),
            lead, flat, flat, flat, flat, flat,
            pltpu.VMEM((RING, CHUNK + 8, channels), F32),
            flat, thin,
            flat, flat, thin, thin, thin, thin, lead, thin,
            pltpu.VMEM((LEAD, channels), F32),
            pltpu.VMEM((RING, 8, channels), F32),
            pltpu.VMEM((2, RING, 8, channels), F32),
            pltpu.VMEM((2, channels, channels), BF16),
            pltpu.VMEM(pack, BF16),
            pltpu.VMEM((RING, half, 256), BF16),
            pltpu.VMEM((3, half, 256), BF16),
            pltpu.VMEM((RING, half, 256), BF16),
            pltpu.VMEM((16, channels), F32),
            pltpu.VMEM((4, RING, 8, model // 4), F32),
            pltpu.VMEM((8, model), F32),
            pltpu.VMEM((RING, 2 * width, model), BF16),
            pltpu.VMEM((count, model), F32),
        ]
        + ROW_SCRATCH
        + [rows_held]
        + ROW_SCRATCH
        + scatter_scratch(width)
        + scatter_scratch(2 * width)
        + sems(128),
        compiler_params=options(3, 63),
    )(*args)


def place_rows(rows):
    count, model = rows.shape
    held = rows.reshape(8, count // 8, RING, 2, 256).transpose(1, 0, 3, 2, 4)
    return held.reshape(count, model)


def restore_rows(rows):
    count, model = rows.shape
    held = rows.reshape(count // 8, 8, 2, RING, 256).transpose(1, 0, 3, 2, 4)
    return held.reshape(count, 1, model)


def place_width(vector):
    return vector.reshape(RING, 2, 256).transpose(1, 0, 2).reshape(1, -1)


def restore_width(vector):
    return vector.reshape(2, RING, 256).transpose(1, 0, 2).reshape(-1)


def position_masks(resets, z):
    rows = RING * CHUNK
    flags = jnp.pad(resets.reshape(-1).astype(F32), (8, 24), constant_values=1.0)
    window = lax.dynamic_slice(flags, (z * rows,), (rows + 32,))
    keep = 1.0 - window
    first = keep[8:]
    second = first * keep[7:-1]
    third = second * keep[6:-2]
    columns = jnp.stack([window[8:], first, second, third] + [jnp.zeros_like(first)] * 4, axis=1)

    def steps(start):
        held = columns[start : start + rows].reshape(RING, 8, STEPS, 8)
        return held.transpose(0, 2, 1, 3)

    both = jnp.concatenate([steps(0), steps(STEPS)[:, :3]], axis=1)
    return both.reshape(RING, CHUNK + LEAD, 8)


def on_device(
    inputs,
    resets,
    gain_rec,
    w_branch,
    w_gelu,
    conv_weight,
    conv_bias,
    gate_a_weight,
    gate_a_bias,
    gate_x_weight,
    gate_x_bias,
    decay_param,
    w_out,
    gain_mlp,
    w_gate,
    w_up,
    w_down,
    cotangent,
):
    count, _, model = inputs.shape
    z = lax.axis_index("z")
    width, hidden = w_branch.shape[1], w_gate.shape[1]
    masks = position_masks(resets, z)
    vectors = jnp.concatenate(
        [conv_weight, jnp.stack([conv_bias, gate_a_bias, gate_x_bias, decay_param])], axis=0
    )
    vectors = lax.dynamic_update_slice(jnp.zeros((8, RING * width), F32), vectors, (0, z * width))
    gate_pack = jnp.concatenate([gate_a_weight[0], gate_x_weight[0]], axis=1)
    gate_pack = jnp.pad(gate_pack, ((0, 0), (0, -gate_pack.shape[1] % 128)))
    weights = jnp.concatenate([w_branch, w_gelu, w_out, w_gate, w_up, w_down], axis=1).T
    x_in = place_rows(inputs.reshape(count, model))
    cot = place_rows(cotangent.reshape(count, model))
    gain_rec, gain_mlp = place_width(gain_rec), place_width(gain_mlp)

    (
        mixed, seq_normed, seq_mlp, seq_grad, w_pair, w_out_all, w_gate_all, w_up_all, w_down_all,
        branch, conv, rate, admit, decay, scaling, states, gelu_pre, gated, params, gate_a, gate_x,
    ) = call_a(x_in, cot, gain_rec, gain_mlp, weights, vectors, gate_pack, masks, width, hidden)
    g_mixed, seq_mixed, part_out, grad_gate, grad_up, grad_down, gain_part = call_b(
        seq_mlp, seq_grad, w_gate_all, w_up_all, w_down_all, mixed, cot, gain_mlp
    )
    g_inputs, output, grad_pair, grad_out, packed, gains = call_c(
        seq_mixed, seq_normed, w_pair, w_out_all, branch, conv, rate, admit, decay, scaling,
        states, gelu_pre, gated, params, gate_a, gate_x, masks, g_mixed, mixed, x_in, gain_rec, gain_part,
        part_out,
    )
    packed = packed[:, :width].astype(F32)
    vector = packed[2 * width : 2 * width + 8]
    return (
        restore_rows(output),
        restore_rows(g_inputs),
        restore_width(gains[:4]),
        grad_pair[:width].T,
        grad_pair[width:].T,
        vector[:4],
        vector[4],
        packed[:width].reshape(1, width, width),
        vector[5],
        packed[width : 2 * width].reshape(1, width, width),
        vector[6],
        vector[7],
        grad_out.T,
        restore_width(gains[4:]),
        grad_gate.T,
        grad_up.T,
        grad_down.T,
    )


def solution(mesh):
    sizes = {"blk": mesh.shape["blk"], "tok": mesh.shape["tok"]}
    grid = Mesh(mesh.devices.reshape(RING, sizes["blk"] // RING, sizes["tok"] // 2, 2), AXES)
    blk, tok = ("z", "y"), ("x", "core")
    in_specs = (
        P(blk, tok, None),
        P(None, tok),
        P(),
        P(tok, blk),
        P(tok, blk),
        P(None, blk),
        P(blk),
        P(blk, None, None),
        P(blk),
        P(blk, None, None),
        P(blk),
        P(blk),
        P(tok, blk),
        P(),
        P(tok, blk),
        P(tok, blk),
        P(tok, blk),
        P(blk, tok, None),
    )
    out_specs = (
        P(blk, tok, None),
        P(blk, tok, None),
        P(),
        P(tok, blk),
        P(tok, blk),
        P(None, blk),
        P(blk),
        P(blk, None, None),
        P(blk),
        P(blk, None, None),
        P(blk),
        P(blk),
        P(tok, blk),
        P(),
        P(tok, blk),
        P(tok, blk),
        P(tok, blk),
    )
    return jax.shard_map(
        on_device, mesh=grid, in_specs=in_specs, out_specs=out_specs, check_vma=False
    )
```

```python
import enum
import math

import jax
import jax.numpy as jnp
from jax import lax
from jax.experimental import pallas as pl
from jax.experimental.pallas import tpu as pltpu
from jax.sharding import Mesh
from jax.sharding import PartitionSpec as P

EPSILON = 1e-06
MESH = pl.DeviceIdType.MESH
AXES = ("z", "y", "x", "core")
GELU_A = math.sqrt(2.0 / math.pi)
GELU_B = 0.044715
F32 = jnp.float32
BF16 = jnp.bfloat16
RING = 4
CHUNK = 128
STEPS = CHUNK // 8
LEAD = 24


def dot_nn(left, right):
    return lax.dot_general(left, right, (((1,), (0,)), ((), ())), preferred_element_type=F32)


def dot_nt(left, right):
    return lax.dot_general(left, right, (((1,), (1,)), ((), ())), preferred_element_type=F32)


def dot_tn(left, right):
    return lax.dot_general(left, right, (((0,), (0,)), ((), ())), preferred_element_type=F32)


def gelu_parts(v):
    t = jnp.tanh(GELU_A * (v + GELU_B * v * v * v))
    return 0.5 * v * (1.0 + t), t


def gelu_slope(v, t):
    return 0.5 * (1.0 + t) + 0.5 * v * (1.0 - t * t) * (GELU_A * (1.0 + 3.0 * GELU_B * v * v))


def one_minus_exp(v):
    series = 1.0 + v * (1.0 / 9.0)
    for order in (8.0, 7.0, 6.0, 5.0, 4.0, 3.0, 2.0):
        series = 1.0 + v * (1.0 / order) * series
    return jnp.where(v > -0.5, -v * series, 1.0 - jnp.exp(v))


def inverse_rms(values):
    return lax.rsqrt(jnp.mean(values * values, axis=-1, keepdims=True) + EPSILON)


def norm_back(grads, values, scale, gain):
    held = grads * gain
    return scale * held - values * (scale * scale * scale) * jnp.mean(held * values, axis=-1, keepdims=True)


def around(axis, size, step):
    return {axis: lax.rem(lax.axis_index(axis) + (step + size), size)}


def turned(index, step):
    return lax.rem(index + (step + RING), RING)


class Links:
    def __init__(self, send, recv):
        self.send, self.recv, self.used = send, recv, 0

    def start(self, src, dst, axis, step):
        copy = pltpu.make_async_remote_copy(
            src_ref=src,
            dst_ref=dst,
            send_sem=self.send.at[self.used],
            recv_sem=self.recv.at[self.used],
            device_id=around(axis, lax.axis_size(axis), step),
            device_id_type=MESH,
        )
        self.used += 1
        copy.start()
        return copy

    def local(self, src, dst):
        copy = pltpu.make_async_copy(src, dst, self.send.at[self.used])
        self.used += 1
        copy.start()
        return copy


def greet():
    barrier = pltpu.get_barrier_semaphore()
    total = 0
    for axis in AXES:
        size = lax.axis_size(axis)
        for step in range(1, size):
            pl.semaphore_signal(barrier, inc=1, device_id=around(axis, size, step), device_id_type=MESH)
            total += 1
    pl.semaphore_wait(barrier, total)


class Task:
    def __init__(self, stages):
        self.stages = stages

    def step(self):
        next(self.stages, None)

    def finish(self):
        for _ in self.stages:
            pass


def strips(count, body, carry=0, size=16):
    def step(i, carry):
        return body(pl.ds(pl.multiple_of(i * size, size), size), carry)

    return lax.fori_loop(0, count // size, step, carry)


def add_rows(out, terms):
    def body(here, carry):
        total = terms[0][here, :].astype(F32)
        for term in terms[1:]:
            total = total + term[here, :].astype(F32)
        out[here, :] = total.astype(out.dtype)
        return carry

    strips(out.shape[0], body)


def gather_weight(links, own, full):
    z, x, core = lax.axis_index("z"), lax.axis_index("x"), lax.axis_index("core")
    rows = own.shape[0]
    half = rows // 2
    mine = pl.ds(pl.multiple_of((core * 4 + x) * 256, 256), 256)
    ours = pl.ds(pl.multiple_of(core * 1024, 1024), 1024)
    top, low = pl.ds(0, half), pl.ds(half, rows - half)
    here = links.local(own, full.at[z, :, mine])
    first_a = [links.start(own.at[top], full.at[z, top, mine], "x", s) for s in (1, 3, 2)]
    first_b = [links.start(own.at[low], full.at[z, low, mine], "z", s) for s in (1, 3, 2)]
    yield
    mates = []

    def share(block):
        mates.append(links.start(block, block, "core", 1))

    def beside(step):
        return full.at[:, low, pl.ds(pl.multiple_of((core * 4 + turned(x, step)) * 256, 256), 256)]

    here.wait()
    for copy in first_a:
        copy.wait_recv()
    block = full.at[z, top, ours]
    second_a = [links.start(block, block, "z", s) for s in (1, -1)]
    share(block)
    for copy in first_b:
        copy.wait_recv()
    block = beside(0)
    second_b = [links.start(block, block, "x", s) for s in (1, -1)]
    share(block)
    yield
    relays = []
    for way in (0, 1):
        step = 1 - 2 * way
        second_a[way].wait_recv()
        lanes = pl.ds(pl.multiple_of(core * 1024 + way * 512, 512), 512)
        block = full.at[turned(z, -step), top, lanes]
        relays.append(links.start(block, block, "z", step))
        second_b[way].wait_recv()
        lanes = pl.ds(pl.multiple_of((core * 4 + turned(x, -step)) * 256, 256), 256)
        block = full.at[pl.ds(2 * way, 2), low, lanes]
        relays.append(links.start(block, block, "x", step))
    for step in (1, -1):
        share(full.at[turned(z, step), top, ours])
        share(beside(step))
    yield
    for copy in relays:
        copy.wait_recv()
    share(full.at[turned(z, 2), top, ours])
    share(beside(2))
    yield
    for copy in mates:
        copy.wait_recv()
    for copy in first_a + first_b + second_a + second_b + relays + mates:
        copy.wait_send()


def gather_rows(links, seq):
    y = lax.axis_index("y")
    own = seq.at[y]
    first = [links.start(own, own, "y", s) for s in (1, -1)]
    yield
    relays = []
    for way in (0, 1):
        step = 1 - 2 * way
        first[way].wait_recv()
        block = seq.at[turned(y, -step), :, pl.ds(way * 1024, 1024)]
        relays.append(links.start(block, block, "y", step))
    yield
    for copy in relays:
        copy.wait_recv()
    for copy in first + relays:
        copy.wait_send()


def scatter_rows(links, produce, part, far, near, out):
    y = lax.axis_index("y")
    across = turned(y, 2)
    produce(across)
    first = [
        links.start(part.at[across, :, pl.ds(way * 1024, 1024)], far.at[way], "y", 1 - 2 * way)
        for way in (0, 1)
    ]
    for step in (1, -1):
        produce(turned(y, step))
    yield
    second = []
    for way in (0, 1):
        step = 1 - 2 * way
        first[way].wait_recv()
        chunk = part.at[turned(y, step)]
        half = chunk.at[:, pl.ds(way * 1024, 1024)]
        add_rows(half, [half, far.at[way]])
        second.append(links.start(chunk, near.at[way], "y", step))
    produce(y)
    yield
    for copy in second:
        copy.wait_recv()
    add_rows(out, [part.at[y], near.at[0], near.at[1]])
    for copy in first + second:
        copy.wait_send()


ROW_SCRATCH = [pltpu.VMEM((2, CHUNK, 1024), BF16), pltpu.VMEM((2, CHUNK, 2048), BF16)]


def share_core(links, part, mate):
    core = lax.axis_index("core")
    ours = pl.ds(pl.multiple_of(core * 1024, 1024), 1024)
    theirs = part.at[:, :, pl.ds(pl.multiple_of((1 - core) * 1024, 1024), 1024)]
    across = links.start(theirs, mate, "core", 1)
    yield
    across.wait_recv()
    for block in range(4):
        held = part.at[block, :, ours]
        add_rows(held, [held, mate.at[block]])
    across.wait_send()


def scatter_weight(links, part, mate, far_a, near_a, far_b, near_b, light_a, light_b, out):
    yield from share_core(links, part, mate)
    base = lax.axis_index("core") * 1024
    yield from scatter_chips(links, part, base, far_a, near_a, far_b, near_b, light_a, light_b, out)


def scatter_chips(links, part, base, far_a, near_a, far_b, near_b, light_a, light_b, out):
    z, x = lax.axis_index("z"), lax.axis_index("x")
    rows = part.shape[1]
    half = rows // 2
    top, low = pl.ds(0, half), pl.ds(half, rows - half)
    ours = pl.ds(pl.multiple_of(base, 1024), 1024)

    def lanes(place):
        return pl.ds(pl.multiple_of(base + place * 256, 256), 256)

    first = []
    for way in (0, 1):
        step = 1 - 2 * way
        half_lanes = pl.ds(pl.multiple_of(base + way * 512, 512), 512)
        first.append(links.start(part.at[turned(z, 2), top, half_lanes], far_a.at[way], "z", step))
        block = part.at[pl.ds(2 * way, 2), low, lanes(turned(x, 2))]
        first.append(links.start(block, far_b.at[way], "x", step))
    yield
    second = []
    for way in (0, 1):
        step = 1 - 2 * way
        first[2 * way].wait_recv()
        half_lanes = pl.ds(pl.multiple_of(base + way * 512, 512), 512)
        held = part.at[turned(z, step), top, half_lanes]
        add_rows(held, [held, far_a.at[way]])
        second.append(links.start(part.at[turned(z, step), top, ours], near_a.at[way], "z", step))
        first[2 * way + 1].wait_recv()
        for i in range(2):
            held = part.at[2 * way + i, low, lanes(turned(x, step))]
            add_rows(held, [held, far_b.at[way, i]])
        second.append(links.start(part.at[:, low, lanes(turned(x, step))], near_b.at[way], "x", step))
    yield
    for way in (0, 1):
        second[2 * way].wait_recv()
    held = part.at[z, top, ours]
    add_rows(held, [held, near_a.at[0], near_a.at[1]])
    third = []
    for i, step in enumerate((1, 3, 2)):
        third.append(links.start(part.at[z, top, lanes(turned(x, step))], light_a.at[i], "x", step))
    for way in (0, 1):
        second[2 * way + 1].wait_recv()
    for block in range(4):
        held = part.at[block, low, lanes(x)]
        add_rows(held, [held, near_b.at[0, block], near_b.at[1, block]])
    for i, step in enumerate((1, 3, 2)):
        third.append(links.start(part.at[turned(z, step), low, lanes(x)], light_b.at[i], "z", step))
    yield
    for copy in third:
        copy.wait_recv()
    add_rows(out.at[top], [part.at[z, top, lanes(x)]] + [light_a.at[i] for i in range(3)])
    add_rows(out.at[low], [part.at[z, low, lanes(x)]] + [light_b.at[i] for i in range(3)])
    for copy in first + second + third:
        copy.wait_send()


def scatter_scratch(rows):
    half = rows // 2
    return [
        pltpu.VMEM((4, rows, 1024), BF16),
        pltpu.VMEM((2, half, 512), BF16),
        pltpu.VMEM((2, half, 1024), BF16),
        pltpu.VMEM((2, 2, half, 256), BF16),
        pltpu.VMEM((2, 4, half, 256), BF16),
        pltpu.VMEM((3, half, 256), BF16),
        pltpu.VMEM((3, half, 256), BF16),
    ]


SCATTER_REFS = 7


def sum_everywhere(links, slots, axis):
    size = lax.axis_size(axis)
    own = slots.at[lax.axis_index(axis)]
    copies = [links.start(own, own, axis, s) for s in range(1, size)]
    yield
    for copy in copies:
        copy.wait_recv()
    for copy in copies:
        copy.wait_send()


def any_space(count):
    return [pl.BlockSpec(memory_space=pl.ANY)] * count


def vmem(count):
    return [pl.BlockSpec(memory_space=pltpu.VMEM)] * count


def shape(dims, dtype):
    return jax.ShapeDtypeStruct(dims, dtype)


def sems(count):
    return [pltpu.SemaphoreType.DMA((count,)), pltpu.SemaphoreType.DMA((count,))]


def options(number, mib=60):
    return pltpu.CompilerParams(
        collective_id=number, has_side_effects=True, vmem_limit_bytes=mib * 2**20
    )


def spots(q, at, size):
    return pl.ds(pl.multiple_of(q * CHUNK + at, 8), size)


def flat2(ref):
    value = ref[...]
    return value.reshape(value.shape[0] * value.shape[1], value.shape[2])


def column(i, j, low, high, shift):
    row = lax.broadcasted_iota(jnp.int32, (i, j), 0)
    col = lax.broadcasted_iota(jnp.int32, (i, j), 1)
    hit = (col == row + shift) & (row >= low) & (row < high)
    return jnp.where(hit, 1.0, 0.0).astype(BF16)


def gather_small(links, vectors, gate_pack, vector_slots, gate_slots, params, gate_a, gate_x):
    z, core = lax.axis_index("z"), lax.axis_index("core")
    width = gate_pack.shape[0]
    half = width // 2
    part = pl.ds(pl.multiple_of(core * half, 16), half)
    here = [
        links.local(vectors, vector_slots.at[z]),
        links.local(gate_pack.at[part], gate_slots.at[z, part]),
    ]
    sent = []
    for step in (1, 3, 2):
        sent.append(links.start(vectors, vector_slots.at[z], "z", step))
        sent.append(links.start(gate_pack.at[part], gate_slots.at[z, part], "z", step))
    yield
    for copy in here:
        copy.wait()
    for copy in sent:
        copy.wait_recv()
    block = gate_slots.at[:, part]
    last = links.start(block, block, "core", 1)
    found = vector_slots[0] + vector_slots[1] + vector_slots[2] + vector_slots[3]
    params[8:16, :] = jnp.zeros_like(found)
    params[0:8, :] = found
    minus = -found[7:8, :]
    params[8:9, :] = jnp.maximum(minus, 0.0) + jnp.log1p(jnp.exp(-jnp.abs(minus)))
    params[9:10, :] = jax.nn.sigmoid(minus)
    yield
    last.wait_recv()
    channels = gate_a.shape[1]
    for place in range(RING):
        rows = pl.ds(place * width, width)
        packed = gate_slots[place]
        size = packed.shape[1]
        pick = column(size, channels, 0, width, place * width)
        gate_a[rows, :] = dot_nn(packed, pick).astype(BF16)
        pick = column(size, channels, width, 2 * width, place * width - width)
        gate_x[rows, :] = dot_nn(packed, pick).astype(BF16)
    for copy in sent + [last]:
        copy.wait_send()


def fill_lead(buf, halo, tiles):
    count = tiles * 8
    for q in range(RING):
        for i in range(tiles):
            at = buf.shape[1] - count + i * 8
            tile = buf[q, pl.ds(at, 8), :]
            before = halo[i * 8 + 7 : i * 8 + 8, :] if q == 0 else buf[q - 1, pl.ds(at + 7, 1), :]
            buf[q, pl.ds(i * 8, 8), :] = jnp.concatenate([before, tile[:7, :]], axis=0)


def fill_tail(buf, halo, tiles):
    for q in range(RING):
        for i in range(tiles):
            tile = buf[q, pl.ds(i * 8, 8), :]
            after = halo[i * 8 : i * 8 + 1, :] if q == RING - 1 else buf[q + 1, pl.ds(i * 8, 1), :]
            buf[q, pl.ds(CHUNK + i * 8, 8), :] = jnp.concatenate([tile[1:, :], after], axis=0)


def conv_taps(branch, masks, params, conv, low):
    for q in range(RING):

        def taps(here, carry):
            at = here.start
            mask = masks[q, here, :]
            total = params[4:5, :] + params[0:1, :] * branch[q, pl.ds(pl.multiple_of(at + LEAD, 8), 32), :]
            for k in range(1, 4):
                moved = branch[q, pl.ds(pl.multiple_of(at + LEAD - 8 * k, 8), 32), :]
                total = total + params[k : k + 1, :] * (moved * mask[:, k : k + 1])
            conv[spots(q, at, 32), :] = total
            low[spots(q, at, 32), :] = total.astype(BF16)
            return carry

        strips(CHUNK, taps, size=32)


def gate_values(masks, params, conv, rate, admit, decay, scaling, local):
    for q in range(RING):

        def point(here, carry):
            spot = spots(q, here.start, 32)
            restart = masks[q, here, 0:1] > 0.5
            rated = jax.nn.sigmoid(rate[spot, :] + params[5:6, :])
            admitted = jax.nn.sigmoid(admit[spot, :] + params[6:7, :])
            log_decay = -8.0 * rated * params[8:9, :]
            scaled = jnp.where(restart, 1.0, jnp.sqrt(one_minus_exp(2.0 * log_decay)))
            rate[spot, :] = rated
            admit[spot, :] = admitted
            decay[spot, :] = jnp.where(restart, 0.0, jnp.exp(log_decay))
            scaling[spot, :] = scaled
            local[spot, :] = scaled * admitted * conv[spot, :]
            return carry

        strips(CHUNK, point, size=32)


def scan_start(channels):
    return (jnp.zeros((8, channels), F32), jnp.ones((8, channels), F32)) * RING


def scan_forward(decay, local, product):
    def step(j, carry):
        kept = []
        for q in range(RING):
            here = spots(q, j * 8, 8)
            rated = decay[here, :]
            state = rated * carry[2 * q] + local[here, :]
            prod = rated * carry[2 * q + 1]
            local[here, :] = state
            product[here, :] = prod
            kept += [state, prod]
        return tuple(kept)

    return lax.fori_loop(0, STEPS, step, scan_start(local.shape[1]))


def scan_backward(decay, local, product):
    def step(i, carry):
        kept = []
        for q in range(RING):
            here = spots(q, (STEPS - 1 - i) * 8, 8)
            rated = decay[here, :]
            total = local[here, :] + carry[2 * q]
            local[here, :] = total
            product[here, :] = carry[2 * q + 1]
            kept += [rated * total, rated * carry[2 * q + 1]]
        return tuple(kept)

    return lax.fori_loop(0, STEPS, step, scan_start(local.shape[1]))


def join_segments(ends, heads, totals, order):
    channels = totals.shape[2]
    prod, state = jnp.ones((1, channels), F32), jnp.zeros((1, channels), F32)
    for q in order(RING):
        for s in order(8):
            heads[0, q, s : s + 1, :] = prod
            heads[1, q, s : s + 1, :] = state
            rated = ends[2 * q + 1][s : s + 1, :]
            state = rated * state + ends[2 * q][s : s + 1, :]
            prod = rated * prod
    totals[0, 0:1, :] = prod
    totals[0, 1:2, :] = state


def share_totals(links, totals, way):
    return [links.start(totals.at[0], totals.at[step], "z", way * step) for step in range(1, RING)]


def entering_state(copies, totals, way):
    z = lax.axis_index("z")
    for copy in copies:
        copy.wait()
    entering = jnp.zeros((1, totals.shape[2]), F32)
    for step in range(RING - 1, 0, -1):
        later = totals[step, 0:1, :] * entering + totals[step, 1:2, :]
        valid = z - step >= 0 if way > 0 else z + step < RING
        entering = jnp.where(valid, later, entering)
    return entering


def spread_head(heads, q, entering):
    tile = heads[0, q] * entering + heads[1, q]
    return jnp.concatenate([tile] * 4, axis=0)


def follow(plan, actions):
    for name in plan:
        actions[name]()


class A(enum.IntEnum):
    SMALL, WB, WG, WO, W1, W2, W3, NORM, ROWS, COTS, BRANCH, GELU, EDGE, CONV, GATES, POINT, SCAN, FIX, SUMS, RENORM, MLP = range(21)


def kernel_a(
    x_in, cot, gain_rec, gain_mlp, weights, vectors, gate_pack, masks,
    mixed, seq_normed, seq_mlp, seq_grad, wb_out, wg_out, out_out, gate_out, up_out, down_out,
    branch_out, conv_out, rate_out, admit_out, decay_out, scaling_out, states_out, gelu_out, gated_out,
    params_out, gate_a_out, gate_x_out,
    seq, w_branch, w_gelu, w_out, branch, gelu_pre, conv, low, rate, admit, decay, scaling, local, product,
    states, gated, params, gate_a, gate_x, vector_slots, gate_slots, halo, totals, heads, part, far, near, normed,
    send, recv,
):
    links = Links(send, recv)
    y = lax.axis_index("y")
    count = x_in.shape[0]
    width = vectors.shape[1] // RING
    hidden = gate_out.shape[1]
    own_cot = links.local(cot, seq_grad.at[y])
    greet()
    saves, kept = [], {}

    def save(*pairs):
        for source, target in pairs:
            saves.append(links.local(source, target))

    def norm():
        def body(here, carry):
            values = x_in[here, :].astype(F32)
            seq[y, here, :] = (values * inverse_rms(values) * gain_rec[...]).astype(BF16)
            return carry

        strips(count, body)

    def cots():
        own_cot.wait()
        yield from gather_rows(links, seq_grad)

    def to_branch():
        result = dot_nt(flat2(seq), flat2(w_branch))
        for q in range(RING):
            branch[q, LEAD:, :] = result[q * CHUNK : (q + 1) * CHUNK, :]
        kept["edge"] = links.start(branch.at[RING - 1, pl.ds(CHUNK, LEAD)], halo, "z", 1)

    def to_gelu():
        gelu_pre[...] = dot_nt(flat2(seq), flat2(w_gelu))

    def edge():
        kept["edge"].wait()
        fill_lead(branch, halo, 3)

    def conv_all():
        conv_taps(branch, masks, params, conv, low)

    def gates():
        rate[...] = dot_nn(low[...], gate_a[...])
        admit[...] = dot_nn(low[...], gate_x[...])

    def point_all():
        gate_values(masks, params, conv, rate, admit, decay, scaling, local)

    def scan():
        ends = scan_forward(decay, local, product)
        join_segments(ends, heads, totals, range)
        kept["totals"] = share_totals(links, totals, 1)

    def fix_all():
        entering = entering_state(kept["totals"], totals, 1)
        for q in range(RING):
            head = spread_head(heads, q, entering)

            def fix(here, carry):
                spot = spots(q, here.start, 32)
                state = local[spot, :] + product[spot, :] * head
                states[q, pl.ds(pl.multiple_of(here.start + 8, 8), 32), :] = state
                gated[spot, :] = (state * gelu_parts(gelu_pre[spot, :])[0]).astype(BF16)
                return carry

            strips(CHUNK, fix, size=32)
        halo[0:8, :] = jnp.broadcast_to(entering, (8, entering.shape[1]))
        fill_lead(states, halo, 1)
        save(
            (seq, seq_normed), (w_branch, wb_out), (w_gelu, wg_out), (params, params_out),
            (gate_a, gate_a_out), (gate_x, gate_x_out), (branch, branch_out), (gelu_pre, gelu_out),
            (conv, conv_out), (rate, rate_out), (admit, admit_out), (decay, decay_out), (scaling, scaling_out),
            (states, states_out), (gated, gated_out),
        )

    def produce(q):
        spot = pl.ds(pl.multiple_of(q * CHUNK, CHUNK), CHUNK)
        part[q] = dot_nn(gated[spot, :], flat2(w_out)).astype(BF16)

    def renorm_all():
        def renorm(here, carry):
            values = x_in[here, :].astype(F32) + mixed[here, :]
            mixed[here, :] = values
            normed[here, :] = (values * inverse_rms(values) * gain_mlp[...]).astype(BF16)
            return carry

        strips(count, renorm)
        links.local(normed, seq_mlp.at[y]).wait()
        save((w_out, out_out))

    tasks = {
        A.SMALL: gather_small(links, vectors, gate_pack, vector_slots, gate_slots, params, gate_a, gate_x),
        A.ROWS: gather_rows(links, seq),
        A.COTS: cots(),
        A.SUMS: scatter_rows(links, produce, part, far, near, mixed),
        A.MLP: gather_rows(links, seq_mlp),
    }
    fulls = (w_branch, w_gelu, w_out, gate_out, up_out, down_out)
    for i, name in enumerate((A.WB, A.WG, A.WO, A.W1, A.W2, A.W3)):
        size = width if i < 3 else hidden
        start = i * width if i < 3 else 3 * width + (i - 3) * hidden
        tasks[name] = gather_weight(links, weights.at[pl.ds(start, size)], fulls[i])
    tasks = {name: Task(stages) for name, stages in tasks.items()}
    actions = {
        A.NORM: norm, A.BRANCH: to_branch, A.GELU: to_gelu, A.EDGE: edge, A.CONV: conv_all, A.GATES: gates,
        A.POINT: point_all, A.SCAN: scan, A.FIX: fix_all, A.RENORM: renorm_all,
    }
    actions.update({name: task.step for name, task in tasks.items()})
    follow(PLAN_A, actions)
    for task in tasks.values():
        task.finish()
    for copy in saves:
        copy.wait()


class B(enum.IntEnum):
    TILE, SUMS, OUTS, GRAD_DOWN, DOWNS, GRAD_GATE, GATES, GRAD_UP, UPS, BACK, MIXED, OUTSUM = range(12)


def kernel_b(
    seq_mlp, seq_grad, w_gate, w_up, w_down, mixed, cot, gain,
    g_mixed, seq_mixed, output, up_part, gate_grad, down_grad, gain_out,
    mlp, grads, gate, up, down, pre_gate, pre_up, pre_hidden, hidden, g_gate, g_up,
    part, outs, total, low, far, near, far_out, near_out, *rest,
):
    send, recv = rest[-2:]
    links = Links(send, recv)
    y = lax.axis_index("y")
    count, model = mixed.shape
    width = gate.shape[1]
    load_mlp, load_grads = links.local(seq_mlp, mlp), None
    loads = []
    for n in range(RING):
        loads.append([links.local(w_gate.at[n], gate.at[n]), links.local(w_up.at[n], up.at[n])])
        if n == 0:
            load_grads = links.local(seq_grad, grads)
        loads[n].append(links.local(w_down.at[n], down.at[n]))
    greet()
    ours = pl.ds(pl.multiple_of(lax.axis_index("core") * 1024, 1024), 1024)

    def tiles():
        for n in range(RING):
            if n == 0:
                load_mlp.wait()
            loads[n][0].wait()
            pre_gate[...] = dot_nt(flat2(mlp), gate[n])
            loads[n][1].wait()
            pre_up[...] = dot_nt(flat2(mlp), up[n])
            if n == 0:
                load_grads.wait()
            loads[n][2].wait()
            pre_hidden[...] = dot_nt(flat2(grads), down[n])
            lanes = pl.ds(n * width, width)

            def point(here, carry):
                gates, ups, backs = pre_gate[here, :], pre_up[here, :], pre_hidden[here, :]
                value, tang = gelu_parts(gates)
                hidden[here, lanes] = (value * ups).astype(BF16)
                g_gate[here, lanes] = (backs * ups * gelu_slope(gates, tang)).astype(BF16)
                g_up[here, lanes] = (backs * value).astype(BF16)
                return carry

            strips(RING * CHUNK, point, size=32)
            yield

    def produce(q):
        spot = pl.ds(pl.multiple_of(q * CHUNK, CHUNK), CHUNK)
        result = dot_nn(g_gate[spot, :], flat2(gate)) + dot_nn(g_up[spot, :], flat2(up))
        part[q] = result.astype(BF16)

    def weight_grad(left, right, out):
        def block(n, carry):
            lanes = pl.ds(pl.multiple_of(n * width, 128), width)
            out[n] = dot_tn(left[:, lanes], flat2(right)).astype(BF16)
            return carry

        return lambda: lax.fori_loop(0, RING, block, 0)

    def out_parts():
        for q in range(RING):
            outs[q] = dot_nn(hidden[q * CHUNK : (q + 1) * CHUNK, :], flat2(down)).astype(BF16)

    def back_all():
        def back(here, carry):
            values = mixed[here, :]
            backs = total[here, :]
            scale = inverse_rms(values)
            held = cot[here, :].astype(F32) + norm_back(backs, values, scale, gain[...])
            g_mixed[here, :] = held
            low[here, :] = held.astype(BF16)
            new = backs * values * scale
            return carry + new[:8, :] + new[8:, :]

        acc = strips(count, back, jnp.zeros((8, model), F32))
        gain_out[...] = jnp.broadcast_to(jnp.sum(acc, axis=0, keepdims=True), (8, model))
        links.local(low, seq_mixed.at[y]).wait()

    def out_sums():
        yield from scatter_rows(links, lambda q: None, outs, far_out, near_out, total)

        def last(here, carry):
            output[here, :] = (mixed[here, :] + total[here, :]).astype(BF16)
            return carry

        strips(count, last)

    def ups():
        yield from share_core(links, up, rest[2 * SCATTER_REFS])
        copy = links.local(up.at[:, :, ours], up_part)
        yield
        copy.wait()

    tasks = {
        B.TILE: tiles(),
        B.SUMS: scatter_rows(links, produce, part, far, near, total),
        B.DOWNS: scatter_weight(links, down, *rest[:SCATTER_REFS], down_grad),
        B.GATES: scatter_weight(links, gate, *rest[SCATTER_REFS : 2 * SCATTER_REFS], gate_grad),
        B.UPS: ups(),
        B.MIXED: gather_rows(links, seq_mixed),
        B.OUTSUM: out_sums(),
    }
    tasks = {name: Task(stages) for name, stages in tasks.items()}
    actions = {
        B.OUTS: out_parts, B.BACK: back_all, B.GRAD_DOWN: weight_grad(hidden, grads, down),
        B.GRAD_GATE: weight_grad(g_gate, mlp, gate), B.GRAD_UP: weight_grad(g_up, mlp, up),
    }
    actions.update({name: task.step for name, task in tasks.items()})
    follow(PLAN_B, actions)
    for task in tasks.values():
        task.finish()


class C(enum.IntEnum):
    UPS, GATED, POINT, SCAN, GRAD_OUT, OUTW, GRAD_GELU, GELUW, FIX, GATES, SQUARES, CONV, SUMS, GRAD_BRANCH, BRANCHW, PACK, SMALLS, GAINS, FINISH = range(19)


def kernel_c(
    seq_mixed, seq_normed, wb_in, wg_in, w_out, branch_in, conv_in, rate_in, admit_in, decay_in, scaling_in,
    states_in, gelu_in, gated_in, up_part, params, gate_a, gate_x, masks, g_mixed, x_in, gain, gain_part,
    g_inputs, branch_grad, gelu_grad, out_grad, up_grad, small_out, gain_out,
    seq, normed, w_branch, w_gelu, w_o, branch, conv, rate, admit, decay, scaling, states, gelu_pre, gated,
    local, product, g_gelu, rate_low, admit_low, low, g_conv, halo, totals, heads,
    squares, pack, pack_mate, pack_z, pack_x, small_rows, gain_slots, gain_acc,
    up, branch_part, gelu_part, total, far, near, *rest,
):
    send, recv = rest[-2:]
    links = Links(send, recv)
    count, model = g_mixed.shape
    width = out_grad.shape[0]
    channels = RING * width
    z, x, core = lax.axis_index("z"), lax.axis_index("x"), lax.axis_index("core")
    part, g_branch = seq, low
    loads, kept = {}, {}
    for source, target in (
        (seq_mixed, seq), (w_out, w_o), (gelu_in, gelu_pre), (states_in, states), (decay_in, decay), (up_part, up),
        (gated_in, gated), (seq_normed, normed), (conv_in, conv), (rate_in, rate), (admit_in, admit),
        (scaling_in, scaling), (branch_in, branch), (wb_in, w_branch), (wg_in, w_gelu),
    ):
        loads[id(target)] = links.local(source, target)
    greet()

    def need(*targets):
        for target in targets:
            copy = loads.pop(id(target), None)
            if copy is not None:
                copy.wait()

    def ups():
        need(up)
        yield from scatter_chips(links, up, 0, *rest[3 * SCATTER_REFS : 4 * SCATTER_REFS - 1], up_grad)

    def to_gated():
        need(seq, w_o)
        product[...] = dot_nt(flat2(seq), flat2(w_o))

    def point_all():
        need(gelu_pre, states)
        for q in range(RING):

            def point(here, carry):
                spot = spots(q, here.start, 32)
                held = product[spot, :]
                pre = gelu_pre[spot, :]
                value, tang = gelu_parts(pre)
                state = states[q, pl.ds(pl.multiple_of(here.start + 8, 8), 32), :]
                g_gelu[spot, :] = (held * state * gelu_slope(pre, tang)).astype(BF16)
                local[spot, :] = held * value
                return carry

            strips(CHUNK, point, size=32)

    def scan():
        need(decay)
        ends = scan_backward(decay, local, product)
        join_segments(ends, heads, totals, lambda n: range(n - 1, -1, -1))
        kept["totals"] = share_totals(links, totals, -1)

    def weight_grad(left, right, out):
        def run():
            need(left, right)
            for first, size in ((0, 256), (256, 256), (512, 128)):
                result = dot_tn(left[:, first : first + size], flat2(right)).astype(BF16)
                at = first
                while at < first + size:
                    place, row = at // width, at % width
                    take = min(width - row, first + size - at)
                    out[place, row : row + take, :] = result[at - first : at - first + take, :]
                    at += take

        return run

    zero = jnp.zeros((8, channels), F32)

    def eights(value):
        return value[0:8, :] + value[8:16, :] + value[16:24, :] + value[24:32, :]

    def fix_all():
        need(conv, rate, admit, scaling)
        entering = entering_state(kept["totals"], totals, -1)
        sums = (zero, zero, zero)
        for q in range(RING):
            head = spread_head(heads, q, entering)

            def fix(here, carry):
                spot = spots(q, here.start, 32)
                running = masks[q, here, 0:1] < 0.5
                before = states[q, here, :]
                carried = local[spot, :] + product[spot, :] * head
                rated, admitted, held = rate[spot, :], admit[spot, :], conv[spot, :]
                spread, scaled = decay[spot, :], scaling[spot, :]
                g_log = jnp.where(
                    running, carried * spread * (before - admitted * held * spread / scaled), 0.0
                )
                g_rate = g_log * (-8.0 * params[8:9, :]) * rated * (1.0 - rated)
                driven = carried * scaled * admitted
                g_admit = driven * held * (1.0 - admitted)
                rate_low[spot, :] = g_rate.astype(BF16)
                admit_low[spot, :] = g_admit.astype(BF16)
                low[spot, :] = held.astype(BF16)
                g_conv[q, here, :] = driven
                return carry[0] + eights(g_rate), carry[1] + eights(g_admit), carry[2] + eights(g_log * rated)

            sums = strips(CHUNK, fix, sums, size=32)
        kept["sums"] = sums

    def gates():
        back = dot_nt(rate_low[...], gate_a[...]) + dot_nt(admit_low[...], gate_x[...])
        for q in range(RING):
            g_conv[q, 0:CHUNK, :] = g_conv[q, 0:CHUNK, :] + back[q * CHUNK : (q + 1) * CHUNK, :]
        kept["edge"] = links.start(g_conv.at[0, pl.ds(0, LEAD)], halo, "z", -1)

    def gate_squares():
        squares[0] = dot_tn(low[...], rate_low[...]).astype(BF16)
        squares[1] = dot_tn(low[...], admit_low[...]).astype(BF16)

    def conv_all():
        need(branch)
        kept["edge"].wait()
        fill_tail(g_conv, halo, 3)
        taps = (zero,) * 5
        for q in range(RING):

            def conv_back(here, carry):
                at = here.start
                own = g_conv[q, here, :]
                total_here = params[0:1, :] * own
                new = [carry[0] + eights(own * branch[q, pl.ds(pl.multiple_of(at + LEAD, 8), 32), :])]
                for k in range(1, 4):
                    later = pl.ds(pl.multiple_of(at + 8 * k, 8), 32)
                    total_here = total_here + params[k : k + 1, :] * (
                        g_conv[q, later, :] * masks[q, later, k : k + 1]
                    )
                    moved = branch[q, pl.ds(pl.multiple_of(at + LEAD - 8 * k, 8), 32), :]
                    new.append(carry[k] + eights(own * masks[q, here, k : k + 1] * moved))
                new.append(carry[4] + eights(own))
                g_branch[spots(q, at, 32), :] = total_here.astype(BF16)
                return tuple(new)

            taps = strips(CHUNK, conv_back, taps, size=32)
        kept["taps"] = taps
        gain_acc[...] = jnp.zeros((8, model), F32)

    def produce(q):
        need(w_branch, w_gelu, normed)
        spot = pl.ds(pl.multiple_of(q * CHUNK, CHUNK), CHUNK)
        result = dot_nn(g_branch[spot, :], flat2(w_branch)) + dot_nn(g_gelu[spot, :], flat2(w_gelu))
        part[q] = result.astype(BF16)

        def gather_gain(here, carry):
            new = part[q, here, :].astype(F32) * normed[q, here, :].astype(F32)
            gain_acc[...] = gain_acc[...] + new[:8, :] + new[8:, :]
            return carry

        strips(CHUNK, gather_gain)

    def pack_all():
        for i, value in enumerate(kept["taps"] + kept["sums"]):
            row = jnp.sum(value, axis=0, keepdims=True)
            small_rows[i : i + 1, :] = row * 8.0 * params[9:10, :] if i == 7 else row
        small_rows[8:16, :] = jnp.zeros((8, channels), F32)
        size = pack.shape[2]
        for place in range(RING):
            pick = column(channels, size, place * width, (place + 1) * width, -place * width)
            rows_here = pl.ds(place * width, width)
            pack[place, 0:width, :] = dot_nn(squares[0, rows_here, :], pick).astype(BF16)
            pack[place, width : 2 * width, :] = dot_nn(squares[1, rows_here, :], pick).astype(BF16)
            pack[place, 2 * width : 2 * width + 16, :] = dot_nn(small_rows[...].astype(BF16), pick).astype(BF16)
            pack[place, 2 * width + 16 :, :] = jnp.zeros((pack.shape[1] - 2 * width - 16, size), BF16)

    def smalls():
        half = pack.shape[1] // 2
        ours = pl.ds(pl.multiple_of(core * half, 16), half)
        theirs = pl.ds(pl.multiple_of((1 - core) * half, 16), half)
        across = links.start(pack.at[:, theirs], pack_mate, "core", 1)
        yield
        across.wait_recv()
        for place in range(RING):
            held = pack.at[place, ours]
            add_rows(held, [held, pack_mate.at[place]])
        sent = [
            links.start(pack.at[turned(z, step), ours], pack_z.at[i], "z", step)
            for i, step in enumerate((1, 3, 2))
        ]
        yield
        for copy in sent:
            copy.wait_recv()
        add_rows(pack_x.at[x], [pack.at[z, ours]] + [pack_z.at[i] for i in range(3)])
        yield from sum_everywhere(links, pack_x, "x")
        add_rows(small_out.at[ours], [pack_x.at[i] for i in range(RING)])
        held = small_out.at[ours]
        final = links.start(held, held, "core", 1)
        yield
        final.wait()
        for copy in [across] + sent:
            copy.wait_send()

    def gains():
        rec = jnp.sum(gain_acc[...], axis=0, keepdims=True) / gain[...]
        quarter = model // 4
        for i in range(4):
            gain_out[i : i + 1, :] = rec[:, i * quarter : (i + 1) * quarter]
            gain_out[4 + i : 5 + i, :] = gain_part[0:1, i * quarter : (i + 1) * quarter]
        for n, axis in enumerate(("y", "z", "x", "core")):
            slots = gain_slots.at[n, pl.ds(0, lax.axis_size(axis))]
            slots[lax.axis_index(axis)] = gain_out[...]
            yield from sum_everywhere(links, slots, axis)
            found = slots[0]
            for i in range(1, lax.axis_size(axis)):
                found = found + slots[i]
            gain_out[...] = found

    def finish_all():
        def finish(here, carry):
            values = x_in[here, :].astype(F32)
            g_inputs[here, :] = g_mixed[here, :] + norm_back(
                total[here, :], values, inverse_rms(values), gain[...]
            )
            return carry

        strips(count, finish)

    first, second, third = (rest[i * SCATTER_REFS : (i + 1) * SCATTER_REFS] for i in range(3))
    tasks = {
        C.UPS: ups(),
        C.OUTW: scatter_weight(links, w_o, *first, out_grad),
        C.GELUW: scatter_weight(links, gelu_part, *second, gelu_grad),
        C.BRANCHW: scatter_weight(links, branch_part, *third, branch_grad),
        C.SUMS: scatter_rows(links, produce, part, far, near, total),
        C.SMALLS: smalls(),
        C.GAINS: gains(),
    }
    tasks = {name: Task(stages) for name, stages in tasks.items()}
    actions = {
        C.GATED: to_gated, C.POINT: point_all, C.SCAN: scan, C.FIX: fix_all, C.GATES: gates,
        C.SQUARES: gate_squares, C.CONV: conv_all, C.PACK: pack_all, C.FINISH: finish_all,
        C.GRAD_OUT: weight_grad(gated, seq, w_o), C.GRAD_GELU: weight_grad(g_gelu, normed, gelu_part),
        C.GRAD_BRANCH: weight_grad(g_branch, normed, branch_part),
    }
    actions.update({name: task.step for name, task in tasks.items()})
    follow(PLAN_C, actions)
    for task in tasks.values():
        task.finish()


PLAN_A = (
    A.WB, A.NORM, A.WG, A.ROWS, A.WB, A.SMALL, A.WG, A.ROWS, A.WO, A.WB, A.SMALL, A.WO, A.WB, A.WG, A.WO, A.COTS, A.ROWS, A.WB, A.BRANCH, A.SMALL, A.W1, A.EDGE, A.CONV, A.WG, A.W2, A.GATES, A.POINT, A.W1, A.WG, A.WO, A.SCAN, A.COTS, A.GELU, A.W3, A.WO, A.FIX, A.SUMS, A.W2, A.SUMS, A.W1, A.W2, A.SUMS, A.RENORM, A.MLP, A.COTS, A.W3, A.W1, A.W3, A.W2, A.MLP, A.W3, A.W1, A.MLP, A.W2, A.W3,
)
PLAN_B = (
    B.TILE, B.TILE, B.TILE, B.TILE, B.SUMS, B.OUTS, B.SUMS, B.GRAD_DOWN, B.DOWNS, B.GRAD_GATE, B.SUMS, B.OUTSUM, B.DOWNS, B.GATES, B.BACK, B.MIXED, B.DOWNS, B.GATES, B.GRAD_UP, B.GATES, B.UPS, B.MIXED, B.OUTSUM, B.UPS, B.DOWNS, B.GATES, B.MIXED, B.OUTSUM, B.DOWNS, B.GATES, B.UPS,
)
PLAN_C = (
    C.UPS, C.GATED, C.POINT, C.SCAN, C.UPS, C.GRAD_GELU, C.GELUW, C.FIX, C.GATES, C.GRAD_OUT, C.SQUARES, C.OUTW, C.GELUW, C.CONV, C.UPS, C.SUMS, C.OUTW, C.GRAD_BRANCH, C.GELUW, C.PACK, C.OUTW, C.BRANCHW, C.SUMS, C.BRANCHW, C.SMALLS, C.GAINS, C.SMALLS, C.UPS, C.BRANCHW, C.GELUW, C.SMALLS, C.GAINS, C.SUMS, C.GAINS, C.FINISH, C.BRANCHW, C.OUTW, C.GELUW, C.GAINS, C.GAINS, C.SMALLS, C.SMALLS, C.BRANCHW, C.OUTW,
)


def call_a(x_in, cot, gain_rec, gain_mlp, weights, vectors, gate_pack, masks, width, hidden):
    count, model = x_in.shape
    channels = RING * width
    rows = RING * CHUNK
    wide = shape((rows, channels), F32)
    seq = shape((RING, count, model), BF16)
    square = shape((channels, channels), BF16)
    big = shape((RING, hidden, model), BF16)
    lead = (RING, CHUNK + LEAD, channels)
    held = (RING, CHUNK + 8, channels)
    flat = pltpu.VMEM((rows, channels), F32)
    weight = shape((RING, width, model), BF16)
    return pl.pallas_call(
        kernel_a,
        out_shape=[
            shape((count, model), F32), seq, seq, seq,
            weight, weight, weight, big, big, big,
            shape(lead, F32), wide, wide, wide, wide, wide, shape(held, F32), wide,
            shape((rows, channels), BF16), shape((16, channels), F32), square, square,
        ],
        in_specs=vmem(4) + any_space(1) + vmem(3),
        out_specs=vmem(1) + any_space(21),
        scratch_shapes=[
            pltpu.VMEM((RING, count, model), BF16),
            pltpu.VMEM((RING, width, model), BF16),
            pltpu.VMEM((RING, width, model), BF16),
            pltpu.VMEM((RING, width, model), BF16),
            pltpu.VMEM(lead, F32),
            flat, flat,
            pltpu.VMEM((rows, channels), BF16),
            flat, flat, flat, flat, flat, flat,
            pltpu.VMEM(held, F32),
            pltpu.VMEM((rows, channels), BF16),
            pltpu.VMEM((16, channels), F32),
            pltpu.VMEM((channels, channels), BF16),
            pltpu.VMEM((channels, channels), BF16),
            pltpu.VMEM((RING, 8, channels), F32),
            pltpu.VMEM((RING,) + gate_pack.shape, BF16),
            pltpu.VMEM((LEAD, channels), F32),
            pltpu.VMEM((RING, 8, channels), F32),
            pltpu.VMEM((2, RING, 8, channels), F32),
            pltpu.VMEM((RING, count, model), BF16),
        ]
        + ROW_SCRATCH
        + [pltpu.VMEM((count, model), BF16)]
        + sems(200),
        compiler_params=options(1),
    )(x_in, cot, gain_rec, gain_mlp, weights, vectors, gate_pack, masks)


def call_b(seq_mlp, seq_grad, w_gate, w_up, w_down, mixed, cot, gain):
    count, model = mixed.shape
    hidden = w_gate.shape[1]
    rows = RING * CHUNK
    seq = shape((RING, count, model), BF16)
    big = pltpu.VMEM((RING, hidden, model), BF16)
    final = shape((hidden, 256), F32)
    wide = pltpu.VMEM((rows, RING * hidden), BF16)
    pre = pltpu.VMEM((rows, hidden), F32)
    rows_held = pltpu.VMEM((RING, count, model), BF16)
    return pl.pallas_call(
        kernel_b,
        out_shape=[
            shape((count, model), F32),
            seq,
            shape((count, model), BF16),
            shape((RING, hidden, 1024), BF16),
            final,
            final,
            shape((8, model), F32),
        ],
        in_specs=any_space(5) + vmem(3),
        out_specs=vmem(1) + any_space(1) + vmem(1) + any_space(1) + vmem(3),
        scratch_shapes=[
            rows_held, rows_held, big, big, big, pre, pre, pre, wide, wide, wide, rows_held, rows_held,
            pltpu.VMEM((count, model), F32),
            pltpu.VMEM((count, model), BF16),
        ]
        + ROW_SCRATCH * 2
        + scatter_scratch(hidden) * 2
        + scatter_scratch(hidden)[:1]
        + sems(128),
        compiler_params=options(2, 63),
    )(seq_mlp, seq_grad, w_gate, w_up, w_down, mixed, cot, gain)


def call_c(*args):
    w_branch, up_part, g_mixed = args[2], args[14], args[19]
    count, model = g_mixed.shape
    width, hidden = w_branch.shape[1], up_part.shape[1]
    channels = RING * width
    rows = RING * CHUNK
    pack = (RING, 2 * width + 32, 256)
    flat = pltpu.VMEM((rows, channels), F32)
    thin = pltpu.VMEM((rows, channels), BF16)
    rows_held = pltpu.VMEM((RING, count, model), BF16)
    lead = pltpu.VMEM((RING, CHUNK + LEAD, channels), F32)
    weight = pltpu.VMEM((RING, width, model), BF16)
    half = pack[1] // 2
    grad = shape((width, 256), F32)
    return pl.pallas_call(
        kernel_c,
        out_shape=[
            shape((count, model), F32),
            grad,
            grad,
            grad,
            shape((hidden, 256), F32),
            shape(pack[1:], BF16),
            shape((8, model // 4), F32),
        ],
        in_specs=any_space(15) + vmem(8),
        out_specs=vmem(7),
        scratch_shapes=[
            rows_held, rows_held, weight, weight, weight,
            lead, flat, flat, flat, flat, flat,
            pltpu.VMEM((RING, CHUNK + 8, channels), F32),
            flat, thin,
            flat, flat, thin, thin, thin, thin, lead,
            pltpu.VMEM((LEAD, channels), F32),
            pltpu.VMEM((RING, 8, channels), F32),
            pltpu.VMEM((2, RING, 8, channels), F32),
            pltpu.VMEM((2, channels, channels), BF16),
            pltpu.VMEM(pack, BF16),
            pltpu.VMEM((RING, half, 256), BF16),
            pltpu.VMEM((3, half, 256), BF16),
            pltpu.VMEM((RING, half, 256), BF16),
            pltpu.VMEM((16, channels), F32),
            pltpu.VMEM((4, RING, 8, model // 4), F32),
            pltpu.VMEM((8, model), F32),
            pltpu.VMEM((RING, hidden, 1024), BF16),
            weight, weight,
            pltpu.VMEM((count, model), F32),
        ]
        + ROW_SCRATCH
        + scatter_scratch(width) * 3
        + scatter_scratch(hidden)[1:]
        + sems(160),
        compiler_params=options(3, 63),
    )(*args)


def place_rows(rows):
    count, model = rows.shape
    held = rows.reshape(8, count // 8, RING, 2, 256).transpose(1, 0, 3, 2, 4)
    return held.reshape(count, model)


def restore_rows(rows):
    count, model = rows.shape
    held = rows.reshape(count // 8, 8, 2, RING, 256).transpose(1, 0, 3, 2, 4)
    return held.reshape(count, 1, model)


def place_width(vector):
    return vector.reshape(RING, 2, 256).transpose(1, 0, 2).reshape(1, -1)


def restore_width(vector):
    return vector.reshape(2, RING, 256).transpose(1, 0, 2).reshape(-1)


def position_masks(resets, z):
    rows = RING * CHUNK
    flags = jnp.pad(resets.reshape(-1).astype(F32), (8, 24), constant_values=1.0)
    window = lax.dynamic_slice(flags, (z * rows,), (rows + 32,))
    keep = 1.0 - window
    first = keep[8:]
    second = first * keep[7:-1]
    third = second * keep[6:-2]
    columns = jnp.stack([window[8:], first, second, third] + [jnp.zeros_like(first)] * 4, axis=1)

    def steps(start):
        held = columns[start : start + rows].reshape(RING, 8, STEPS, 8)
        return held.transpose(0, 2, 1, 3)

    both = jnp.concatenate([steps(0), steps(STEPS)[:, :3]], axis=1)
    return both.reshape(RING, CHUNK + LEAD, 8)


def on_device(
    inputs,
    resets,
    gain_rec,
    w_branch,
    w_gelu,
    conv_weight,
    conv_bias,
    gate_a_weight,
    gate_a_bias,
    gate_x_weight,
    gate_x_bias,
    decay_param,
    w_out,
    gain_mlp,
    w_gate,
    w_up,
    w_down,
    cotangent,
):
    count, _, model = inputs.shape
    z = lax.axis_index("z")
    width, hidden = w_branch.shape[1], w_gate.shape[1]
    masks = position_masks(resets, z)
    vectors = jnp.concatenate(
        [conv_weight, jnp.stack([conv_bias, gate_a_bias, gate_x_bias, decay_param])], axis=0
    )
    vectors = lax.dynamic_update_slice(jnp.zeros((8, RING * width), F32), vectors, (0, z * width))
    gate_pack = jnp.concatenate([gate_a_weight[0], gate_x_weight[0]], axis=1)
    gate_pack = jnp.pad(gate_pack, ((0, 0), (0, -gate_pack.shape[1] % 128)))
    weights = jnp.concatenate([w_branch, w_gelu, w_out, w_gate, w_up, w_down], axis=1).T
    x_in = place_rows(inputs.reshape(count, model))
    cot = place_rows(cotangent.reshape(count, model))
    gain_rec, gain_mlp = place_width(gain_rec), place_width(gain_mlp)

    (
        mixed, seq_normed, seq_mlp, seq_grad, w_b_all, w_g_all, w_out_all, w_gate_all, w_up_all, w_down_all,
        branch, conv, rate, admit, decay, scaling, states, gelu_pre, gated, params, gate_a, gate_x,
    ) = call_a(x_in, cot, gain_rec, gain_mlp, weights, vectors, gate_pack, masks, width, hidden)
    g_mixed, seq_mixed, output, up_part, grad_gate, grad_down, gain_part = call_b(
        seq_mlp, seq_grad, w_gate_all, w_up_all, w_down_all, mixed, cot, gain_mlp
    )
    g_inputs, grad_branch, grad_gelu, grad_out, grad_up, packed, gains = call_c(
        seq_mixed, seq_normed, w_b_all, w_g_all, w_out_all, branch, conv, rate, admit, decay, scaling,
        states, gelu_pre, gated, up_part, params, gate_a, gate_x, masks, g_mixed, x_in, gain_rec, gain_part,
    )
    packed = packed[:, :width].astype(F32)
    vector = packed[2 * width : 2 * width + 8]
    return (
        restore_rows(output),
        restore_rows(g_inputs),
        restore_width(gains[:4]),
        grad_branch.T,
        grad_gelu.T,
        vector[:4],
        vector[4],
        packed[:width].reshape(1, width, width),
        vector[5],
        packed[width : 2 * width].reshape(1, width, width),
        vector[6],
        vector[7],
        grad_out.T,
        restore_width(gains[4:]),
        grad_gate.T,
        grad_up.T,
        grad_down.T,
    )


def solution(mesh):
    sizes = {"blk": mesh.shape["blk"], "tok": mesh.shape["tok"]}
    grid = Mesh(mesh.devices.reshape(RING, sizes["blk"] // RING, sizes["tok"] // 2, 2), AXES)
    blk, tok = ("z", "y"), ("x", "core")
    in_specs = (
        P(blk, tok, None),
        P(None, tok),
        P(),
        P(tok, blk),
        P(tok, blk),
        P(None, blk),
        P(blk),
        P(blk, None, None),
        P(blk),
        P(blk, None, None),
        P(blk),
        P(blk),
        P(tok, blk),
        P(),
        P(tok, blk),
        P(tok, blk),
        P(tok, blk),
        P(blk, tok, None),
    )
    out_specs = (
        P(blk, tok, None),
        P(blk, tok, None),
        P(),
        P(tok, blk),
        P(tok, blk),
        P(None, blk),
        P(blk),
        P(blk, None, None),
        P(blk),
        P(blk, None, None),
        P(blk),
        P(blk),
        P(tok, blk),
        P(),
        P(tok, blk),
        P(tok, blk),
        P(tok, blk),
    )
    return jax.shard_map(
        on_device, mesh=grid, in_specs=in_specs, out_specs=out_specs, check_vma=False
    )
```

```python
import enum
import math

import jax
import jax.numpy as jnp
from jax import lax
from jax.experimental import pallas as pl
from jax.experimental.pallas import tpu as pltpu
from jax.sharding import Mesh
from jax.sharding import PartitionSpec as P

EPSILON = 1e-06
MESH = pl.DeviceIdType.MESH
AXES = ("z", "y", "x", "core")
GELU_A = math.sqrt(2.0 / math.pi)
GELU_B = 0.044715
F32 = jnp.float32
BF16 = jnp.bfloat16
RING = 4
CHUNK = 128
STEPS = CHUNK // 8
LEAD = 24


def dot_nn(left, right):
    return lax.dot_general(left, right, (((1,), (0,)), ((), ())), preferred_element_type=F32)


def dot_nt(left, right):
    return lax.dot_general(left, right, (((1,), (1,)), ((), ())), preferred_element_type=F32)


def dot_tn(left, right):
    return lax.dot_general(left, right, (((0,), (0,)), ((), ())), preferred_element_type=F32)


def gelu_parts(v):
    t = jnp.tanh(GELU_A * (v + GELU_B * v * v * v))
    return 0.5 * v * (1.0 + t), t


def gelu_slope(v, t):
    return 0.5 * (1.0 + t) + 0.5 * v * (1.0 - t * t) * (GELU_A * (1.0 + 3.0 * GELU_B * v * v))


def one_minus_exp(v):
    series = 1.0 + v * (1.0 / 9.0)
    for order in (8.0, 7.0, 6.0, 5.0, 4.0, 3.0, 2.0):
        series = 1.0 + v * (1.0 / order) * series
    return jnp.where(v > -0.5, -v * series, 1.0 - jnp.exp(v))


def inverse_rms(values):
    return lax.rsqrt(jnp.mean(values * values, axis=-1, keepdims=True) + EPSILON)


def norm_back(grads, values, scale, gain):
    held = grads * gain
    return scale * held - values * (scale * scale * scale) * jnp.mean(held * values, axis=-1, keepdims=True)


def around(axis, size, step):
    return {axis: lax.rem(lax.axis_index(axis) + (step + size), size)}


def turned(index, step):
    return lax.rem(index + (step + RING), RING)


class Links:
    def __init__(self, send, recv):
        self.send, self.recv, self.used = send, recv, 0

    def start(self, src, dst, axis, step):
        copy = pltpu.make_async_remote_copy(
            src_ref=src,
            dst_ref=dst,
            send_sem=self.send.at[self.used],
            recv_sem=self.recv.at[self.used],
            device_id=around(axis, lax.axis_size(axis), step),
            device_id_type=MESH,
        )
        self.used += 1
        copy.start()
        return copy

    def local(self, src, dst):
        copy = pltpu.make_async_copy(src, dst, self.send.at[self.used])
        self.used += 1
        copy.start()
        return copy


def greet():
    barrier = pltpu.get_barrier_semaphore()
    total = 0
    for axis in AXES:
        size = lax.axis_size(axis)
        for step in range(1, size):
            pl.semaphore_signal(barrier, inc=1, device_id=around(axis, size, step), device_id_type=MESH)
            total += 1
    pl.semaphore_wait(barrier, total)


class Task:
    def __init__(self, stages):
        self.stages = stages

    def step(self):
        next(self.stages, None)

    def finish(self):
        for _ in self.stages:
            pass


def strips(count, body, carry=0, size=16):
    def step(i, carry):
        return body(pl.ds(pl.multiple_of(i * size, size), size), carry)

    return lax.fori_loop(0, count // size, step, carry)


def add_rows(out, terms):
    def body(here, carry):
        total = terms[0][here, :].astype(F32)
        for term in terms[1:]:
            total = total + term[here, :].astype(F32)
        out[here, :] = total.astype(out.dtype)
        return carry

    strips(out.shape[0], body)


def gather_weight(links, own, full):
    z, x, core = lax.axis_index("z"), lax.axis_index("x"), lax.axis_index("core")
    rows = own.shape[0]
    half = rows // 2
    mine = pl.ds(pl.multiple_of((core * 4 + x) * 256, 256), 256)
    ours = pl.ds(pl.multiple_of(core * 1024, 1024), 1024)
    top, low = pl.ds(0, half), pl.ds(half, rows - half)
    here = links.local(own, full.at[z, :, mine])
    first_a = [links.start(own.at[top], full.at[z, top, mine], "x", s) for s in (1, 3, 2)]
    first_b = [links.start(own.at[low], full.at[z, low, mine], "z", s) for s in (1, 3, 2)]
    yield
    mates = []

    def share(block):
        mates.append(links.start(block, block, "core", 1))

    def beside(step):
        return full.at[:, low, pl.ds(pl.multiple_of((core * 4 + turned(x, step)) * 256, 256), 256)]

    here.wait()
    for copy in first_a:
        copy.wait_recv()
    block = full.at[z, top, ours]
    second_a = [links.start(block, block, "z", s) for s in (1, -1)]
    share(block)
    for copy in first_b:
        copy.wait_recv()
    block = beside(0)
    second_b = [links.start(block, block, "x", s) for s in (1, -1)]
    share(block)
    yield
    relays = []
    for way in (0, 1):
        step = 1 - 2 * way
        second_a[way].wait_recv()
        lanes = pl.ds(pl.multiple_of(core * 1024 + way * 512, 512), 512)
        block = full.at[turned(z, -step), top, lanes]
        relays.append(links.start(block, block, "z", step))
        second_b[way].wait_recv()
        lanes = pl.ds(pl.multiple_of((core * 4 + turned(x, -step)) * 256, 256), 256)
        block = full.at[pl.ds(2 * way, 2), low, lanes]
        relays.append(links.start(block, block, "x", step))
    for step in (1, -1):
        share(full.at[turned(z, step), top, ours])
        share(beside(step))
    yield
    for copy in relays:
        copy.wait_recv()
    share(full.at[turned(z, 2), top, ours])
    share(beside(2))
    yield
    for copy in mates:
        copy.wait_recv()
    for copy in first_a + first_b + second_a + second_b + relays + mates:
        copy.wait_send()


def spread_gain(gain, row):
    for p in range(8):
        for part in range(2):
            at = placed(p) // 128 + part
            row[:, p * 256 + part * 128 : p * 256 + part * 128 + 128] = gain[at : at + 1, :]


def placed(p):
    return ((p % 4) * 2 + p // 4) * 256


def exchange(inward):
    row = lax.broadcasted_iota(jnp.int32, (CHUNK, CHUNK), 0)
    col = lax.broadcasted_iota(jnp.int32, (CHUNK, CHUNK), 1)
    if inward:
        hit = col == lax.rem(row, 8) * STEPS + row // 8
    else:
        hit = col == lax.rem(row, STEPS) * 8 + row // STEPS
    return jnp.where(hit, 1.0, 0.0).astype(BF16)


def place_rows(source, target):
    pick = exchange(True)
    for p in range(8):
        target[:, p * 256 : (p + 1) * 256] = dot_nn(pick, source[:, placed(p) : placed(p) + 256]).astype(BF16)


def restore_low(source, target):
    pick = exchange(False)
    for p in range(8):
        held = dot_nn(pick, source[:, p * 256 : (p + 1) * 256].astype(BF16))
        target[:, placed(p) : placed(p) + 256] = held.astype(BF16)


def restore_wide(source, target):
    pick = exchange(False)
    for p in range(8):
        value = source[:, p * 256 : (p + 1) * 256]
        high = value.astype(BF16)
        rest = value - high.astype(F32)
        middle = rest.astype(BF16)
        small = (rest - middle.astype(F32)).astype(BF16)
        moved = dot_nn(pick, high) + dot_nn(pick, middle) + dot_nn(pick, small)
        target[:, placed(p) : placed(p) + 256] = moved


def gather_rows(links, seq):
    y = lax.axis_index("y")
    own = seq.at[y]
    first = [links.start(own, own, "y", s) for s in (1, -1)]
    yield
    relays = []
    for way in (0, 1):
        step = 1 - 2 * way
        first[way].wait_recv()
        block = seq.at[turned(y, -step), :, pl.ds(way * 1024, 1024)]
        relays.append(links.start(block, block, "y", step))
    yield
    for copy in relays:
        copy.wait_recv()
    for copy in first + relays:
        copy.wait_send()


def scatter_rows(links, produce, part, far, near, out):
    y = lax.axis_index("y")
    across = turned(y, 2)
    produce(across)
    first = [
        links.start(part.at[across, :, pl.ds(way * 1024, 1024)], far.at[way], "y", 1 - 2 * way)
        for way in (0, 1)
    ]
    yield
    for step in (1, -1):
        produce(turned(y, step))
    yield
    second = []
    for way in (0, 1):
        step = 1 - 2 * way
        first[way].wait_recv()
        chunk = part.at[turned(y, step)]
        half = chunk.at[:, pl.ds(way * 1024, 1024)]
        add_rows(half, [half, far.at[way]])
        second.append(links.start(chunk, near.at[way], "y", step))
    yield
    produce(y)
    yield
    for copy in second:
        copy.wait_recv()
    add_rows(out, [part.at[y], near.at[0], near.at[1]])
    for copy in first + second:
        copy.wait_send()


ROW_SCRATCH = [pltpu.VMEM((2, CHUNK, 1024), BF16), pltpu.VMEM((2, CHUNK, 2048), BF16)]


def share_core(links, part, mate, make):
    core = lax.axis_index("core")
    ours = pl.ds(pl.multiple_of(core * 1024, 1024), 1024)
    theirs = pl.ds(pl.multiple_of((1 - core) * 1024, 1024), 1024)
    across = []
    for n in range(RING):
        if make(n):
            yield
        across.append(links.start(part.at[n, :, theirs], mate.at[n], "core", 1))
    yield
    for n in range(RING):
        across[n].wait_recv()
        held = part.at[n, :, ours]
        add_rows(held, [held, mate.at[n]])
    for copy in across:
        copy.wait_send()


def scatter_weight(links, part, make, mate, far_a, near_a, far_b, near_b, light_a, light_b, out):
    yield from share_core(links, part, mate, make)
    base = lax.axis_index("core") * 1024
    yield from scatter_chips(links, part, base, far_a, near_a, far_b, near_b, light_a, light_b, out)


def scatter_chips(links, part, base, far_a, near_a, far_b, near_b, light_a, light_b, out):
    z, x = lax.axis_index("z"), lax.axis_index("x")
    rows = part.shape[1]
    half = rows // 2
    top, low = pl.ds(0, half), pl.ds(half, rows - half)
    ours = pl.ds(pl.multiple_of(base, 1024), 1024)

    def lanes(place):
        return pl.ds(pl.multiple_of(base + place * 256, 256), 256)

    first = []
    for way in (0, 1):
        step = 1 - 2 * way
        half_lanes = pl.ds(pl.multiple_of(base + way * 512, 512), 512)
        first.append(links.start(part.at[turned(z, 2), top, half_lanes], far_a.at[way], "z", step))
        block = part.at[pl.ds(2 * way, 2), low, lanes(turned(x, 2))]
        first.append(links.start(block, far_b.at[way], "x", step))
    yield
    second = []
    for way in (0, 1):
        step = 1 - 2 * way
        first[2 * way].wait_recv()
        half_lanes = pl.ds(pl.multiple_of(base + way * 512, 512), 512)
        held = part.at[turned(z, step), top, half_lanes]
        add_rows(held, [held, far_a.at[way]])
        second.append(links.start(part.at[turned(z, step), top, ours], near_a.at[way], "z", step))
        first[2 * way + 1].wait_recv()
        for i in range(2):
            held = part.at[2 * way + i, low, lanes(turned(x, step))]
            add_rows(held, [held, far_b.at[way, i]])
        second.append(links.start(part.at[:, low, lanes(turned(x, step))], near_b.at[way], "x", step))
    yield
    for way in (0, 1):
        second[2 * way].wait_recv()
    held = part.at[z, top, ours]
    add_rows(held, [held, near_a.at[0], near_a.at[1]])
    third = []
    for i, step in enumerate((1, 3, 2)):
        third.append(links.start(part.at[z, top, lanes(turned(x, step))], light_a.at[i], "x", step))
    for way in (0, 1):
        second[2 * way + 1].wait_recv()
    for block in range(4):
        held = part.at[block, low, lanes(x)]
        add_rows(held, [held, near_b.at[0, block], near_b.at[1, block]])
    for i, step in enumerate((1, 3, 2)):
        third.append(links.start(part.at[turned(z, step), low, lanes(x)], light_b.at[i], "z", step))
    yield
    for copy in third:
        copy.wait_recv()
    add_rows(out.at[top], [part.at[z, top, lanes(x)]] + [light_a.at[i] for i in range(3)])
    add_rows(out.at[low], [part.at[z, low, lanes(x)]] + [light_b.at[i] for i in range(3)])
    for copy in first + second + third:
        copy.wait_send()


def scatter_scratch(rows):
    half = rows // 2
    return [
        pltpu.VMEM((4, rows, 1024), BF16),
        pltpu.VMEM((2, half, 512), BF16),
        pltpu.VMEM((2, half, 1024), BF16),
        pltpu.VMEM((2, 2, half, 256), BF16),
        pltpu.VMEM((2, 4, half, 256), BF16),
        pltpu.VMEM((3, half, 256), BF16),
        pltpu.VMEM((3, half, 256), BF16),
    ]


SCATTER_REFS = 7


def sum_everywhere(links, slots, axis):
    size = lax.axis_size(axis)
    own = slots.at[lax.axis_index(axis)]
    copies = [links.start(own, own, axis, s) for s in range(1, size)]
    yield
    for copy in copies:
        copy.wait_recv()
    for copy in copies:
        copy.wait_send()


def any_space(count):
    return [pl.BlockSpec(memory_space=pl.ANY)] * count


def vmem(count):
    return [pl.BlockSpec(memory_space=pltpu.VMEM)] * count


def shape(dims, dtype):
    return jax.ShapeDtypeStruct(dims, dtype)


def sems(count):
    return [pltpu.SemaphoreType.DMA((count,)), pltpu.SemaphoreType.DMA((count,))]


def options(number, mib=60):
    return pltpu.CompilerParams(
        collective_id=number, has_side_effects=True, vmem_limit_bytes=mib * 2**20
    )


def spots(q, at, size):
    return pl.ds(pl.multiple_of(q * CHUNK + at, 8), size)


def flat2(ref):
    value = ref[...]
    return value.reshape(value.shape[0] * value.shape[1], value.shape[2])


def column(i, j, low, high, shift):
    row = lax.broadcasted_iota(jnp.int32, (i, j), 0)
    col = lax.broadcasted_iota(jnp.int32, (i, j), 1)
    hit = (col == row + shift) & (row >= low) & (row < high)
    return jnp.where(hit, 1.0, 0.0).astype(BF16)


def gather_small(links, vectors, gates, gate_pack, vector_slots, gate_slots, params, gate_a, gate_x):
    z, core = lax.axis_index("z"), lax.axis_index("core")
    width = gate_pack.shape[0]
    gate_pack[...] = jnp.zeros(gate_pack.shape, BF16)
    gate_pack[:, 0:width] = gates[0][0]
    gate_pack[:, 256 : 256 + width] = gates[1][0]
    half = width // 2
    part = pl.ds(pl.multiple_of(core * half, 16), half)
    here = [
        links.local(vectors, vector_slots.at[z]),
        links.local(gate_pack.at[part], gate_slots.at[z, part]),
    ]
    sent = []
    for step in (1, 3, 2):
        sent.append(links.start(vectors, vector_slots.at[z], "z", step))
        sent.append(links.start(gate_pack.at[part], gate_slots.at[z, part], "z", step))
    yield
    for copy in here:
        copy.wait()
    for copy in sent:
        copy.wait_recv()
    block = gate_slots.at[:, part]
    last = links.start(block, block, "core", 1)
    found = vector_slots[0] + vector_slots[1] + vector_slots[2] + vector_slots[3]
    params[8:16, :] = jnp.zeros_like(found)
    params[0:8, :] = found
    minus = -found[7:8, :]
    params[8:9, :] = jnp.maximum(minus, 0.0) + jnp.log1p(jnp.exp(-jnp.abs(minus)))
    params[9:10, :] = jax.nn.sigmoid(minus)
    yield
    last.wait_recv()
    channels = gate_a.shape[1]
    for place in range(RING):
        rows = pl.ds(place * width, width)
        packed = gate_slots[place]
        size = packed.shape[1]
        pick = column(size, channels, 0, width, place * width)
        gate_a[rows, :] = dot_nn(packed, pick).astype(BF16)
        pick = column(size, channels, 256, 256 + width, place * width - 256)
        gate_x[rows, :] = dot_nn(packed, pick).astype(BF16)
    for copy in sent + [last]:
        copy.wait_send()


def fill_lead(buf, halo, tiles):
    count = tiles * 8
    for q in range(RING):
        for i in range(tiles):
            at = buf.shape[1] - count + i * 8
            tile = buf[q, pl.ds(at, 8), :]
            before = halo[i * 8 + 7 : i * 8 + 8, :] if q == 0 else buf[q - 1, pl.ds(at + 7, 1), :]
            buf[q, pl.ds(i * 8, 8), :] = jnp.concatenate([before, tile[:7, :]], axis=0)


def fill_tail(buf, halo, tiles):
    for q in range(RING):
        for i in range(tiles):
            tile = buf[q, pl.ds(i * 8, 8), :]
            after = halo[i * 8 : i * 8 + 1, :] if q == RING - 1 else buf[q + 1, pl.ds(i * 8, 1), :]
            buf[q, pl.ds(CHUNK + i * 8, 8), :] = jnp.concatenate([tile[1:, :], after], axis=0)


def conv_taps(branch, masks, params, conv, low):
    for q in range(RING):

        def taps(here, carry):
            at = here.start
            mask = masks[q, here, :]
            total = params[4:5, :] + params[0:1, :] * branch[q, pl.ds(pl.multiple_of(at + LEAD, 8), 32), :]
            for k in range(1, 4):
                moved = branch[q, pl.ds(pl.multiple_of(at + LEAD - 8 * k, 8), 32), :]
                total = total + params[k : k + 1, :] * (moved * mask[:, k : k + 1])
            conv[spots(q, at, 32), :] = total
            low[spots(q, at, 32), :] = total.astype(BF16)
            return carry

        strips(CHUNK, taps, size=32)


def gate_values(masks, params, conv, rate, admit, decay, scaling, local):
    for q in range(RING):

        def point(here, carry):
            spot = spots(q, here.start, 32)
            restart = masks[q, here, 0:1] > 0.5
            rated = jax.nn.sigmoid(rate[spot, :] + params[5:6, :])
            admitted = jax.nn.sigmoid(admit[spot, :] + params[6:7, :])
            log_decay = -8.0 * rated * params[8:9, :]
            scaled = jnp.where(restart, 1.0, jnp.sqrt(one_minus_exp(2.0 * log_decay)))
            rate[spot, :] = rated
            admit[spot, :] = admitted
            decay[spot, :] = jnp.where(restart, 0.0, jnp.exp(log_decay))
            scaling[spot, :] = scaled
            local[spot, :] = scaled * admitted * conv[spot, :]
            return carry

        strips(CHUNK, point, size=32)


def scan_start(channels):
    return (jnp.zeros((8, channels), F32), jnp.ones((8, channels), F32)) * RING


def scan_forward(decay, local, product):
    def step(j, carry):
        kept = []
        for q in range(RING):
            here = spots(q, j * 8, 8)
            rated = decay[here, :]
            state = rated * carry[2 * q] + local[here, :]
            prod = rated * carry[2 * q + 1]
            local[here, :] = state
            product[here, :] = prod
            kept += [state, prod]
        return tuple(kept)

    return lax.fori_loop(0, STEPS, step, scan_start(local.shape[1]))


def scan_backward(decay, local, product):
    def step(i, carry):
        kept = []
        for q in range(RING):
            here = spots(q, (STEPS - 1 - i) * 8, 8)
            rated = decay[here, :]
            total = local[here, :] + carry[2 * q]
            local[here, :] = total
            product[here, :] = carry[2 * q + 1]
            kept += [rated * total, rated * carry[2 * q + 1]]
        return tuple(kept)

    return lax.fori_loop(0, STEPS, step, scan_start(local.shape[1]))


def join_segments(ends, heads, totals, order):
    channels = totals.shape[2]
    prod, state = jnp.ones((1, channels), F32), jnp.zeros((1, channels), F32)
    for q in order(RING):
        for s in order(8):
            heads[0, q, s : s + 1, :] = prod
            heads[1, q, s : s + 1, :] = state
            rated = ends[2 * q + 1][s : s + 1, :]
            state = rated * state + ends[2 * q][s : s + 1, :]
            prod = rated * prod
    totals[0, 0:1, :] = prod
    totals[0, 1:2, :] = state


def share_totals(links, totals, way):
    return [links.start(totals.at[0], totals.at[step], "z", way * step) for step in range(1, RING)]


def entering_state(copies, totals, way):
    z = lax.axis_index("z")
    for copy in copies:
        copy.wait()
    entering = jnp.zeros((1, totals.shape[2]), F32)
    for step in range(RING - 1, 0, -1):
        later = totals[step, 0:1, :] * entering + totals[step, 1:2, :]
        valid = z - step >= 0 if way > 0 else z + step < RING
        entering = jnp.where(valid, later, entering)
    return entering


def spread_head(heads, q, entering):
    tile = heads[0, q] * entering + heads[1, q]
    return jnp.concatenate([tile] * 4, axis=0)


def follow(plan, actions):
    for name in plan:
        actions[name]()


class A(enum.IntEnum):
    SMALL, WB, WG, WO, W1, W2, W3, NORM, ROWS, COTS, BRANCH, GELU, EDGE, CONV, GATES, POINT, SCAN, FIX, SUMS, RENORM, MLP = range(21)


def kernel_a(
    x_raw, cot_raw, gain_rec_in, gain_mlp_in, vectors, gate_a_in, gate_x_in, masks, *more,
):
    weights, more = more[:6], more[6:]
    kernel_a_body(
        x_raw, cot_raw, gain_rec_in, gain_mlp_in, weights, vectors, (gate_a_in, gate_x_in), masks, *more
    )


def kernel_a_body(
    x_raw, cot_raw, gain_rec_in, gain_mlp_in, weights, vectors, gates_in, masks,
    mixed_out, x_out, seq_normed, seq_mlp, seq_grad, wb_out, wg_out, out_out, gate_out, up_out, down_out,
    branch_out, conv_out, rate_out, admit_out, decay_out, scaling_out, states_out, gelu_out, gated_out,
    params_out, gate_a_out, gate_x_out,
    mixed, x_in, cot, cot_held, gain_rec, gain_mlp, gate_pack,
    seq, w_branch, w_gelu, w_out, branch, gelu_pre, conv, low, rate, admit, decay, scaling, local, product,
    states, gated, params, gate_a, gate_x, vector_slots, gate_slots, halo, totals, heads, part, far, near, normed,
    send, recv,
):
    links = Links(send, recv)
    y = lax.axis_index("y")
    count = x_in.shape[0]
    width = vectors.shape[1] // RING
    load_cot = links.local(cot_raw, cot_held)
    place_rows(x_raw, x_in)
    spread_gain(gain_rec_in, gain_rec)
    spread_gain(gain_mlp_in, gain_mlp)
    greet()
    saves, kept = [], {}

    def save(*pairs):
        for source, target in pairs:
            saves.append(links.local(source, target))

    def norm():
        def body(here, carry):
            values = x_in[here, :].astype(F32)
            seq[y, here, :] = (values * inverse_rms(values) * gain_rec[...]).astype(BF16)
            return carry

        strips(count, body)

    def cots():
        load_cot.wait()
        place_rows(cot_held, cot)
        own_cot = links.local(cot, seq_grad.at[y])
        save((x_in, x_out))
        yield
        own_cot.wait()
        yield from gather_rows(links, seq_grad)

    def to_branch():
        result = dot_nt(flat2(seq), flat2(w_branch))
        for q in range(RING):
            branch[q, LEAD:, :] = result[q * CHUNK : (q + 1) * CHUNK, :]
        kept["edge"] = links.start(branch.at[RING - 1, pl.ds(CHUNK, LEAD)], halo, "z", 1)

    def to_gelu():
        gelu_pre[...] = dot_nt(flat2(seq), flat2(w_gelu))

    def edge():
        kept["edge"].wait()
        fill_lead(branch, halo, 3)

    def conv_all():
        conv_taps(branch, masks, params, conv, low)

    def gates():
        rate[...] = dot_nn(low[...], gate_a[...])
        admit[...] = dot_nn(low[...], gate_x[...])

    def point_all():
        gate_values(masks, params, conv, rate, admit, decay, scaling, local)

    def scan():
        ends = scan_forward(decay, local, product)
        join_segments(ends, heads, totals, range)
        kept["totals"] = share_totals(links, totals, 1)

    def fix_all():
        entering = entering_state(kept["totals"], totals, 1)
        for q in range(RING):
            head = spread_head(heads, q, entering)

            def fix(here, carry):
                spot = spots(q, here.start, 32)
                state = local[spot, :] + product[spot, :] * head
                states[q, pl.ds(pl.multiple_of(here.start + 8, 8), 32), :] = state
                gated[spot, :] = (state * gelu_parts(gelu_pre[spot, :])[0]).astype(BF16)
                return carry

            strips(CHUNK, fix, size=32)
        halo[0:8, :] = jnp.broadcast_to(entering, (8, entering.shape[1]))
        fill_lead(states, halo, 1)
        save(
            (seq, seq_normed), (w_branch, wb_out), (w_gelu, wg_out), (params, params_out),
            (gate_a, gate_a_out), (gate_x, gate_x_out), (branch, branch_out), (gelu_pre, gelu_out),
            (conv, conv_out), (rate, rate_out), (admit, admit_out), (decay, decay_out), (scaling, scaling_out),
            (states, states_out), (gated, gated_out),
        )

    def produce(q):
        spot = pl.ds(pl.multiple_of(q * CHUNK, CHUNK), CHUNK)
        part[q] = dot_nn(gated[spot, :], flat2(w_out)).astype(BF16)

    def renorm_all():
        def renorm(here, carry):
            values = x_in[here, :].astype(F32) + mixed[here, :]
            mixed[here, :] = values
            normed[here, :] = (values * inverse_rms(values) * gain_mlp[...]).astype(BF16)
            return carry

        strips(count, renorm)
        links.local(normed, seq_mlp.at[y]).wait()
        save((w_out, out_out), (mixed, mixed_out))

    tasks = {
        A.SMALL: gather_small(links, vectors, gates_in, gate_pack, vector_slots, gate_slots, params, gate_a, gate_x),
        A.ROWS: gather_rows(links, seq),
        A.COTS: cots(),
        A.SUMS: scatter_rows(links, produce, part, far, near, mixed),
        A.MLP: gather_rows(links, seq_mlp),
    }
    fulls = (w_branch, w_gelu, w_out, gate_out, up_out, down_out)
    for i, name in enumerate((A.WB, A.WG, A.WO, A.W1, A.W2, A.W3)):
        tasks[name] = gather_weight(links, weights[i], fulls[i])
    tasks = {name: Task(stages) for name, stages in tasks.items()}
    actions = {
        A.NORM: norm, A.BRANCH: to_branch, A.GELU: to_gelu, A.EDGE: edge, A.CONV: conv_all, A.GATES: gates,
        A.POINT: point_all, A.SCAN: scan, A.FIX: fix_all, A.RENORM: renorm_all,
    }
    actions.update({name: task.step for name, task in tasks.items()})
    follow(PLAN_A, actions)
    for task in tasks.values():
        task.finish()
    for copy in saves:
        copy.wait()


class B(enum.IntEnum):
    TILE, SUMS, OUTS, DOWNS, GATES, UPS, BACK, MIXED, OUTSUM = range(9)


def kernel_b(
    seq_mlp, seq_grad, w_gate, w_up, w_down, mixed_in, gain_in,
    g_mixed_out, seq_mixed, output, up_part, gate_grad, down_grad, gain_out,
    mixed, gain, g_mixed, mlp, grads, gate, up, down, pre_gate, pre_up, pre_hidden, hidden, g_gate, g_up,
    part, outs, total, low, far, near, far_out, near_out, *rest,
):
    send, recv = rest[-2:]
    links = Links(send, recv)
    y = lax.axis_index("y")
    count, model = mixed.shape
    width = gate.shape[1]
    load_mlp, load_grads = links.local(seq_mlp, mlp), None
    loads = []
    for n in range(RING):
        loads.append([links.local(w_gate.at[n], gate.at[n]), links.local(w_up.at[n], up.at[n])])
        if n == 0:
            load_grads = links.local(seq_grad, grads)
        loads[n].append(links.local(w_down.at[n], down.at[n]))
    load_mixed = links.local(mixed_in, mixed)
    spread_gain(gain_in, gain)
    greet()
    kept = {}
    ours = pl.ds(pl.multiple_of(lax.axis_index("core") * 1024, 1024), 1024)

    def tiles():
        for n in range(RING):
            if n == 0:
                load_mlp.wait()
            loads[n][0].wait()
            pre_gate[...] = dot_nt(flat2(mlp), gate[n])
            loads[n][1].wait()
            pre_up[...] = dot_nt(flat2(mlp), up[n])
            if n == 0:
                load_grads.wait()
            loads[n][2].wait()
            pre_hidden[...] = dot_nt(flat2(grads), down[n])
            lanes = pl.ds(n * width, width)

            def point(here, carry):
                gates, ups, backs = pre_gate[here, :], pre_up[here, :], pre_hidden[here, :]
                value, tang = gelu_parts(gates)
                hidden[here, lanes] = (value * ups).astype(BF16)
                g_gate[here, lanes] = (backs * ups * gelu_slope(gates, tang)).astype(BF16)
                g_up[here, lanes] = (backs * value).astype(BF16)
                return carry

            strips(RING * CHUNK, point, size=32)
            yield

    def produce(q):
        spot = pl.ds(pl.multiple_of(q * CHUNK, CHUNK), CHUNK)
        result = dot_nn(g_gate[spot, :], flat2(gate)) + dot_nn(g_up[spot, :], flat2(up))
        part[q] = result.astype(BF16)

    def weight_grad(left, right, out):
        def make(n):
            out[n] = dot_tn(left[:, n * width : (n + 1) * width], flat2(right)).astype(BF16)
            return n < RING - 1

        return make

    def out_parts():
        for q in range(RING):
            outs[q] = dot_nn(hidden[q * CHUNK : (q + 1) * CHUNK, :], flat2(down)).astype(BF16)

    def back_all():
        load_mixed.wait()

        def back(here, carry):
            values = mixed[here, :]
            backs = total[here, :]
            scale = inverse_rms(values)
            held = grads[y, here, :].astype(F32) + norm_back(backs, values, scale, gain[...])
            g_mixed[here, :] = held
            low[here, :] = held.astype(BF16)
            new = backs * values * scale
            return carry + new[:8, :] + new[8:, :]

        acc = strips(count, back, jnp.zeros((8, model), F32))
        gain_out[...] = jnp.broadcast_to(jnp.sum(acc, axis=0, keepdims=True), (8, model))
        kept["save"] = links.local(g_mixed, g_mixed_out)
        links.local(low, seq_mixed.at[y]).wait()

    def out_sums():
        yield from scatter_rows(links, lambda q: None, outs, far_out, near_out, total)

        def last(here, carry):
            total[here, :] = mixed[here, :] + total[here, :]
            return carry

        strips(count, last)
        restore_low(total, output)

    def ups():
        yield from share_core(links, up, rest[2 * SCATTER_REFS], weight_grad(g_up, mlp, up))
        copy = links.local(up.at[:, :, ours], up_part)
        yield
        copy.wait()

    tasks = {
        B.TILE: tiles(),
        B.SUMS: scatter_rows(links, produce, part, far, near, total),
        B.DOWNS: scatter_weight(
            links, down, weight_grad(hidden, grads, down), *rest[:SCATTER_REFS], down_grad
        ),
        B.GATES: scatter_weight(
            links, gate, weight_grad(g_gate, mlp, gate), *rest[SCATTER_REFS : 2 * SCATTER_REFS], gate_grad
        ),
        B.UPS: ups(),
        B.MIXED: gather_rows(links, seq_mixed),
        B.OUTSUM: out_sums(),
    }
    tasks = {name: Task(stages) for name, stages in tasks.items()}
    actions = {
        B.OUTS: out_parts, B.BACK: back_all,
    }
    actions.update({name: task.step for name, task in tasks.items()})
    follow(PLAN_B, actions)
    for task in tasks.values():
        task.finish()
    kept["save"].wait()


class C(enum.IntEnum):
    UPS, GATED, POINT, SCAN, OUTW, GELUW, FIX, GATES, SQUARES, CONV, SUMS, BRANCHW, PACK, SMALLS, GAINS, FINISH = range(16)


def kernel_c(
    seq_mixed, seq_normed, wb_in, wg_in, w_out, branch_in, conv_in, rate_in, admit_in, decay_in, scaling_in,
    states_in, gelu_in, gated_in, up_part, params_in, gate_a_in, gate_x_in, masks_in, g_mixed_in, x_saved,
    gain_in, gain_part,
    g_inputs, branch_grad, gelu_grad, out_grad, up_grad, small_out, gain_out,
    params, gate_a, gate_x, masks, g_mixed, x_in, gain,
    seq, normed, w_branch, w_gelu, w_o, branch, conv, rate, admit, decay, scaling, states, gelu_pre, gated,
    local, product, g_gelu, rate_low, admit_low, low, g_conv, halo, totals, heads,
    squares, pack, pack_mate, pack_z, pack_x, small_rows, gain_slots, gain_acc, gain_sum,
    up, branch_part, gelu_part, total, far, near, *rest,
):
    send, recv = rest[-2:]
    links = Links(send, recv)
    count, model = g_mixed.shape
    width = out_grad.shape[0]
    channels = RING * width
    z, x, core = lax.axis_index("z"), lax.axis_index("x"), lax.axis_index("core")
    part, g_branch = seq, low
    loads, kept = {}, {}
    for source, target in (
        (seq_mixed, seq), (w_out, w_o), (gelu_in, gelu_pre), (states_in, states), (up_part, up), (decay_in, decay),
        (masks_in, masks), (params_in, params), (conv_in, conv), (rate_in, rate), (admit_in, admit),
        (scaling_in, scaling), (gated_in, gated), (seq_normed, normed), (gate_a_in, gate_a), (gate_x_in, gate_x),
        (branch_in, branch), (wb_in, w_branch), (wg_in, w_gelu), (x_saved, x_in), (g_mixed_in, g_mixed),
    ):
        loads[id(target)] = links.local(source, target)
    spread_gain(gain_in, gain)
    greet()

    def need(*targets):
        for target in targets:
            copy = loads.pop(id(target), None)
            if copy is not None:
                copy.wait()

    def ups():
        need(up)
        yield from scatter_chips(links, up, 0, *rest[3 * SCATTER_REFS : 4 * SCATTER_REFS - 1], up_grad)

    def to_gated():
        need(seq, w_o)
        product[...] = dot_nt(flat2(seq), flat2(w_o))

    def point_all():
        need(gelu_pre, states)
        for q in range(RING):

            def point(here, carry):
                spot = spots(q, here.start, 32)
                held = product[spot, :]
                pre = gelu_pre[spot, :]
                value, tang = gelu_parts(pre)
                state = states[q, pl.ds(pl.multiple_of(here.start + 8, 8), 32), :]
                g_gelu[spot, :] = (held * state * gelu_slope(pre, tang)).astype(BF16)
                local[spot, :] = held * value
                return carry

            strips(CHUNK, point, size=32)

    def scan():
        need(decay)
        ends = scan_backward(decay, local, product)
        join_segments(ends, heads, totals, lambda n: range(n - 1, -1, -1))
        kept["totals"] = share_totals(links, totals, -1)

    def weight_grad(left, right, out):
        def make(n):
            if n > 0:
                return False
            need(left, right)
            for first, size in ((0, 256), (256, 256), (512, 128)):
                result = dot_tn(left[:, first : first + size], flat2(right)).astype(BF16)
                at = first
                while at < first + size:
                    place, row = at // width, at % width
                    take = min(width - row, first + size - at)
                    out[place, row : row + take, :] = result[at - first : at - first + take, :]
                    at += take
            return False

        return make

    zero = jnp.zeros((8, channels), F32)

    def eights(value):
        return value[0:8, :] + value[8:16, :] + value[16:24, :] + value[24:32, :]

    def fix_all():
        need(conv, rate, admit, scaling, masks, params)
        entering = entering_state(kept["totals"], totals, -1)
        sums = (zero, zero, zero)
        for q in range(RING):
            head = spread_head(heads, q, entering)

            def fix(here, carry):
                spot = spots(q, here.start, 32)
                running = masks[q, here, 0:1] < 0.5
                before = states[q, here, :]
                carried = local[spot, :] + product[spot, :] * head
                rated, admitted, held = rate[spot, :], admit[spot, :], conv[spot, :]
                spread, scaled = decay[spot, :], scaling[spot, :]
                g_log = jnp.where(
                    running, carried * spread * (before - admitted * held * spread / scaled), 0.0
                )
                g_rate = g_log * (-8.0 * params[8:9, :]) * rated * (1.0 - rated)
                driven = carried * scaled * admitted
                g_admit = driven * held * (1.0 - admitted)
                rate_low[spot, :] = g_rate.astype(BF16)
                admit_low[spot, :] = g_admit.astype(BF16)
                low[spot, :] = held.astype(BF16)
                g_conv[q, here, :] = driven
                return carry[0] + eights(g_rate), carry[1] + eights(g_admit), carry[2] + eights(g_log * rated)

            sums = strips(CHUNK, fix, sums, size=32)
        kept["sums"] = sums

    def gates():
        need(gate_a, gate_x)
        back = dot_nt(rate_low[...], gate_a[...]) + dot_nt(admit_low[...], gate_x[...])
        for q in range(RING):
            g_conv[q, 0:CHUNK, :] = g_conv[q, 0:CHUNK, :] + back[q * CHUNK : (q + 1) * CHUNK, :]
        kept["edge"] = links.start(g_conv.at[0, pl.ds(0, LEAD)], halo, "z", -1)

    def gate_squares():
        squares[0] = dot_tn(low[...], rate_low[...]).astype(BF16)
        squares[1] = dot_tn(low[...], admit_low[...]).astype(BF16)

    def conv_all():
        need(branch)
        kept["edge"].wait()
        fill_tail(g_conv, halo, 3)
        taps = (zero,) * 5
        for q in range(RING):

            def conv_back(here, carry):
                at = here.start
                own = g_conv[q, here, :]
                total_here = params[0:1, :] * own
                new = [carry[0] + eights(own * branch[q, pl.ds(pl.multiple_of(at + LEAD, 8), 32), :])]
                for k in range(1, 4):
                    later = pl.ds(pl.multiple_of(at + 8 * k, 8), 32)
                    total_here = total_here + params[k : k + 1, :] * (
                        g_conv[q, later, :] * masks[q, later, k : k + 1]
                    )
                    moved = branch[q, pl.ds(pl.multiple_of(at + LEAD - 8 * k, 8), 32), :]
                    new.append(carry[k] + eights(own * masks[q, here, k : k + 1] * moved))
                new.append(carry[4] + eights(own))
                g_branch[spots(q, at, 32), :] = total_here.astype(BF16)
                return tuple(new)

            taps = strips(CHUNK, conv_back, taps, size=32)
        kept["taps"] = taps
        gain_acc[...] = jnp.zeros((8, model), F32)

    def produce(q):
        need(w_branch, w_gelu, normed)
        spot = pl.ds(pl.multiple_of(q * CHUNK, CHUNK), CHUNK)
        result = dot_nn(g_branch[spot, :], flat2(w_branch)) + dot_nn(g_gelu[spot, :], flat2(w_gelu))
        part[q] = result.astype(BF16)

        def gather_gain(here, carry):
            new = part[q, here, :].astype(F32) * normed[q, here, :].astype(F32)
            gain_acc[...] = gain_acc[...] + new[:8, :] + new[8:, :]
            return carry

        strips(CHUNK, gather_gain)

    def pack_all():
        for i, value in enumerate(kept["taps"] + kept["sums"]):
            row = jnp.sum(value, axis=0, keepdims=True)
            small_rows[i : i + 1, :] = row * 8.0 * params[9:10, :] if i == 7 else row
        small_rows[8:16, :] = jnp.zeros((8, channels), F32)
        size = pack.shape[2]
        for place in range(RING):
            pick = column(channels, size, place * width, (place + 1) * width, -place * width)
            rows_here = pl.ds(place * width, width)
            pack[place, 0:width, :] = dot_nn(squares[0, rows_here, :], pick).astype(BF16)
            pack[place, width : 2 * width, :] = dot_nn(squares[1, rows_here, :], pick).astype(BF16)
            pack[place, 2 * width : 2 * width + 16, :] = dot_nn(small_rows[...].astype(BF16), pick).astype(BF16)
            pack[place, 2 * width + 16 :, :] = jnp.zeros((pack.shape[1] - 2 * width - 16, size), BF16)

    def smalls():
        half = pack.shape[1] // 2
        ours = pl.ds(pl.multiple_of(core * half, 16), half)
        theirs = pl.ds(pl.multiple_of((1 - core) * half, 16), half)
        across = links.start(pack.at[:, theirs], pack_mate, "core", 1)
        yield
        across.wait_recv()
        for place in range(RING):
            held = pack.at[place, ours]
            add_rows(held, [held, pack_mate.at[place]])
        sent = [
            links.start(pack.at[turned(z, step), ours], pack_z.at[i], "z", step)
            for i, step in enumerate((1, 3, 2))
        ]
        yield
        for copy in sent:
            copy.wait_recv()
        add_rows(pack_x.at[x], [pack.at[z, ours]] + [pack_z.at[i] for i in range(3)])
        yield from sum_everywhere(links, pack_x, "x")
        add_rows(small_out.at[ours], [pack_x.at[i] for i in range(RING)])
        held = small_out.at[ours]
        final = links.start(held, held, "core", 1)
        yield
        final.wait()
        for copy in [across] + sent:
            copy.wait_send()

    def gains():
        rec = jnp.sum(gain_acc[...], axis=0, keepdims=True) / gain[...]
        other = gain_part[0:1, :]
        for i in range(4):
            for part in range(2):
                block = 2 * i + part
                at = ((block % 2) * 4 + block // 2) * 256
                lanes = pl.ds(part * 256, 256)
                gain_sum[i : i + 1, lanes] = rec[:, at : at + 256]
                gain_sum[4 + i : 5 + i, lanes] = other[:, at : at + 256]
        for n, axis in enumerate(("y", "z", "x", "core")):
            slots = gain_slots.at[n, pl.ds(0, lax.axis_size(axis))]
            slots[lax.axis_index(axis)] = gain_sum[...]
            yield from sum_everywhere(links, slots, axis)
            found = slots[0]
            for i in range(1, lax.axis_size(axis)):
                found = found + slots[i]
            gain_sum[...] = found
        for i in range(8):
            for part in range(4):
                at = i * 4 + part
                gain_out[at : at + 1, :] = gain_sum[i : i + 1, part * 128 : (part + 1) * 128]

    def finish_all():
        need(x_in, g_mixed)

        def finish(here, carry):
            values = x_in[here, :].astype(F32)
            total[here, :] = g_mixed[here, :] + norm_back(
                total[here, :], values, inverse_rms(values), gain[...]
            )
            return carry

        strips(count, finish)
        restore_wide(total, g_inputs)

    first, second, third = (rest[i * SCATTER_REFS : (i + 1) * SCATTER_REFS] for i in range(3))
    tasks = {
        C.UPS: ups(),
        C.OUTW: scatter_weight(links, w_o, weight_grad(gated, seq, w_o), *first, out_grad),
        C.GELUW: scatter_weight(links, gelu_part, weight_grad(g_gelu, normed, gelu_part), *second, gelu_grad),
        C.BRANCHW: scatter_weight(links, branch_part, weight_grad(g_branch, normed, branch_part), *third, branch_grad),
        C.SUMS: scatter_rows(links, produce, part, far, near, total),
        C.SMALLS: smalls(),
        C.GAINS: gains(),
    }
    tasks = {name: Task(stages) for name, stages in tasks.items()}
    actions = {
        C.GATED: to_gated, C.POINT: point_all, C.SCAN: scan, C.FIX: fix_all, C.GATES: gates,
        C.SQUARES: gate_squares, C.CONV: conv_all, C.PACK: pack_all, C.FINISH: finish_all,
    }
    actions.update({name: task.step for name, task in tasks.items()})
    follow(PLAN_C, actions)
    for task in tasks.values():
        task.finish()


PLAN_A = (
    A.WG, A.WB, A.NORM, A.SMALL, A.ROWS, A.WB, A.WG, A.WB, A.W2, A.SMALL, A.ROWS, A.WB, A.WO, A.COTS, A.WB, A.ROWS, A.COTS, A.WG, A.BRANCH, A.SMALL, A.WO, A.W1, A.EDGE, A.CONV, A.GATES, A.WG, A.POINT, A.WO, A.SCAN, A.WG, A.W3, A.COTS, A.GELU, A.W2, A.WO, A.W1, A.FIX, A.WO, A.SUMS, A.SUMS, A.SUMS, A.W3, A.W2, A.SUMS, A.W1, A.SUMS, A.RENORM, A.MLP, A.COTS, A.W3, A.MLP, A.W2, A.W3, A.W1, A.MLP, A.W3, A.W1, A.W2,
)
PLAN_B = (
    B.TILE, B.TILE, B.TILE, B.TILE, B.SUMS, B.OUTS, B.DOWNS, B.DOWNS, B.OUTSUM, B.OUTSUM, B.DOWNS, B.DOWNS, B.SUMS, B.SUMS, B.DOWNS, B.SUMS, B.GATES, B.OUTSUM, B.DOWNS, B.GATES, B.GATES, B.UPS, B.OUTSUM, B.GATES, B.UPS, B.SUMS, B.GATES, B.UPS, B.DOWNS, B.BACK, B.MIXED, B.GATES, B.UPS, B.OUTSUM, B.UPS, B.MIXED, B.UPS, B.GATES, B.GATES, B.DOWNS, B.MIXED,
)
PLAN_C = (
    C.UPS, C.GATED, C.POINT, C.SCAN, C.UPS, C.GELUW, C.FIX, C.OUTW, C.GATES, C.SQUARES, C.GELUW, C.UPS, C.OUTW, C.CONV, C.SUMS, C.GELUW, C.PACK, C.SMALLS, C.BRANCHW, C.OUTW, C.SUMS, C.SUMS, C.BRANCHW, C.SMALLS, C.OUTW, C.SUMS, C.GELUW, C.GAINS, C.BRANCHW, C.SMALLS, C.OUTW, C.GAINS, C.GAINS, C.SMALLS, C.SUMS, C.BRANCHW, C.FINISH, C.GAINS, C.SMALLS, C.GELUW, C.BRANCHW, C.UPS, C.GAINS,
)


def call_a(x_in, cot, gain_rec, gain_mlp, vectors, gate_a, gate_x, masks, *weights):
    count, model = x_in.shape
    width, hidden = weights[0].shape[0], weights[3].shape[0]
    channels = RING * width
    rows = RING * CHUNK
    wide = shape((rows, channels), F32)
    seq = shape((RING, count, model), BF16)
    square = shape((channels, channels), BF16)
    big = shape((RING, hidden, model), BF16)
    lead = (RING, CHUNK + LEAD, channels)
    held = (RING, CHUNK + 8, channels)
    flat = pltpu.VMEM((rows, channels), F32)
    weight = shape((RING, width, model), BF16)
    return pl.pallas_call(
        kernel_a,
        out_shape=[
            shape((count, model), F32), shape((count, model), BF16), seq, seq, seq,
            weight, weight, weight, big, big, big,
            shape(lead, F32), wide, wide, wide, wide, wide, shape(held, F32), wide,
            shape((rows, channels), BF16), shape((16, channels), F32), square, square,
        ],
        in_specs=vmem(1) + any_space(1) + vmem(2) + vmem(4) + any_space(6),
        out_specs=any_space(23),
        scratch_shapes=[
            pltpu.VMEM((count, model), F32),
            pltpu.VMEM((count, model), BF16),
            pltpu.VMEM((count, model), BF16),
            pltpu.VMEM((count, model), BF16),
            pltpu.VMEM((1, model), F32),
            pltpu.VMEM((1, model), F32),
            pltpu.VMEM((width, 512), BF16),
            pltpu.VMEM((RING, count, model), BF16),
            pltpu.VMEM((RING, width, model), BF16),
            pltpu.VMEM((RING, width, model), BF16),
            pltpu.VMEM((RING, width, model), BF16),
            pltpu.VMEM(lead, F32),
            flat, flat,
            pltpu.VMEM((rows, channels), BF16),
            flat, flat, flat, flat, flat, flat,
            pltpu.VMEM(held, F32),
            pltpu.VMEM((rows, channels), BF16),
            pltpu.VMEM((16, channels), F32),
            pltpu.VMEM((channels, channels), BF16),
            pltpu.VMEM((channels, channels), BF16),
            pltpu.VMEM((RING, 8, channels), F32),
            pltpu.VMEM((RING, width, 512), BF16),
            pltpu.VMEM((LEAD, channels), F32),
            pltpu.VMEM((RING, 8, channels), F32),
            pltpu.VMEM((2, RING, 8, channels), F32),
            pltpu.VMEM((RING, count, model), BF16),
        ]
        + ROW_SCRATCH
        + [pltpu.VMEM((count, model), BF16)]
        + sems(200),
        compiler_params=options(1),
    )(x_in, cot, gain_rec, gain_mlp, vectors, gate_a, gate_x, masks, *weights)


def call_b(seq_mlp, seq_grad, w_gate, w_up, w_down, mixed, gain):
    count, model = mixed.shape
    hidden = w_gate.shape[1]
    rows = RING * CHUNK
    seq = shape((RING, count, model), BF16)
    big = pltpu.VMEM((RING, hidden, model), BF16)
    final = shape((hidden, 256), F32)
    wide = pltpu.VMEM((rows, RING * hidden), BF16)
    pre = pltpu.VMEM((rows, hidden), F32)
    rows_held = pltpu.VMEM((RING, count, model), BF16)
    return pl.pallas_call(
        kernel_b,
        out_shape=[
            shape((count, model), F32),
            seq,
            shape((count, model), BF16),
            shape((RING, hidden, 1024), BF16),
            final,
            final,
            shape((8, model), F32),
        ],
        in_specs=any_space(6) + vmem(1),
        out_specs=any_space(2) + vmem(1) + any_space(1) + vmem(3),
        scratch_shapes=[
            pltpu.VMEM((count, model), F32),
            pltpu.VMEM((1, model), F32),
            pltpu.VMEM((count, model), F32),
            rows_held, rows_held, big, big, big, pre, pre, pre, wide, wide, wide, rows_held, rows_held,
            pltpu.VMEM((count, model), F32),
            pltpu.VMEM((count, model), BF16),
        ]
        + ROW_SCRATCH * 2
        + scatter_scratch(hidden) * 2
        + scatter_scratch(hidden)[:1]
        + sems(128),
        compiler_params=options(2, 63),
    )(seq_mlp, seq_grad, w_gate, w_up, w_down, mixed, gain)


def call_c(*args):
    w_branch, up_part, g_mixed = args[2], args[14], args[19]
    count, model = g_mixed.shape
    width, hidden = w_branch.shape[1], up_part.shape[1]
    channels = RING * width
    rows = RING * CHUNK
    pack = (RING, 2 * width + 32, 256)
    flat = pltpu.VMEM((rows, channels), F32)
    thin = pltpu.VMEM((rows, channels), BF16)
    rows_held = pltpu.VMEM((RING, count, model), BF16)
    lead = pltpu.VMEM((RING, CHUNK + LEAD, channels), F32)
    weight = pltpu.VMEM((RING, width, model), BF16)
    half = pack[1] // 2
    grad = shape((width, 256), F32)
    return pl.pallas_call(
        kernel_c,
        out_shape=[
            shape((count, model), F32),
            grad,
            grad,
            grad,
            shape((hidden, 256), F32),
            shape(pack[1:], BF16),
            shape((32, 128), F32),
        ],
        in_specs=any_space(21) + vmem(2),
        out_specs=vmem(7),
        scratch_shapes=[
            pltpu.VMEM((16, channels), F32),
            pltpu.VMEM((channels, channels), BF16),
            pltpu.VMEM((channels, channels), BF16),
            pltpu.VMEM(args[18].shape, F32),
            pltpu.VMEM((count, model), F32),
            pltpu.VMEM((count, model), BF16),
            pltpu.VMEM((1, model), F32),
            rows_held, rows_held, weight, weight, weight,
            lead, flat, flat, flat, flat, flat,
            pltpu.VMEM((RING, CHUNK + 8, channels), F32),
            flat, thin,
            flat, flat, thin, thin, thin, thin, lead,
            pltpu.VMEM((LEAD, channels), F32),
            pltpu.VMEM((RING, 8, channels), F32),
            pltpu.VMEM((2, RING, 8, channels), F32),
            pltpu.VMEM((2, channels, channels), BF16),
            pltpu.VMEM(pack, BF16),
            pltpu.VMEM((RING, half, 256), BF16),
            pltpu.VMEM((3, half, 256), BF16),
            pltpu.VMEM((RING, half, 256), BF16),
            pltpu.VMEM((16, channels), F32),
            pltpu.VMEM((4, RING, 8, model // 4), F32),
            pltpu.VMEM((8, model), F32),
            pltpu.VMEM((8, model // 4), F32),
            pltpu.VMEM((RING, hidden, 1024), BF16),
            weight, weight,
            pltpu.VMEM((count, model), F32),
        ]
        + ROW_SCRATCH
        + scatter_scratch(width) * 3
        + scatter_scratch(hidden)[1:]
        + sems(160),
        compiler_params=options(3, 63),
    )(*args)


def position_masks(resets, z):
    rows = RING * CHUNK
    flags = jnp.pad(resets.reshape(-1).astype(F32), (8, 24), constant_values=1.0)
    window = lax.dynamic_slice(flags, (z * rows,), (rows + 32,))
    keep = 1.0 - window
    first = keep[8:]
    second = first * keep[7:-1]
    third = second * keep[6:-2]
    columns = jnp.stack([window[8:], first, second, third] + [jnp.zeros_like(first)] * 4, axis=1)

    def steps(start):
        held = columns[start : start + rows].reshape(RING, 8, STEPS, 8)
        return held.transpose(0, 2, 1, 3)

    both = jnp.concatenate([steps(0), steps(STEPS)[:, :3]], axis=1)
    return both.reshape(RING, CHUNK + LEAD, 8)


def on_device(
    inputs,
    resets,
    gain_rec,
    w_branch,
    w_gelu,
    conv_weight,
    conv_bias,
    gate_a_weight,
    gate_a_bias,
    gate_x_weight,
    gate_x_bias,
    decay_param,
    w_out,
    gain_mlp,
    w_gate,
    w_up,
    w_down,
    cotangent,
):
    count, _, model = inputs.shape
    z = lax.axis_index("z")
    width = w_branch.shape[1]
    masks = position_masks(resets, z)
    vectors = jnp.concatenate(
        [conv_weight, jnp.stack([conv_bias, gate_a_bias, gate_x_bias, decay_param])], axis=0
    )
    vectors = lax.dynamic_update_slice(jnp.zeros((8, RING * width), F32), vectors, (0, z * width))
    weights = [w.T for w in (w_branch, w_gelu, w_out, w_gate, w_up, w_down)]
    gain_rec, gain_mlp = gain_rec.reshape(-1, 128), gain_mlp.reshape(-1, 128)
    (
        mixed, x_placed, seq_normed, seq_mlp, seq_grad,
        w_b_all, w_g_all, w_out_all, w_gate_all, w_up_all, w_down_all,
        branch, conv, rate, admit, decay, scaling, states, gelu_pre, gated, params, gate_a, gate_x,
    ) = call_a(
        inputs.reshape(count, model), cotangent.reshape(count, model), gain_rec, gain_mlp, vectors,
        gate_a_weight, gate_x_weight, masks, *weights,
    )
    g_mixed, seq_mixed, output, up_part, grad_gate, grad_down, gain_part = call_b(
        seq_mlp, seq_grad, w_gate_all, w_up_all, w_down_all, mixed, gain_mlp
    )
    g_inputs, grad_branch, grad_gelu, grad_out, grad_up, packed, gains = call_c(
        seq_mixed, seq_normed, w_b_all, w_g_all, w_out_all, branch, conv, rate, admit, decay, scaling,
        states, gelu_pre, gated, up_part, params, gate_a, gate_x, masks, g_mixed, x_placed, gain_rec, gain_part,
    )
    packed = packed[:, :width].astype(F32)
    vector = packed[2 * width : 2 * width + 8]
    return (
        output.reshape(count, 1, model),
        g_inputs.reshape(count, 1, model),
        gains[:16].reshape(-1),
        grad_branch.T,
        grad_gelu.T,
        vector[:4],
        vector[4],
        packed[:width].reshape(1, width, width),
        vector[5],
        packed[width : 2 * width].reshape(1, width, width),
        vector[6],
        vector[7],
        grad_out.T,
        gains[16:].reshape(-1),
        grad_gate.T,
        grad_up.T,
        grad_down.T,
    )


def solution(mesh):
    sizes = {"blk": mesh.shape["blk"], "tok": mesh.shape["tok"]}
    grid = Mesh(mesh.devices.reshape(RING, sizes["blk"] // RING, sizes["tok"] // 2, 2), AXES)
    blk, tok = ("z", "y"), ("x", "core")
    in_specs = (
        P(blk, tok, None),
        P(None, tok),
        P(),
        P(tok, blk),
        P(tok, blk),
        P(None, blk),
        P(blk),
        P(blk, None, None),
        P(blk),
        P(blk, None, None),
        P(blk),
        P(blk),
        P(tok, blk),
        P(),
        P(tok, blk),
        P(tok, blk),
        P(tok, blk),
        P(blk, tok, None),
    )
    out_specs = (
        P(blk, tok, None),
        P(blk, tok, None),
        P(),
        P(tok, blk),
        P(tok, blk),
        P(None, blk),
        P(blk),
        P(blk, None, None),
        P(blk),
        P(blk, None, None),
        P(blk),
        P(blk),
        P(tok, blk),
        P(),
        P(tok, blk),
        P(tok, blk),
        P(tok, blk),
    )
    return jax.shard_map(
        on_device, mesh=grid, in_specs=in_specs, out_specs=out_specs, check_vma=False
    )
```

```python
import enum
import math

import jax
import jax.numpy as jnp
from jax import lax
from jax.experimental import pallas as pl
from jax.experimental.pallas import tpu as pltpu
from jax.sharding import Mesh
from jax.sharding import PartitionSpec as P

EPSILON = 1e-06
MESH = pl.DeviceIdType.MESH
AXES = ("z", "y", "x", "core")
GELU_A = math.sqrt(2.0 / math.pi)
GELU_B = 0.044715
F32 = jnp.float32
BF16 = jnp.bfloat16
RING = 4
CHUNK = 128
STEPS = CHUNK // 8
LEAD = 24


def dot_nn(left, right):
    return lax.dot_general(left, right, (((1,), (0,)), ((), ())), preferred_element_type=F32)


def dot_nt(left, right):
    return lax.dot_general(left, right, (((1,), (1,)), ((), ())), preferred_element_type=F32)


def dot_tn(left, right):
    return lax.dot_general(left, right, (((0,), (0,)), ((), ())), preferred_element_type=F32)


def gelu_parts(v):
    t = jnp.tanh(GELU_A * (v + GELU_B * v * v * v))
    return 0.5 * v * (1.0 + t), t


def gelu_slope(v, t):
    return 0.5 * (1.0 + t) + 0.5 * v * (1.0 - t * t) * (GELU_A * (1.0 + 3.0 * GELU_B * v * v))


def one_minus_exp(v):
    series = 1.0 + v * (1.0 / 9.0)
    for order in (8.0, 7.0, 6.0, 5.0, 4.0, 3.0, 2.0):
        series = 1.0 + v * (1.0 / order) * series
    return jnp.where(v > -0.5, -v * series, 1.0 - jnp.exp(v))


def inverse_rms(values):
    return lax.rsqrt(jnp.mean(values * values, axis=-1, keepdims=True) + EPSILON)


def norm_back(grads, values, scale, gain):
    held = grads * gain
    return scale * held - values * (scale * scale * scale) * jnp.mean(held * values, axis=-1, keepdims=True)


def around(axis, size, step):
    return {axis: lax.rem(lax.axis_index(axis) + (step + size), size)}


def turned(index, step):
    return lax.rem(index + (step + RING), RING)


class Links:
    def __init__(self, send, recv):
        self.send, self.recv, self.used = send, recv, 0

    def start(self, src, dst, axis, step):
        copy = pltpu.make_async_remote_copy(
            src_ref=src,
            dst_ref=dst,
            send_sem=self.send.at[self.used],
            recv_sem=self.recv.at[self.used],
            device_id=around(axis, lax.axis_size(axis), step),
            device_id_type=MESH,
        )
        self.used += 1
        copy.start()
        return copy

    def local(self, src, dst):
        copy = pltpu.make_async_copy(src, dst, self.send.at[self.used])
        self.used += 1
        copy.start()
        return copy


def greet():
    barrier = pltpu.get_barrier_semaphore()
    total = 0
    for axis in AXES:
        size = lax.axis_size(axis)
        for step in range(1, size):
            pl.semaphore_signal(barrier, inc=1, device_id=around(axis, size, step), device_id_type=MESH)
            total += 1
    pl.semaphore_wait(barrier, total)


class Task:
    def __init__(self, stages):
        self.stages = stages

    def step(self):
        next(self.stages, None)

    def finish(self):
        for _ in self.stages:
            pass


def strips(count, body, carry=0, size=16):
    def step(i, carry):
        return body(pl.ds(pl.multiple_of(i * size, size), size), carry)

    return lax.fori_loop(0, count // size, step, carry)


def add_rows(out, terms):
    def body(here, carry):
        total = terms[0][here, :].astype(F32)
        for term in terms[1:]:
            total = total + term[here, :].astype(F32)
        out[here, :] = total.astype(out.dtype)
        return carry

    strips(out.shape[0], body)


def gather_weight(links, own, full):
    z, x, core = lax.axis_index("z"), lax.axis_index("x"), lax.axis_index("core")
    rows = own.shape[0]
    half = rows // 2
    mine = pl.ds(pl.multiple_of((core * 4 + x) * 256, 256), 256)
    ours = pl.ds(pl.multiple_of(core * 1024, 1024), 1024)
    top, low = pl.ds(0, half), pl.ds(half, rows - half)
    here = links.local(own, full.at[z, :, mine])
    first_a = [links.start(own.at[top], full.at[z, top, mine], "x", s) for s in (1, 3, 2)]
    first_b = [links.start(own.at[low], full.at[z, low, mine], "z", s) for s in (1, 3, 2)]
    yield
    mates = []

    def share(block):
        mates.append(links.start(block, block, "core", 1))

    def beside(step):
        return full.at[:, low, pl.ds(pl.multiple_of((core * 4 + turned(x, step)) * 256, 256), 256)]

    here.wait()
    for copy in first_a:
        copy.wait_recv()
    block = full.at[z, top, ours]
    second_a = [links.start(block, block, "z", s) for s in (1, -1)]
    share(block)
    for copy in first_b:
        copy.wait_recv()
    block = beside(0)
    second_b = [links.start(block, block, "x", s) for s in (1, -1)]
    share(block)
    yield
    relays = []
    for way in (0, 1):
        step = 1 - 2 * way
        second_a[way].wait_recv()
        lanes = pl.ds(pl.multiple_of(core * 1024 + way * 512, 512), 512)
        block = full.at[turned(z, -step), top, lanes]
        relays.append(links.start(block, block, "z", step))
        second_b[way].wait_recv()
        lanes = pl.ds(pl.multiple_of((core * 4 + turned(x, -step)) * 256, 256), 256)
        block = full.at[pl.ds(2 * way, 2), low, lanes]
        relays.append(links.start(block, block, "x", step))
    for step in (1, -1):
        share(full.at[turned(z, step), top, ours])
        share(beside(step))
    yield
    for copy in relays:
        copy.wait_recv()
    share(full.at[turned(z, 2), top, ours])
    share(beside(2))
    yield
    for copy in mates:
        copy.wait_recv()
    for copy in first_a + first_b + second_a + second_b + relays + mates:
        copy.wait_send()


def spread_gain(gain, row):
    for p in range(8):
        for part in range(2):
            at = placed(p) // 128 + part
            row[:, p * 256 + part * 128 : p * 256 + part * 128 + 128] = gain[at : at + 1, :]


def placed(p):
    return ((p % 4) * 2 + p // 4) * 256


def exchange(inward):
    row = lax.broadcasted_iota(jnp.int32, (CHUNK, CHUNK), 0)
    col = lax.broadcasted_iota(jnp.int32, (CHUNK, CHUNK), 1)
    if inward:
        hit = col == lax.rem(row, 8) * STEPS + row // 8
    else:
        hit = col == lax.rem(row, STEPS) * 8 + row // STEPS
    return jnp.where(hit, 1.0, 0.0).astype(BF16)


def place_rows(source, target):
    pick = exchange(True)
    for p in range(8):
        target[:, p * 256 : (p + 1) * 256] = dot_nn(pick, source[:, placed(p) : placed(p) + 256]).astype(BF16)


def restore_low(source, target):
    pick = exchange(False)
    for p in range(8):
        held = dot_nn(pick, source[:, p * 256 : (p + 1) * 256].astype(BF16))
        target[:, placed(p) : placed(p) + 256] = held.astype(BF16)


def restore_wide(source, target):
    pick = exchange(False)
    for p in range(8):
        value = source[:, p * 256 : (p + 1) * 256]
        high = value.astype(BF16)
        rest = value - high.astype(F32)
        middle = rest.astype(BF16)
        small = (rest - middle.astype(F32)).astype(BF16)
        moved = dot_nn(pick, high) + dot_nn(pick, middle) + dot_nn(pick, small)
        target[:, 0, placed(p) : placed(p) + 256] = moved


def gather_rows(links, seq):
    y = lax.axis_index("y")

    def half(place, part):
        return seq.at[place, :, pl.ds(part * 1024, 1024)]

    first = [links.start(half(y, way), half(y, way), "y", 1 - 2 * way) for way in (0, 1)]
    other = [links.start(half(y, 1 - way), half(y, 1 - way), "y", 1 - 2 * way) for way in (0, 1)]
    yield
    relays = []
    for way in (0, 1):
        step = 1 - 2 * way
        first[way].wait_recv()
        block = half(turned(y, -step), way)
        relays.append(links.start(block, block, "y", step))
    yield
    for copy in other + relays:
        copy.wait_recv()
    for copy in first + other + relays:
        copy.wait_send()


def scatter_rows(links, produce, part, far, near, out):
    y = lax.axis_index("y")
    across = turned(y, 2)
    lanes = [pl.ds(way * 1024, 1024) for way in (0, 1)]
    produce(across)
    first = [links.start(part.at[across, :, lanes[way]], far.at[way], "y", 1 - 2 * way) for way in (0, 1)]
    yield
    second = []
    for way in (0, 1):
        step = 1 - 2 * way
        produce(turned(y, step))
        free = lanes[1 - way]
        second.append(links.start(part.at[turned(y, step), :, free], near.at[way, :, free], "y", step))
    yield
    produce(y)
    yield
    for way in (0, 1):
        step = 1 - 2 * way
        first[way].wait_recv()
        held = part.at[turned(y, step), :, lanes[way]]
        add_rows(held, [held, far.at[way]])
        second.append(links.start(held, near.at[way, :, lanes[way]], "y", step))
    yield
    for copy in second:
        copy.wait_recv()
    add_rows(out, [part.at[y], near.at[0], near.at[1]])
    for copy in first + second:
        copy.wait_send()


ROW_SCRATCH = [pltpu.VMEM((2, CHUNK, 1024), BF16), pltpu.VMEM((2, CHUNK, 2048), BF16)]


def share_core(links, part, mate, make):
    core = lax.axis_index("core")
    ours = pl.ds(pl.multiple_of(core * 1024, 1024), 1024)
    theirs = pl.ds(pl.multiple_of((1 - core) * 1024, 1024), 1024)
    across = []
    for n in range(RING):
        if make(n):
            yield
        across.append(links.start(part.at[n, :, theirs], mate.at[n], "core", 1))
    yield
    for n in range(RING):
        across[n].wait_recv()
        held = part.at[n, :, ours]
        add_rows(held, [held, mate.at[n]])
    for copy in across:
        copy.wait_send()


def scatter_weight(links, part, make, mate, far_a, near_a, far_b, near_b, light_a, light_b, out):
    yield from share_core(links, part, mate, make)
    base = lax.axis_index("core") * 1024
    yield from scatter_chips(links, part, base, far_a, near_a, far_b, near_b, light_a, light_b, out)


def scatter_chips(links, part, base, far_a, near_a, far_b, near_b, light_a, light_b, out):
    z, x = lax.axis_index("z"), lax.axis_index("x")
    rows = part.shape[1]
    half = rows // 2
    top, low = pl.ds(0, half), pl.ds(half, rows - half)
    ours = pl.ds(pl.multiple_of(base, 1024), 1024)

    def lanes(place):
        return pl.ds(pl.multiple_of(base + place * 256, 256), 256)

    first = []
    for way in (0, 1):
        step = 1 - 2 * way
        half_lanes = pl.ds(pl.multiple_of(base + way * 512, 512), 512)
        first.append(links.start(part.at[turned(z, 2), top, half_lanes], far_a.at[way], "z", step))
        block = part.at[pl.ds(2 * way, 2), low, lanes(turned(x, 2))]
        first.append(links.start(block, far_b.at[way], "x", step))
    yield
    second = []
    for way in (0, 1):
        step = 1 - 2 * way
        first[2 * way].wait_recv()
        half_lanes = pl.ds(pl.multiple_of(base + way * 512, 512), 512)
        held = part.at[turned(z, step), top, half_lanes]
        add_rows(held, [held, far_a.at[way]])
        second.append(links.start(part.at[turned(z, step), top, ours], near_a.at[way], "z", step))
        first[2 * way + 1].wait_recv()
        for i in range(2):
            held = part.at[2 * way + i, low, lanes(turned(x, step))]
            add_rows(held, [held, far_b.at[way, i]])
        second.append(links.start(part.at[:, low, lanes(turned(x, step))], near_b.at[way], "x", step))
    yield
    for way in (0, 1):
        second[2 * way].wait_recv()
    held = part.at[z, top, ours]
    add_rows(held, [held, near_a.at[0], near_a.at[1]])
    third = []
    for i, step in enumerate((1, 3, 2)):
        third.append(links.start(part.at[z, top, lanes(turned(x, step))], light_a.at[i], "x", step))
    for way in (0, 1):
        second[2 * way + 1].wait_recv()
    for block in range(4):
        held = part.at[block, low, lanes(x)]
        add_rows(held, [held, near_b.at[0, block], near_b.at[1, block]])
    for i, step in enumerate((1, 3, 2)):
        third.append(links.start(part.at[turned(z, step), low, lanes(x)], light_b.at[i], "z", step))
    yield
    for copy in third:
        copy.wait_recv()
    add_rows(out.at[top], [part.at[z, top, lanes(x)]] + [light_a.at[i] for i in range(3)])
    add_rows(out.at[low], [part.at[z, low, lanes(x)]] + [light_b.at[i] for i in range(3)])
    for copy in first + second + third:
        copy.wait_send()


def scatter_scratch(rows):
    half = rows // 2
    return [
        pltpu.VMEM((4, rows, 1024), BF16),
        pltpu.VMEM((2, half, 512), BF16),
        pltpu.VMEM((2, half, 1024), BF16),
        pltpu.VMEM((2, 2, half, 256), BF16),
        pltpu.VMEM((2, 4, half, 256), BF16),
        pltpu.VMEM((3, half, 256), BF16),
        pltpu.VMEM((3, half, 256), BF16),
    ]


SCATTER_REFS = 7


def sum_everywhere(links, slots, axis):
    size = lax.axis_size(axis)
    own = slots.at[lax.axis_index(axis)]
    copies = [links.start(own, own, axis, s) for s in range(1, size)]
    yield
    for copy in copies:
        copy.wait_recv()
    for copy in copies:
        copy.wait_send()


def any_space(count):
    return [pl.BlockSpec(memory_space=pl.ANY)] * count


def vmem(count):
    return [pl.BlockSpec(memory_space=pltpu.VMEM)] * count


def shape(dims, dtype):
    return jax.ShapeDtypeStruct(dims, dtype)


def sems(count):
    return [pltpu.SemaphoreType.DMA((count,)), pltpu.SemaphoreType.DMA((count,))]


def options(number, mib=60):
    return pltpu.CompilerParams(
        collective_id=number, has_side_effects=True, vmem_limit_bytes=mib * 2**20
    )


def spots(q, at, size):
    return pl.ds(pl.multiple_of(q * CHUNK + at, 8), size)


def flat2(ref):
    value = ref[...]
    return value.reshape(value.shape[0] * value.shape[1], value.shape[2])


def column(i, j, low, high, shift):
    row = lax.broadcasted_iota(jnp.int32, (i, j), 0)
    col = lax.broadcasted_iota(jnp.int32, (i, j), 1)
    hit = (col == row + shift) & (row >= low) & (row < high)
    return jnp.where(hit, 1.0, 0.0).astype(BF16)


def gather_small(links, vectors, gates, gate_pack, vector_slots, gate_slots, params, gate_a, gate_x):
    z, core = lax.axis_index("z"), lax.axis_index("core")
    width = gate_pack.shape[0]
    gate_pack[...] = jnp.zeros(gate_pack.shape, BF16)
    gate_pack[:, 0:width] = gates[0][0]
    gate_pack[:, 256 : 256 + width] = gates[1][0]
    half = width // 2
    part = pl.ds(pl.multiple_of(core * half, 16), half)
    here = [
        links.local(vectors, vector_slots.at[z]),
        links.local(gate_pack.at[part], gate_slots.at[z, part]),
    ]
    sent = []
    for step in (1, 3, 2):
        sent.append(links.start(vectors, vector_slots.at[z], "z", step))
        sent.append(links.start(gate_pack.at[part], gate_slots.at[z, part], "z", step))
    yield
    for copy in here:
        copy.wait()
    for copy in sent:
        copy.wait_recv()
    block = gate_slots.at[:, part]
    last = links.start(block, block, "core", 1)
    found = vector_slots[0] + vector_slots[1] + vector_slots[2] + vector_slots[3]
    params[8:16, :] = jnp.zeros_like(found)
    params[0:8, :] = found
    minus = -found[7:8, :]
    params[8:9, :] = jnp.maximum(minus, 0.0) + jnp.log1p(jnp.exp(-jnp.abs(minus)))
    params[9:10, :] = jax.nn.sigmoid(minus)
    yield
    last.wait_recv()
    channels = gate_a.shape[1]
    for place in range(RING):
        rows = pl.ds(place * width, width)
        packed = gate_slots[place]
        size = packed.shape[1]
        pick = column(size, channels, 0, width, place * width)
        gate_a[rows, :] = dot_nn(packed, pick).astype(BF16)
        pick = column(size, channels, 256, 256 + width, place * width - 256)
        gate_x[rows, :] = dot_nn(packed, pick).astype(BF16)
    for copy in sent + [last]:
        copy.wait_send()


def fill_lead(buf, halo, tiles):
    count = tiles * 8
    for q in range(RING):
        for i in range(tiles):
            at = buf.shape[1] - count + i * 8
            tile = buf[q, pl.ds(at, 8), :]
            before = halo[i * 8 + 7 : i * 8 + 8, :] if q == 0 else buf[q - 1, pl.ds(at + 7, 1), :]
            buf[q, pl.ds(i * 8, 8), :] = jnp.concatenate([before, tile[:7, :]], axis=0)


def fill_tail(buf, halo, tiles):
    for q in range(RING):
        for i in range(tiles):
            tile = buf[q, pl.ds(i * 8, 8), :]
            after = halo[i * 8 : i * 8 + 1, :] if q == RING - 1 else buf[q + 1, pl.ds(i * 8, 1), :]
            buf[q, pl.ds(CHUNK + i * 8, 8), :] = jnp.concatenate([tile[1:, :], after], axis=0)


def conv_taps(branch, masks, params, conv, low):
    for q in range(RING):

        def taps(here, carry):
            at = here.start
            mask = masks[q, here, :]
            total = params[4:5, :] + params[0:1, :] * branch[q, pl.ds(pl.multiple_of(at + LEAD, 8), 32), :]
            for k in range(1, 4):
                moved = branch[q, pl.ds(pl.multiple_of(at + LEAD - 8 * k, 8), 32), :]
                total = total + params[k : k + 1, :] * (moved * mask[:, k : k + 1])
            conv[spots(q, at, 32), :] = total
            low[spots(q, at, 32), :] = total.astype(BF16)
            return carry

        strips(CHUNK, taps, size=32)


def gate_values(masks, params, conv, rate, admit, decay, scaling, local):
    for q in range(RING):

        def point(here, carry):
            spot = spots(q, here.start, 32)
            restart = masks[q, here, 0:1] > 0.5
            rated = jax.nn.sigmoid(rate[spot, :] + params[5:6, :])
            admitted = jax.nn.sigmoid(admit[spot, :] + params[6:7, :])
            log_decay = -8.0 * rated * params[8:9, :]
            scaled = jnp.where(restart, 1.0, jnp.sqrt(one_minus_exp(2.0 * log_decay)))
            rate[spot, :] = rated
            admit[spot, :] = admitted
            decay[spot, :] = jnp.where(restart, 0.0, jnp.exp(log_decay))
            scaling[spot, :] = scaled
            local[spot, :] = scaled * admitted * conv[spot, :]
            return carry

        strips(CHUNK, point, size=32)


def scan_start(channels):
    return (jnp.zeros((8, channels), F32), jnp.ones((8, channels), F32)) * RING


def scan_forward(decay, local, product):
    def step(j, carry):
        kept = []
        for q in range(RING):
            here = spots(q, j * 8, 8)
            rated = decay[here, :]
            state = rated * carry[2 * q] + local[here, :]
            prod = rated * carry[2 * q + 1]
            local[here, :] = state
            product[here, :] = prod
            kept += [state, prod]
        return tuple(kept)

    return lax.fori_loop(0, STEPS, step, scan_start(local.shape[1]))


def scan_backward(decay, local, product):
    def step(i, carry):
        kept = []
        for q in range(RING):
            here = spots(q, (STEPS - 1 - i) * 8, 8)
            rated = decay[here, :]
            total = local[here, :] + carry[2 * q]
            local[here, :] = total
            product[here, :] = carry[2 * q + 1]
            kept += [rated * total, rated * carry[2 * q + 1]]
        return tuple(kept)

    return lax.fori_loop(0, STEPS, step, scan_start(local.shape[1]))


def join_segments(ends, heads, totals, order):
    channels = totals.shape[2]
    prod, state = jnp.ones((1, channels), F32), jnp.zeros((1, channels), F32)
    for q in order(RING):
        for s in order(8):
            heads[0, q, s : s + 1, :] = prod
            heads[1, q, s : s + 1, :] = state
            rated = ends[2 * q + 1][s : s + 1, :]
            state = rated * state + ends[2 * q][s : s + 1, :]
            prod = rated * prod
    totals[0, 0:1, :] = prod
    totals[0, 1:2, :] = state


def share_totals(links, totals, way):
    return [links.start(totals.at[0], totals.at[step], "z", way * step) for step in range(1, RING)]


def entering_state(copies, totals, way):
    z = lax.axis_index("z")
    for copy in copies:
        copy.wait()
    entering = jnp.zeros((1, totals.shape[2]), F32)
    for step in range(RING - 1, 0, -1):
        later = totals[step, 0:1, :] * entering + totals[step, 1:2, :]
        valid = z - step >= 0 if way > 0 else z + step < RING
        entering = jnp.where(valid, later, entering)
    return entering


def spread_head(heads, q, entering):
    tile = heads[0, q] * entering + heads[1, q]
    return jnp.concatenate([tile] * 4, axis=0)


def follow(plan, actions):
    for name in plan:
        actions[name]()


class A(enum.IntEnum):
    SMALL, WB, WG, WO, W1, W2, W3, NORM, ROWS, COTS, BRANCH, GELU, EDGE, CONV, GATES, POINT, SCAN, FIX, SUMS, RENORM, MLP, TURN = range(22)


def kernel_a(
    x_raw, cot_raw, gain_rec_in, gain_mlp_in, vectors, gate_a_in, gate_x_in, masks, *more,
):
    weights, more = more[:6], more[6:]
    kernel_a_body(
        x_raw, cot_raw, gain_rec_in, gain_mlp_in, weights, vectors, (gate_a_in, gate_x_in), masks, *more
    )


def kernel_a_body(
    x_raw, cot_raw, gain_rec_in, gain_mlp_in, weights, vectors, gates_in, masks,
    mixed_out, x_out, seq_normed, seq_mlp, seq_grad, wb_out, wg_out, out_out, gate_out, up_out, down_out,
    branch_out, conv_out, rate_out, admit_out, decay_out, scaling_out, states_out, gelu_out, gated_out,
    params_out, gate_a_out, gate_x_out,
    mixed, x_in, cot, cot_held, gain_rec, gain_mlp, gate_pack, wide, turned_wide,
    seq, w_branch, w_gelu, w_out, branch, gelu_pre, conv, low, rate, admit, decay, scaling, local, product,
    states, gated, params, gate_a, gate_x, vector_slots, gate_slots, halo, totals, heads, part, far, near, normed,
    send, recv,
):
    links = Links(send, recv)
    y = lax.axis_index("y")
    count = x_in.shape[0]
    width = vectors.shape[1] // RING
    load_wide = [links.local(weights[3 + i], wide.at[i]) for i in range(3)]
    load_cot = links.local(cot_raw, cot_held)
    place_rows(x_raw, x_in)
    spread_gain(gain_rec_in, gain_rec)
    spread_gain(gain_mlp_in, gain_mlp)
    greet()
    saves, kept = [], {}

    def save(*pairs):
        for source, target in pairs:
            saves.append(links.local(source, target))

    def norm():
        def body(here, carry):
            values = x_in[here, :].astype(F32)
            seq[y, here, :] = (values * inverse_rms(values) * gain_rec[...]).astype(BF16)
            return carry

        strips(count, body)

    def turn():
        same = column(256, 256, 0, 256, 0)
        for i in range(3):
            load_wide[i].wait()
            turned_wide[i] = dot_tn(wide[i], same).astype(BF16)

    def cots():
        load_cot.wait()
        place_rows(cot_held, cot)
        own_cot = links.local(cot, seq_grad.at[y])
        save((x_in, x_out))
        yield
        own_cot.wait()
        yield from gather_rows(links, seq_grad)

    def to_branch():
        result = dot_nt(flat2(seq), flat2(w_branch))
        for q in range(RING):
            branch[q, LEAD:, :] = result[q * CHUNK : (q + 1) * CHUNK, :]
        kept["edge"] = links.start(branch.at[RING - 1, pl.ds(CHUNK, LEAD)], halo, "z", 1)

    def to_gelu():
        gelu_pre[...] = dot_nt(flat2(seq), flat2(w_gelu))

    def edge():
        kept["edge"].wait()
        fill_lead(branch, halo, 3)

    def conv_all():
        conv_taps(branch, masks, params, conv, low)

    def gates():
        rate[...] = dot_nn(low[...], gate_a[...])
        admit[...] = dot_nn(low[...], gate_x[...])

    def point_all():
        gate_values(masks, params, conv, rate, admit, decay, scaling, local)

    def scan():
        ends = scan_forward(decay, local, product)
        join_segments(ends, heads, totals, range)
        kept["totals"] = share_totals(links, totals, 1)

    def fix_all():
        entering = entering_state(kept["totals"], totals, 1)
        for q in range(RING):
            head = spread_head(heads, q, entering)

            def fix(here, carry):
                spot = spots(q, here.start, 32)
                state = local[spot, :] + product[spot, :] * head
                states[q, pl.ds(pl.multiple_of(here.start + 8, 8), 32), :] = state
                gated[spot, :] = (state * gelu_parts(gelu_pre[spot, :])[0]).astype(BF16)
                return carry

            strips(CHUNK, fix, size=32)
        halo[0:8, :] = jnp.broadcast_to(entering, (8, entering.shape[1]))
        fill_lead(states, halo, 1)
        save(
            (seq, seq_normed), (w_branch, wb_out), (w_gelu, wg_out), (params, params_out),
            (gate_a, gate_a_out), (gate_x, gate_x_out), (branch, branch_out), (gelu_pre, gelu_out),
            (conv, conv_out), (rate, rate_out), (admit, admit_out), (decay, decay_out), (scaling, scaling_out),
            (states, states_out), (gated, gated_out),
        )

    def produce(q):
        spot = pl.ds(pl.multiple_of(q * CHUNK, CHUNK), CHUNK)
        part[q] = dot_nn(gated[spot, :], flat2(w_out)).astype(BF16)

    def renorm_all():
        def renorm(here, carry):
            values = x_in[here, :].astype(F32) + mixed[here, :]
            mixed[here, :] = values
            normed[here, :] = (values * inverse_rms(values) * gain_mlp[...]).astype(BF16)
            return carry

        strips(count, renorm)
        links.local(normed, seq_mlp.at[y]).wait()
        save((w_out, out_out), (mixed, mixed_out))

    tasks = {
        A.SMALL: gather_small(links, vectors, gates_in, gate_pack, vector_slots, gate_slots, params, gate_a, gate_x),
        A.ROWS: gather_rows(links, seq),
        A.COTS: cots(),
        A.SUMS: scatter_rows(links, produce, part, far, near, mixed),
        A.MLP: gather_rows(links, seq_mlp),
    }
    fulls = (w_branch, w_gelu, w_out, gate_out, up_out, down_out)
    for i, name in enumerate((A.WB, A.WG, A.WO, A.W1, A.W2, A.W3)):
        own = weights[i] if i < 3 else turned_wide.at[i - 3]
        tasks[name] = gather_weight(links, own, fulls[i])
    tasks = {name: Task(stages) for name, stages in tasks.items()}
    actions = {
        A.NORM: norm, A.BRANCH: to_branch, A.GELU: to_gelu, A.EDGE: edge, A.CONV: conv_all, A.GATES: gates,
        A.POINT: point_all, A.SCAN: scan, A.FIX: fix_all, A.RENORM: renorm_all, A.TURN: turn,
    }
    actions.update({name: task.step for name, task in tasks.items()})
    follow(PLAN_A, actions)
    for task in tasks.values():
        task.finish()
    for copy in saves:
        copy.wait()


class B(enum.IntEnum):
    TILE, SUMS, OUTS, DOWNS, GATES, UPS, BACK, MIXED, OUTSUM = range(9)


def kernel_b(
    seq_mlp, seq_grad, w_gate, w_up, w_down, mixed_in, gain_in,
    g_mixed_out, seq_mixed, output, up_part, gate_grad, down_grad, gain_out,
    mixed, gain, g_mixed, mlp, grads, gate, up, down, pre_gate, pre_up, pre_hidden, hidden, g_gate, g_up,
    part, outs, total, low, far, near, far_out, near_out, *rest,
):
    send, recv = rest[-2:]
    links = Links(send, recv)
    y = lax.axis_index("y")
    count, model = mixed.shape
    width = gate.shape[1]
    pairs = ((w_gate, gate), (w_up, up), (w_down, down))
    loads = [[None] * 3 for _ in range(RING)]

    def load(n, *which):
        for i in which:
            loads[n][i] = links.local(pairs[i][0].at[n], pairs[i][1].at[n])

    load_mlp = links.local(seq_mlp, mlp)
    load(0, 0, 1)
    spread_gain(gain_in, gain)
    greet()
    load_grads = links.local(seq_grad, grads)
    load(0, 2)
    kept = {}
    ours = pl.ds(pl.multiple_of(lax.axis_index("core") * 1024, 1024), 1024)

    size = pre_gate.shape[2]
    count_tiles = RING * width // size

    def wait_for(t, which):
        for n in range(t * size // width, ((t + 1) * size - 1) // width + 1):
            if loads[n][which] is not None:
                loads[n][which].wait()
                loads[n][which] = None

    def tile_rows(ref, t):
        pieces, at = [], t * size
        while at < (t + 1) * size:
            n, row = at // width, at % width
            take = min(width - row, (t + 1) * size - at)
            pieces.append(ref[n, row : row + take, :])
            at += take
        return pieces[0] if len(pieces) == 1 else jnp.concatenate(pieces, axis=0)

    def point(t, first, last):
        lanes, slot = pl.ds(t * size, size), t % 2
        for i in range(first, last):
            here = pl.ds(i * 32, 32)
            gates, ups, backs = pre_gate[slot, here, :], pre_up[slot, here, :], pre_hidden[slot, here, :]
            value, tang = gelu_parts(gates)
            hidden[here, lanes] = (value * ups).astype(BF16)
            g_gate[here, lanes] = (backs * ups * gelu_slope(gates, tang)).astype(BF16)
            g_up[here, lanes] = (backs * value).astype(BF16)

    def tiles():
        load_mlp.wait()
        for t in range(count_tiles + 1):
            steps = ((pre_gate, mlp, gate), (pre_up, mlp, up), (pre_hidden, grads, down))
            for which, (pre, left, right) in enumerate(steps):
                if t < count_tiles:
                    wait_for(t, which)
                    if t == 0 and which == 0:
                        load(1, 0, 1, 2)
                    if t == 0 and which == 2:
                        load_grads.wait()
                        kept["mixed"] = links.local(mixed_in, mixed)
                    if which == 2 and t in (0, 1):
                        load(t + 2, 0, 1, 2)
                    pre[t % 2] = dot_nt(flat2(left), tile_rows(right, t))
                if t > 0:
                    point(t - 1, (0, 5, 10)[which], (5, 10, 16)[which])
            yield

    def produce(q):
        spot = pl.ds(pl.multiple_of(q * CHUNK, CHUNK), CHUNK)
        result = dot_nn(g_gate[spot, :], flat2(gate)) + dot_nn(g_up[spot, :], flat2(up))
        part[q] = result.astype(BF16)

    def weight_grad(left, right, out):
        def make(n):
            out[n] = dot_tn(left[:, n * width : (n + 1) * width], flat2(right)).astype(BF16)
            return n < RING - 1

        return make

    def out_parts():
        for q in range(RING):
            outs[q] = dot_nn(hidden[q * CHUNK : (q + 1) * CHUNK, :], flat2(down)).astype(BF16)

    def back_all():
        kept["mixed"].wait()

        def back(here, carry):
            values = mixed[here, :]
            backs = total[here, :]
            scale = inverse_rms(values)
            held = grads[y, here, :].astype(F32) + norm_back(backs, values, scale, gain[...])
            g_mixed[here, :] = held
            low[here, :] = held.astype(BF16)
            new = backs * values * scale
            return carry + new[:8, :] + new[8:, :]

        acc = strips(count, back, jnp.zeros((8, model), F32))
        gain_out[...] = jnp.broadcast_to(jnp.sum(acc, axis=0, keepdims=True), (8, model))
        kept["save"] = links.local(g_mixed, g_mixed_out)
        links.local(low, seq_mixed.at[y]).wait()

    def out_sums():
        yield from scatter_rows(links, lambda q: None, outs, far_out, near_out, total)

        def last(here, carry):
            total[here, :] = mixed[here, :] + total[here, :]
            return carry

        strips(count, last)
        restore_low(total, output)

    def ups():
        yield from share_core(links, up, rest[2 * SCATTER_REFS], weight_grad(g_up, mlp, up))
        copy = links.local(up.at[:, :, ours], up_part)
        yield
        copy.wait()

    tasks = {
        B.TILE: tiles(),
        B.SUMS: scatter_rows(links, produce, part, far, near, total),
        B.DOWNS: scatter_weight(
            links, down, weight_grad(hidden, grads, down), *rest[:SCATTER_REFS], down_grad
        ),
        B.GATES: scatter_weight(
            links, gate, weight_grad(g_gate, mlp, gate), *rest[SCATTER_REFS : 2 * SCATTER_REFS], gate_grad
        ),
        B.UPS: ups(),
        B.MIXED: gather_rows(links, seq_mixed),
        B.OUTSUM: out_sums(),
    }
    tasks = {name: Task(stages) for name, stages in tasks.items()}
    actions = {
        B.OUTS: out_parts, B.BACK: back_all,
    }
    actions.update({name: task.step for name, task in tasks.items()})
    follow(PLAN_B, actions)
    for task in tasks.values():
        task.finish()
    kept["save"].wait()


class C(enum.IntEnum):
    UPS, GATED, POINT, SCAN, OUTW, GELUW, FIX, GATES, SQUARES, CONV, SUMS, BRANCHW, PACK, SMALLS, GAINS, FINISH = range(16)


def kernel_c(
    seq_mixed, seq_normed, wb_in, wg_in, w_out, branch_in, conv_in, rate_in, admit_in, decay_in, scaling_in,
    states_in, gelu_in, gated_in, up_part, params_in, gate_a_in, gate_x_in, masks_in, g_mixed_in, x_saved,
    gain_in, gain_part,
    g_inputs, branch_grad, gelu_grad, out_grad, up_grad, small_out, gain_out,
    params, gate_a, gate_x, masks, g_mixed, x_in, gain,
    seq, normed, w_branch, w_gelu, w_o, branch, conv, rate, admit, decay, scaling, states, gelu_pre, gated,
    local, product, g_gelu, rate_low, admit_low, low, g_conv, halo, totals, heads,
    squares, pack, pack_mate, pack_z, pack_x, small_rows, gain_slots, gain_acc, gain_sum,
    up, branch_part, gelu_part, total, far, near, *rest,
):
    send, recv = rest[-2:]
    links = Links(send, recv)
    count, model = g_mixed.shape
    width = out_grad.shape[0]
    channels = RING * width
    z, x, core = lax.axis_index("z"), lax.axis_index("x"), lax.axis_index("core")
    part, g_branch = seq, low
    loads, kept = {}, {}
    batches = [
        ((seq_mixed, seq), (w_out, w_o), (up_part, up)),
        ((gelu_in, gelu_pre), (states_in, states), (decay_in, decay)),
        (
            (masks_in, masks), (params_in, params), (conv_in, conv), (rate_in, rate), (admit_in, admit),
            (scaling_in, scaling), (gated_in, gated), (seq_normed, normed), (gate_a_in, gate_a), (gate_x_in, gate_x),
        ),
        (
            (branch_in, branch), (wb_in, w_branch), (wg_in, w_gelu), (x_saved, x_in), (g_mixed_in, g_mixed),
        ),
    ]

    def load_next():
        for source, target in batches.pop(0):
            loads[id(target)] = links.local(source, target)

    load_next()
    spread_gain(gain_in, gain)
    greet()
    load_next()

    def need(*targets):
        for target in targets:
            copy = loads.pop(id(target), None)
            if copy is not None:
                copy.wait()

    def ups():
        need(up)
        yield from scatter_chips(links, up, 0, *rest[3 * SCATTER_REFS : 4 * SCATTER_REFS - 1], up_grad)

    def to_gated():
        need(seq, w_o)
        load_next()
        product[...] = dot_nt(flat2(seq), flat2(w_o))

    def point_all():
        need(gelu_pre, states)
        for q in range(RING):

            def point(here, carry):
                spot = spots(q, here.start, 32)
                held = product[spot, :]
                pre = gelu_pre[spot, :]
                value, tang = gelu_parts(pre)
                state = states[q, pl.ds(pl.multiple_of(here.start + 8, 8), 32), :]
                g_gelu[spot, :] = (held * state * gelu_slope(pre, tang)).astype(BF16)
                local[spot, :] = held * value
                return carry

            strips(CHUNK, point, size=32)

    def scan():
        need(decay)
        load_next()
        ends = scan_backward(decay, local, product)
        join_segments(ends, heads, totals, lambda n: range(n - 1, -1, -1))
        kept["totals"] = share_totals(links, totals, -1)

    def weight_grad(left, right, out):
        def make(n):
            if n > 0:
                return False
            need(left, right)
            for first, size in ((0, 256), (256, 256), (512, 128)):
                result = dot_tn(left[:, first : first + size], flat2(right)).astype(BF16)
                at = first
                while at < first + size:
                    place, row = at // width, at % width
                    take = min(width - row, first + size - at)
                    out[place, row : row + take, :] = result[at - first : at - first + take, :]
                    at += take
            return False

        return make

    zero = jnp.zeros((8, channels), F32)

    def eights(value):
        return value[0:8, :] + value[8:16, :] + value[16:24, :] + value[24:32, :]

    def fix_all():
        need(conv, rate, admit, scaling, masks, params)
        entering = entering_state(kept["totals"], totals, -1)
        sums = (zero, zero, zero)
        for q in range(RING):
            head = spread_head(heads, q, entering)

            def fix(here, carry):
                spot = spots(q, here.start, 32)
                running = masks[q, here, 0:1] < 0.5
                before = states[q, here, :]
                carried = local[spot, :] + product[spot, :] * head
                rated, admitted, held = rate[spot, :], admit[spot, :], conv[spot, :]
                spread, scaled = decay[spot, :], scaling[spot, :]
                g_log = jnp.where(
                    running, carried * spread * (before - admitted * held * spread / scaled), 0.0
                )
                g_rate = g_log * (-8.0 * params[8:9, :]) * rated * (1.0 - rated)
                driven = carried * scaled * admitted
                g_admit = driven * held * (1.0 - admitted)
                rate_low[spot, :] = g_rate.astype(BF16)
                admit_low[spot, :] = g_admit.astype(BF16)
                low[spot, :] = held.astype(BF16)
                g_conv[q, here, :] = driven
                return carry[0] + eights(g_rate), carry[1] + eights(g_admit), carry[2] + eights(g_log * rated)

            sums = strips(CHUNK, fix, sums, size=32)
        kept["sums"] = sums

    def gates():
        need(gate_a, gate_x)
        back = dot_nt(rate_low[...], gate_a[...]) + dot_nt(admit_low[...], gate_x[...])
        for q in range(RING):
            g_conv[q, 0:CHUNK, :] = g_conv[q, 0:CHUNK, :] + back[q * CHUNK : (q + 1) * CHUNK, :]
        kept["edge"] = links.start(g_conv.at[0, pl.ds(0, LEAD)], halo, "z", -1)

    def gate_squares():
        squares[0] = dot_tn(low[...], rate_low[...]).astype(BF16)
        squares[1] = dot_tn(low[...], admit_low[...]).astype(BF16)

    def conv_all():
        need(branch)
        kept["edge"].wait()
        fill_tail(g_conv, halo, 3)
        taps = (zero,) * 5
        for q in range(RING):

            def conv_back(here, carry):
                at = here.start
                own = g_conv[q, here, :]
                total_here = params[0:1, :] * own
                new = [carry[0] + eights(own * branch[q, pl.ds(pl.multiple_of(at + LEAD, 8), 32), :])]
                for k in range(1, 4):
                    later = pl.ds(pl.multiple_of(at + 8 * k, 8), 32)
                    total_here = total_here + params[k : k + 1, :] * (
                        g_conv[q, later, :] * masks[q, later, k : k + 1]
                    )
                    moved = branch[q, pl.ds(pl.multiple_of(at + LEAD - 8 * k, 8), 32), :]
                    new.append(carry[k] + eights(own * masks[q, here, k : k + 1] * moved))
                new.append(carry[4] + eights(own))
                g_branch[spots(q, at, 32), :] = total_here.astype(BF16)
                return tuple(new)

            taps = strips(CHUNK, conv_back, taps, size=32)
        kept["taps"] = taps
        gain_acc[...] = jnp.zeros((8, model), F32)

    def produce(q):
        need(w_branch, w_gelu, normed)
        spot = pl.ds(pl.multiple_of(q * CHUNK, CHUNK), CHUNK)
        result = dot_nn(g_branch[spot, :], flat2(w_branch)) + dot_nn(g_gelu[spot, :], flat2(w_gelu))
        part[q] = result.astype(BF16)

        def gather_gain(here, carry):
            new = part[q, here, :].astype(F32) * normed[q, here, :].astype(F32)
            gain_acc[...] = gain_acc[...] + new[:8, :] + new[8:, :]
            return carry

        strips(CHUNK, gather_gain)

    def pack_all():
        for i, value in enumerate(kept["taps"] + kept["sums"]):
            row = jnp.sum(value, axis=0, keepdims=True)
            small_rows[i : i + 1, :] = row * 8.0 * params[9:10, :] if i == 7 else row
        small_rows[8:16, :] = jnp.zeros((8, channels), F32)
        size = pack.shape[2]
        for place in range(RING):
            pick = column(channels, size, place * width, (place + 1) * width, -place * width)
            rows_here = pl.ds(place * width, width)
            pack[place, 0:width, :] = dot_nn(squares[0, rows_here, :], pick).astype(BF16)
            pack[place, width : 2 * width, :] = dot_nn(squares[1, rows_here, :], pick).astype(BF16)
            pack[place, 2 * width : 2 * width + 16, :] = dot_nn(small_rows[...].astype(BF16), pick).astype(BF16)
            pack[place, 2 * width + 16 :, :] = jnp.zeros((pack.shape[1] - 2 * width - 16, size), BF16)

    def smalls():
        half = pack.shape[1] // 2
        ours = pl.ds(pl.multiple_of(core * half, 16), half)
        theirs = pl.ds(pl.multiple_of((1 - core) * half, 16), half)
        across = links.start(pack.at[:, theirs], pack_mate, "core", 1)
        yield
        across.wait_recv()
        for place in range(RING):
            held = pack.at[place, ours]
            add_rows(held, [held, pack_mate.at[place]])
        sent = [
            links.start(pack.at[turned(z, step), ours], pack_z.at[i], "z", step)
            for i, step in enumerate((1, 3, 2))
        ]
        yield
        for copy in sent:
            copy.wait_recv()
        add_rows(pack_x.at[x], [pack.at[z, ours]] + [pack_z.at[i] for i in range(3)])
        yield from sum_everywhere(links, pack_x, "x")
        add_rows(small_out.at[ours], [pack_x.at[i] for i in range(RING)])
        held = small_out.at[ours]
        final = links.start(held, held, "core", 1)
        yield
        final.wait()
        for copy in [across] + sent:
            copy.wait_send()

    def gains():
        rec = jnp.sum(gain_acc[...], axis=0, keepdims=True) / gain[...]
        other = gain_part[0:1, :]
        for i in range(4):
            for part in range(2):
                block = 2 * i + part
                at = ((block % 2) * 4 + block // 2) * 256
                lanes = pl.ds(part * 256, 256)
                gain_sum[i : i + 1, lanes] = rec[:, at : at + 256]
                gain_sum[4 + i : 5 + i, lanes] = other[:, at : at + 256]
        for n, axis in enumerate(("y", "z", "x", "core")):
            slots = gain_slots.at[n, pl.ds(0, lax.axis_size(axis))]
            slots[lax.axis_index(axis)] = gain_sum[...]
            yield from sum_everywhere(links, slots, axis)
            found = slots[0]
            for i in range(1, lax.axis_size(axis)):
                found = found + slots[i]
            gain_sum[...] = found
        for i in range(8):
            for part in range(4):
                at = i * 4 + part
                gain_out[at : at + 1, :] = gain_sum[i : i + 1, part * 128 : (part + 1) * 128]

    def finish_all():
        need(x_in, g_mixed)

        def finish(here, carry):
            values = x_in[here, :].astype(F32)
            total[here, :] = g_mixed[here, :] + norm_back(
                total[here, :], values, inverse_rms(values), gain[...]
            )
            return carry

        strips(count, finish)
        restore_wide(total, g_inputs)

    first, second, third = (rest[i * SCATTER_REFS : (i + 1) * SCATTER_REFS] for i in range(3))
    tasks = {
        C.UPS: ups(),
        C.OUTW: scatter_weight(links, w_o, weight_grad(gated, seq, w_o), *first, out_grad),
        C.GELUW: scatter_weight(links, gelu_part, weight_grad(g_gelu, normed, gelu_part), *second, gelu_grad),
        C.BRANCHW: scatter_weight(links, branch_part, weight_grad(g_branch, normed, branch_part), *third, branch_grad),
        C.SUMS: scatter_rows(links, produce, part, far, near, total),
        C.SMALLS: smalls(),
        C.GAINS: gains(),
    }
    tasks = {name: Task(stages) for name, stages in tasks.items()}
    actions = {
        C.GATED: to_gated, C.POINT: point_all, C.SCAN: scan, C.FIX: fix_all, C.GATES: gates,
        C.SQUARES: gate_squares, C.CONV: conv_all, C.PACK: pack_all, C.FINISH: finish_all,
    }
    actions.update({name: task.step for name, task in tasks.items()})
    follow(PLAN_C, actions)
    for task in tasks.values():
        task.finish()


def kernel_d(
    output_in, inputs_in, branch_in, gelu_in, out_in, packed, gains, gate_in, up_in, down_in,
    output, g_inputs, branch, gelu, out, gain_rec, gain_mlp, gate, up, down,
    gate_a, gate_x, taps, conv_bias, bias_a, bias_x, decay, sems,
):
    copies = []
    pairs = ((inputs_in, g_inputs), (output_in, output), (branch_in, branch), (gelu_in, gelu), (out_in, out))
    for i, (source, target) in enumerate(pairs):
        copies.append(pltpu.make_async_copy(source, target, sems.at[i]))
        copies[-1].start()
    for source, target in ((gate_in, gate), (up_in, up), (down_in, down)):
        target[...] = source[...].T
    gain_rec[...] = gains[0:16, :]
    gain_mlp[...] = gains[16:32, :]
    width = gate_a.shape[1]
    gate_a[0] = packed[0:width, 0:width].astype(F32)
    gate_x[0] = packed[width : 2 * width, 0:width].astype(F32)
    vectors = packed[2 * width : 2 * width + 16, 0:width].astype(F32)
    taps[...] = vectors[0:4, :]
    for i, target in enumerate((conv_bias, bias_a, bias_x, decay)):
        target[...] = vectors[4 + i : 5 + i, :]
    for copy in copies:
        copy.wait()


PLAN_A = (
    A.WB, A.NORM, A.WO, A.WG, A.ROWS, A.TURN, A.WB, A.SMALL, A.ROWS, A.COTS, A.COTS, A.WB, A.WG, A.WB, A.WO, A.ROWS, A.SMALL, A.WB, A.BRANCH, A.WG, A.W1, A.EDGE, A.SMALL, A.WO, A.W3, A.CONV, A.GATES, A.POINT, A.WG, A.SCAN, A.COTS, A.W2, A.WO, A.WG, A.WO, A.W3, A.GELU, A.FIX, A.W2, A.SUMS, A.SUMS, A.W1, A.SUMS, A.SUMS, A.SUMS, A.W2, A.COTS, A.RENORM, A.W3, A.MLP, A.MLP, A.W1, A.W3, A.W2, A.W1, A.W1, A.W2, A.MLP, A.W3,
)
PLAN_B = (
    B.TILE, B.TILE, B.TILE, B.TILE, B.TILE, B.TILE, B.TILE, B.SUMS, B.OUTS, B.OUTSUM, B.OUTSUM, B.DOWNS, B.OUTSUM, B.DOWNS, B.DOWNS, B.DOWNS, B.DOWNS, B.SUMS, B.SUMS, B.DOWNS, B.GATES, B.GATES, B.SUMS, B.GATES, B.GATES, B.GATES, B.OUTSUM, B.UPS, B.SUMS, B.BACK, B.GATES, B.MIXED, B.UPS, B.OUTSUM, B.UPS, B.UPS, B.MIXED, B.DOWNS, B.GATES, B.DOWNS, B.UPS, B.MIXED, B.GATES, B.UPS,
)
PLAN_C = (
    C.UPS, C.GATED, C.POINT, C.SCAN, C.UPS, C.GELUW, C.OUTW, C.FIX, C.GATES, C.SQUARES, C.OUTW, C.GELUW, C.UPS, C.CONV, C.BRANCHW, C.OUTW, C.PACK, C.SMALLS, C.SUMS, C.BRANCHW, C.SMALLS, C.GELUW, C.SUMS, C.BRANCHW, C.SUMS, C.GAINS, C.SUMS, C.SMALLS, C.GAINS, C.GELUW, C.OUTW, C.SMALLS, C.UPS, C.GAINS, C.BRANCHW, C.SUMS, C.GELUW, C.OUTW, C.GAINS, C.FINISH, C.GAINS, C.SMALLS, C.BRANCHW,
)


def call_a(x_in, cot, gain_rec, gain_mlp, vectors, gate_a, gate_x, masks, *weights):
    count, model = x_in.shape
    width, hidden = weights[0].shape[0], weights[3].shape[1]
    channels = RING * width
    rows = RING * CHUNK
    wide = shape((rows, channels), F32)
    seq = shape((RING, count, model), BF16)
    square = shape((channels, channels), BF16)
    big = shape((RING, hidden, model), BF16)
    lead = (RING, CHUNK + LEAD, channels)
    held = (RING, CHUNK + 8, channels)
    flat = pltpu.VMEM((rows, channels), F32)
    weight = shape((RING, width, model), BF16)
    return pl.pallas_call(
        kernel_a,
        out_shape=[
            shape((count, model), F32), shape((count, model), BF16), seq, seq, seq,
            weight, weight, weight, big, big, big,
            shape(lead, F32), wide, wide, wide, wide, wide, shape(held, F32), wide,
            shape((rows, channels), BF16), shape((16, channels), F32), square, square,
        ],
        in_specs=vmem(1) + any_space(1) + vmem(2) + vmem(4) + any_space(6),
        out_specs=any_space(23),
        scratch_shapes=[
            pltpu.VMEM((count, model), F32),
            pltpu.VMEM((count, model), BF16),
            pltpu.VMEM((count, model), BF16),
            pltpu.VMEM((count, model), BF16),
            pltpu.VMEM((1, model), F32),
            pltpu.VMEM((1, model), F32),
            pltpu.VMEM((width, 512), BF16),
            pltpu.VMEM((3, 256, hidden), BF16),
            pltpu.VMEM((3, hidden, 256), BF16),
            pltpu.VMEM((RING, count, model), BF16),
            pltpu.VMEM((RING, width, model), BF16),
            pltpu.VMEM((RING, width, model), BF16),
            pltpu.VMEM((RING, width, model), BF16),
            pltpu.VMEM(lead, F32),
            flat, flat,
            pltpu.VMEM((rows, channels), BF16),
            flat, flat, flat, flat, flat, flat,
            pltpu.VMEM(held, F32),
            pltpu.VMEM((rows, channels), BF16),
            pltpu.VMEM((16, channels), F32),
            pltpu.VMEM((channels, channels), BF16),
            pltpu.VMEM((channels, channels), BF16),
            pltpu.VMEM((RING, 8, channels), F32),
            pltpu.VMEM((RING, width, 512), BF16),
            pltpu.VMEM((LEAD, channels), F32),
            pltpu.VMEM((RING, 8, channels), F32),
            pltpu.VMEM((2, RING, 8, channels), F32),
            pltpu.VMEM((RING, count, model), BF16),
        ]
        + ROW_SCRATCH
        + [pltpu.VMEM((count, model), BF16)]
        + sems(200),
        compiler_params=options(1),
    )(x_in, cot, gain_rec, gain_mlp, vectors, gate_a, gate_x, masks, *weights)


def call_b(seq_mlp, seq_grad, w_gate, w_up, w_down, mixed, gain):
    count, model = mixed.shape
    hidden = w_gate.shape[1]
    rows = RING * CHUNK
    seq = shape((RING, count, model), BF16)
    big = pltpu.VMEM((RING, hidden, model), BF16)
    final = shape((hidden, 256), F32)
    wide = pltpu.VMEM((rows, RING * hidden), BF16)
    pre = pltpu.VMEM((2, rows, 256), F32)
    rows_held = pltpu.VMEM((RING, count, model), BF16)
    return pl.pallas_call(
        kernel_b,
        out_shape=[
            shape((count, model), F32),
            seq,
            shape((count, model), BF16),
            shape((RING, hidden, 1024), BF16),
            final,
            final,
            shape((8, model), F32),
        ],
        in_specs=any_space(6) + vmem(1),
        out_specs=any_space(2) + vmem(1) + any_space(1) + vmem(3),
        scratch_shapes=[
            pltpu.VMEM((count, model), F32),
            pltpu.VMEM((1, model), F32),
            pltpu.VMEM((count, model), F32),
            rows_held, rows_held, big, big, big, pre, pre, pre, wide, wide, wide, rows_held, rows_held,
            pltpu.VMEM((count, model), F32),
            pltpu.VMEM((count, model), BF16),
        ]
        + ROW_SCRATCH * 2
        + scatter_scratch(hidden) * 2
        + scatter_scratch(hidden)[:1]
        + sems(128),
        compiler_params=options(2, 63),
    )(seq_mlp, seq_grad, w_gate, w_up, w_down, mixed, gain)


def call_c(*args):
    w_branch, up_part, g_mixed = args[2], args[14], args[19]
    count, model = g_mixed.shape
    width, hidden = w_branch.shape[1], up_part.shape[1]
    channels = RING * width
    rows = RING * CHUNK
    pack = (RING, 2 * width + 32, 256)
    flat = pltpu.VMEM((rows, channels), F32)
    thin = pltpu.VMEM((rows, channels), BF16)
    rows_held = pltpu.VMEM((RING, count, model), BF16)
    lead = pltpu.VMEM((RING, CHUNK + LEAD, channels), F32)
    weight = pltpu.VMEM((RING, width, model), BF16)
    half = pack[1] // 2
    grad = shape((width, 256), F32)
    return pl.pallas_call(
        kernel_c,
        out_shape=[
            shape((count, 1, model), F32),
            grad,
            grad,
            grad,
            shape((hidden, 256), F32),
            shape(pack[1:], BF16),
            shape((32, 128), F32),
        ],
        in_specs=any_space(21) + vmem(2),
        out_specs=vmem(7),
        scratch_shapes=[
            pltpu.VMEM((16, channels), F32),
            pltpu.VMEM((channels, channels), BF16),
            pltpu.VMEM((channels, channels), BF16),
            pltpu.VMEM(args[18].shape, F32),
            pltpu.VMEM((count, model), F32),
            pltpu.VMEM((count, model), BF16),
            pltpu.VMEM((1, model), F32),
            rows_held, rows_held, weight, weight, weight,
            lead, flat, flat, flat, flat, flat,
            pltpu.VMEM((RING, CHUNK + 8, channels), F32),
            flat, thin,
            flat, flat, thin, thin, thin, thin, lead,
            pltpu.VMEM((LEAD, channels), F32),
            pltpu.VMEM((RING, 8, channels), F32),
            pltpu.VMEM((2, RING, 8, channels), F32),
            pltpu.VMEM((2, channels, channels), BF16),
            pltpu.VMEM(pack, BF16),
            pltpu.VMEM((RING, half, 256), BF16),
            pltpu.VMEM((3, half, 256), BF16),
            pltpu.VMEM((RING, half, 256), BF16),
            pltpu.VMEM((16, channels), F32),
            pltpu.VMEM((4, RING, 8, model // 4), F32),
            pltpu.VMEM((8, model), F32),
            pltpu.VMEM((8, model // 4), F32),
            pltpu.VMEM((RING, hidden, 1024), BF16),
            weight, weight,
            pltpu.VMEM((count, model), F32),
        ]
        + ROW_SCRATCH
        + scatter_scratch(width) * 3
        + scatter_scratch(hidden)[1:]
        + sems(160),
        compiler_params=options(3, 63),
    )(*args)


def call_d(output, g_inputs, grad_branch, grad_gelu, grad_out, packed, gains, grad_gate, grad_up, grad_down):
    width = grad_branch.shape[0]
    hidden = grad_gate.shape[0]
    thin = shape((width, 256), F32)
    wide = shape((256, hidden), F32)
    gain = shape((16, 128), F32)
    square = shape((1, width, width), F32)
    row = shape((1, width), F32)
    return pl.pallas_call(
        kernel_d,
        out_shape=[
            shape(output.shape, BF16), shape(g_inputs.shape, F32), thin, thin, thin, gain, gain,
            wide, wide, wide, square, square, shape((4, width), F32), row, row, row, row,
        ],
        in_specs=any_space(5) + vmem(5),
        out_specs=any_space(5) + vmem(12),
        scratch_shapes=[pltpu.SemaphoreType.DMA((5,))],
        compiler_params=pltpu.CompilerParams(vmem_limit_bytes=63 * 2**20),
    )(output, g_inputs, grad_branch, grad_gelu, grad_out, packed, gains, grad_gate, grad_up, grad_down)


def position_masks(resets, z):
    rows = RING * CHUNK
    flags = jnp.pad(resets.reshape(-1).astype(F32), (8, 24), constant_values=1.0)
    window = lax.dynamic_slice(flags, (z * rows,), (rows + 32,))
    keep = 1.0 - window
    first = keep[8:]
    second = first * keep[7:-1]
    third = second * keep[6:-2]
    columns = jnp.stack([window[8:], first, second, third] + [jnp.zeros_like(first)] * 4, axis=1)

    def steps(start):
        held = columns[start : start + rows].reshape(RING, 8, STEPS, 8)
        return held.transpose(0, 2, 1, 3)

    both = jnp.concatenate([steps(0), steps(STEPS)[:, :3]], axis=1)
    return both.reshape(RING, CHUNK + LEAD, 8)


def on_device(
    inputs,
    resets,
    gain_rec,
    w_branch,
    w_gelu,
    conv_weight,
    conv_bias,
    gate_a_weight,
    gate_a_bias,
    gate_x_weight,
    gate_x_bias,
    decay_param,
    w_out,
    gain_mlp,
    w_gate,
    w_up,
    w_down,
    cotangent,
):
    count, _, model = inputs.shape
    z = lax.axis_index("z")
    width = w_branch.shape[1]
    masks = position_masks(resets, z)
    vectors = jnp.concatenate(
        [conv_weight, jnp.stack([conv_bias, gate_a_bias, gate_x_bias, decay_param])], axis=0
    )
    vectors = lax.dynamic_update_slice(jnp.zeros((8, RING * width), F32), vectors, (0, z * width))
    weights = [w.T for w in (w_branch, w_gelu, w_out)] + [w_gate, w_up, w_down]
    gain_rec, gain_mlp = gain_rec.reshape(-1, 128), gain_mlp.reshape(-1, 128)
    (
        mixed, x_placed, seq_normed, seq_mlp, seq_grad,
        w_b_all, w_g_all, w_out_all, w_gate_all, w_up_all, w_down_all,
        branch, conv, rate, admit, decay, scaling, states, gelu_pre, gated, params, gate_a, gate_x,
    ) = call_a(
        inputs.reshape(count, model), cotangent.reshape(count, model), gain_rec, gain_mlp, vectors,
        gate_a_weight, gate_x_weight, masks, *weights,
    )
    g_mixed, seq_mixed, output, up_part, grad_gate, grad_down, gain_part = call_b(
        seq_mlp, seq_grad, w_gate_all, w_up_all, w_down_all, mixed, gain_mlp
    )
    g_inputs, grad_branch, grad_gelu, grad_out, grad_up, packed, gains = call_c(
        seq_mixed, seq_normed, w_b_all, w_g_all, w_out_all, branch, conv, rate, admit, decay, scaling,
        states, gelu_pre, gated, up_part, params, gate_a, gate_x, masks, g_mixed, x_placed, gain_rec, gain_part,
    )
    (
        output, g_inputs, grad_branch, grad_gelu, grad_out, gain_rec, gain_mlp, grad_gate, grad_up, grad_down,
        gate_a, gate_x, taps, *rows,
    ) = call_d(output, g_inputs, grad_branch, grad_gelu, grad_out, packed, gains, grad_gate, grad_up, grad_down)
    conv_bias, bias_a, bias_x, decay = (row.reshape(-1) for row in rows)
    return (
        output.reshape(count, 1, model),
        g_inputs,
        gain_rec.reshape(-1),
        grad_branch.T,
        grad_gelu.T,
        taps,
        conv_bias,
        gate_a,
        bias_a,
        gate_x,
        bias_x,
        decay,
        grad_out.T,
        gain_mlp.reshape(-1),
        grad_gate,
        grad_up,
        grad_down,
    )


def solution(mesh):
    sizes = {"blk": mesh.shape["blk"], "tok": mesh.shape["tok"]}
    grid = Mesh(mesh.devices.reshape(RING, sizes["blk"] // RING, sizes["tok"] // 2, 2), AXES)
    blk, tok = ("z", "y"), ("x", "core")
    in_specs = (
        P(blk, tok, None),
        P(None, tok),
        P(),
        P(tok, blk),
        P(tok, blk),
        P(None, blk),
        P(blk),
        P(blk, None, None),
        P(blk),
        P(blk, None, None),
        P(blk),
        P(blk),
        P(tok, blk),
        P(),
        P(tok, blk),
        P(tok, blk),
        P(tok, blk),
        P(blk, tok, None),
    )
    out_specs = (
        P(blk, tok, None),
        P(blk, tok, None),
        P(),
        P(tok, blk),
        P(tok, blk),
        P(None, blk),
        P(blk),
        P(blk, None, None),
        P(blk),
        P(blk, None, None),
        P(blk),
        P(blk),
        P(tok, blk),
        P(),
        P(tok, blk),
        P(tok, blk),
        P(tok, blk),
    )
    return jax.shard_map(
        on_device, mesh=grid, in_specs=in_specs, out_specs=out_specs, check_vma=False
    )
```

```python
import enum
import math

import jax
import jax.numpy as jnp
from jax import lax
from jax.experimental import pallas as pl
from jax.experimental.pallas import tpu as pltpu
from jax.sharding import Mesh
from jax.sharding import PartitionSpec as P

EPSILON = 1e-06
MESH = pl.DeviceIdType.MESH
AXES = ("z", "y", "x", "core")
GELU_A = math.sqrt(2.0 / math.pi)
GELU_B = 0.044715
F32 = jnp.float32
BF16 = jnp.bfloat16
RING = 4
CHUNK = 128
STEPS = CHUNK // 8
LEAD = 24


def dot_nn(left, right):
    return lax.dot_general(left, right, (((1,), (0,)), ((), ())), preferred_element_type=F32)


def dot_nt(left, right):
    return lax.dot_general(left, right, (((1,), (1,)), ((), ())), preferred_element_type=F32)


def dot_tn(left, right):
    return lax.dot_general(left, right, (((0,), (0,)), ((), ())), preferred_element_type=F32)


def gelu_parts(v):
    t = jnp.tanh(GELU_A * (v + GELU_B * v * v * v))
    return 0.5 * v * (1.0 + t), t


def gelu_slope(v, t):
    return 0.5 * (1.0 + t) + 0.5 * v * (1.0 - t * t) * (GELU_A * (1.0 + 3.0 * GELU_B * v * v))


def one_minus_exp(v):
    series = 1.0 + v * (1.0 / 9.0)
    for order in (8.0, 7.0, 6.0, 5.0, 4.0, 3.0, 2.0):
        series = 1.0 + v * (1.0 / order) * series
    return jnp.where(v > -0.5, -v * series, 1.0 - jnp.exp(v))


def inverse_rms(values):
    return lax.rsqrt(jnp.mean(values * values, axis=-1, keepdims=True) + EPSILON)


def norm_back(grads, values, scale, gain):
    held = grads * gain
    return scale * held - values * (scale * scale * scale) * jnp.mean(held * values, axis=-1, keepdims=True)


def around(axis, size, step):
    return {axis: lax.rem(lax.axis_index(axis) + (step + size), size)}


def turned(index, step):
    return lax.rem(index + (step + RING), RING)


class Links:
    def __init__(self, send, recv):
        self.send, self.recv, self.used = send, recv, 0

    def start(self, src, dst, axis, step):
        copy = pltpu.make_async_remote_copy(
            src_ref=src,
            dst_ref=dst,
            send_sem=self.send.at[self.used],
            recv_sem=self.recv.at[self.used],
            device_id=around(axis, lax.axis_size(axis), step),
            device_id_type=MESH,
        )
        self.used += 1
        copy.start()
        return copy

    def local(self, src, dst):
        copy = pltpu.make_async_copy(src, dst, self.send.at[self.used])
        self.used += 1
        copy.start()
        return copy


def greet():
    barrier = pltpu.get_barrier_semaphore()
    total = 0
    for axis in AXES:
        size = lax.axis_size(axis)
        for step in range(1, size):
            pl.semaphore_signal(barrier, inc=1, device_id=around(axis, size, step), device_id_type=MESH)
            total += 1
    pl.semaphore_wait(barrier, total)


class Task:
    def __init__(self, stages):
        self.stages = stages

    def step(self):
        next(self.stages, None)

    def finish(self):
        for _ in self.stages:
            pass


def strips(count, body, carry=0, size=16):
    def step(i, carry):
        return body(pl.ds(pl.multiple_of(i * size, size), size), carry)

    return lax.fori_loop(0, count // size, step, carry)


def add_rows(out, terms):
    def body(here, carry):
        total = terms[0][here, :].astype(F32)
        for term in terms[1:]:
            total = total + term[here, :].astype(F32)
        out[here, :] = total.astype(out.dtype)
        return carry

    strips(out.shape[0], body)


def gather_weight(links, own, full):
    z, x, core = lax.axis_index("z"), lax.axis_index("x"), lax.axis_index("core")
    rows = own.shape[0]
    half = rows // 2
    mine = pl.ds(pl.multiple_of((core * 4 + x) * 256, 256), 256)
    ours = pl.ds(pl.multiple_of(core * 1024, 1024), 1024)
    top, low = pl.ds(0, half), pl.ds(half, rows - half)
    here = links.local(own, full.at[z, :, mine])
    first_a = [links.start(own.at[top], full.at[z, top, mine], "x", s) for s in (1, 3, 2)]
    first_b = [links.start(own.at[low], full.at[z, low, mine], "z", s) for s in (1, 3, 2)]
    yield
    mates = []

    def share(block):
        mates.append(links.start(block, block, "core", 1))

    def beside(step):
        return full.at[:, low, pl.ds(pl.multiple_of((core * 4 + turned(x, step)) * 256, 256), 256)]

    here.wait()
    for copy in first_a:
        copy.wait_recv()
    block = full.at[z, top, ours]
    second_a = [links.start(block, block, "z", s) for s in (1, -1)]
    share(block)
    for copy in first_b:
        copy.wait_recv()
    block = beside(0)
    second_b = [links.start(block, block, "x", s) for s in (1, -1)]
    share(block)
    yield
    relays = []
    for way in (0, 1):
        step = 1 - 2 * way
        second_a[way].wait_recv()
        lanes = pl.ds(pl.multiple_of(core * 1024 + way * 512, 512), 512)
        block = full.at[turned(z, -step), top, lanes]
        relays.append(links.start(block, block, "z", step))
        second_b[way].wait_recv()
        lanes = pl.ds(pl.multiple_of((core * 4 + turned(x, -step)) * 256, 256), 256)
        block = full.at[pl.ds(2 * way, 2), low, lanes]
        relays.append(links.start(block, block, "x", step))
    for step in (1, -1):
        share(full.at[turned(z, step), top, ours])
        share(beside(step))
    yield
    for copy in relays:
        copy.wait_recv()
    share(full.at[turned(z, 2), top, ours])
    share(beside(2))
    yield
    for copy in mates:
        copy.wait_recv()
    for copy in first_a + first_b + second_a + second_b + relays + mates:
        copy.wait_send()


def spread_gain(gain, row):
    for p in range(8):
        for part in range(2):
            at = placed(p) // 128 + part
            row[:, p * 256 + part * 128 : p * 256 + part * 128 + 128] = gain[at : at + 1, :]


def placed(p):
    return ((p % 4) * 2 + p // 4) * 256


def exchange(inward):
    row = lax.broadcasted_iota(jnp.int32, (CHUNK, CHUNK), 0)
    col = lax.broadcasted_iota(jnp.int32, (CHUNK, CHUNK), 1)
    if inward:
        hit = col == lax.rem(row, 8) * STEPS + row // 8
    else:
        hit = col == lax.rem(row, STEPS) * 8 + row // STEPS
    return jnp.where(hit, 1.0, 0.0).astype(BF16)


def place_rows(source, target):
    pick = exchange(True)
    for p in range(8):
        target[:, p * 256 : (p + 1) * 256] = dot_nn(pick, source[:, placed(p) : placed(p) + 256]).astype(BF16)


def restore_low(source, target):
    pick = exchange(False)
    for p in range(8):
        held = dot_nn(pick, source[:, p * 256 : (p + 1) * 256].astype(BF16))
        target[:, placed(p) : placed(p) + 256] = held.astype(BF16)


def restore_wide(source, target):
    pick = exchange(False)
    for p in range(8):
        value = source[:, p * 256 : (p + 1) * 256]
        high = value.astype(BF16)
        rest = value - high.astype(F32)
        middle = rest.astype(BF16)
        small = (rest - middle.astype(F32)).astype(BF16)
        moved = dot_nn(pick, high) + dot_nn(pick, middle) + dot_nn(pick, small)
        target[:, 0, placed(p) : placed(p) + 256] = moved


def gather_rows(links, seq):
    y = lax.axis_index("y")

    def half(place, part):
        return seq.at[place, :, pl.ds(part * 1024, 1024)]

    first = [links.start(half(y, way), half(y, way), "y", 1 - 2 * way) for way in (0, 1)]
    other = [links.start(half(y, 1 - way), half(y, 1 - way), "y", 1 - 2 * way) for way in (0, 1)]
    yield
    relays = []
    for way in (0, 1):
        step = 1 - 2 * way
        first[way].wait_recv()
        block = half(turned(y, -step), way)
        relays.append(links.start(block, block, "y", step))
    yield
    for copy in other + relays:
        copy.wait_recv()
    for copy in first + other + relays:
        copy.wait_send()


def scatter_rows(links, produce, part, far, near, out):
    y = lax.axis_index("y")
    across = turned(y, 2)
    lanes = [pl.ds(way * 1024, 1024) for way in (0, 1)]
    produce(across)
    first = [links.start(part.at[across, :, lanes[way]], far.at[way], "y", 1 - 2 * way) for way in (0, 1)]
    yield
    second = []
    for way in (0, 1):
        step = 1 - 2 * way
        produce(turned(y, step))
        free = lanes[1 - way]
        second.append(links.start(part.at[turned(y, step), :, free], near.at[way, :, free], "y", step))
    yield
    produce(y)
    yield
    for way in (0, 1):
        step = 1 - 2 * way
        first[way].wait_recv()
        held = part.at[turned(y, step), :, lanes[way]]
        add_rows(held, [held, far.at[way]])
        second.append(links.start(held, near.at[way, :, lanes[way]], "y", step))
    yield
    for copy in second:
        copy.wait_recv()
    add_rows(out, [part.at[y], near.at[0], near.at[1]])
    for copy in first + second:
        copy.wait_send()


ROW_SCRATCH = [pltpu.VMEM((2, CHUNK, 1024), BF16), pltpu.VMEM((2, CHUNK, 2048), BF16)]


def share_core(links, part, mate, make):
    core = lax.axis_index("core")
    ours = pl.ds(pl.multiple_of(core * 1024, 1024), 1024)
    theirs = pl.ds(pl.multiple_of((1 - core) * 1024, 1024), 1024)
    across = []
    for n in range(RING):
        if make(n):
            yield
        across.append(links.start(part.at[n, :, theirs], mate.at[n], "core", 1))
    yield
    for n in range(RING):
        across[n].wait_recv()
        held = part.at[n, :, ours]
        add_rows(held, [held, mate.at[n]])
    for copy in across:
        copy.wait_send()


def scatter_weight(links, part, make, mate, far_a, near_a, far_b, near_b, light_a, light_b, out):
    yield from share_core(links, part, mate, make)
    base = lax.axis_index("core") * 1024
    yield from scatter_chips(links, part, base, far_a, near_a, far_b, near_b, light_a, light_b, out)


def scatter_chips(links, part, base, far_a, near_a, far_b, near_b, light_a, light_b, out):
    z, x = lax.axis_index("z"), lax.axis_index("x")
    rows = part.shape[1]
    half = rows // 2
    top, low = pl.ds(0, half), pl.ds(half, rows - half)
    ours = pl.ds(pl.multiple_of(base, 1024), 1024)

    def lanes(place):
        return pl.ds(pl.multiple_of(base + place * 256, 256), 256)

    first = []
    for way in (0, 1):
        step = 1 - 2 * way
        half_lanes = pl.ds(pl.multiple_of(base + way * 512, 512), 512)
        first.append(links.start(part.at[turned(z, 2), top, half_lanes], far_a.at[way], "z", step))
        block = part.at[pl.ds(2 * way, 2), low, lanes(turned(x, 2))]
        first.append(links.start(block, far_b.at[way], "x", step))
    yield
    second = []
    for way in (0, 1):
        step = 1 - 2 * way
        first[2 * way].wait_recv()
        half_lanes = pl.ds(pl.multiple_of(base + way * 512, 512), 512)
        held = part.at[turned(z, step), top, half_lanes]
        add_rows(held, [held, far_a.at[way]])
        second.append(links.start(part.at[turned(z, step), top, ours], near_a.at[way], "z", step))
        first[2 * way + 1].wait_recv()
        for i in range(2):
            held = part.at[2 * way + i, low, lanes(turned(x, step))]
            add_rows(held, [held, far_b.at[way, i]])
        second.append(links.start(part.at[:, low, lanes(turned(x, step))], near_b.at[way], "x", step))
    yield
    for way in (0, 1):
        second[2 * way].wait_recv()
    held = part.at[z, top, ours]
    add_rows(held, [held, near_a.at[0], near_a.at[1]])
    third = []
    for i, step in enumerate((1, 3, 2)):
        third.append(links.start(part.at[z, top, lanes(turned(x, step))], light_a.at[i], "x", step))
    for way in (0, 1):
        second[2 * way + 1].wait_recv()
    for block in range(4):
        held = part.at[block, low, lanes(x)]
        add_rows(held, [held, near_b.at[0, block], near_b.at[1, block]])
    for i, step in enumerate((1, 3, 2)):
        third.append(links.start(part.at[turned(z, step), low, lanes(x)], light_b.at[i], "z", step))
    yield
    for copy in third:
        copy.wait_recv()
    add_rows(out.at[top], [part.at[z, top, lanes(x)]] + [light_a.at[i] for i in range(3)])
    add_rows(out.at[low], [part.at[z, low, lanes(x)]] + [light_b.at[i] for i in range(3)])
    for copy in first + second + third:
        copy.wait_send()


def scatter_scratch(rows):
    half = rows // 2
    return [
        pltpu.VMEM((4, rows, 1024), BF16),
        pltpu.VMEM((2, half, 512), BF16),
        pltpu.VMEM((2, half, 1024), BF16),
        pltpu.VMEM((2, 2, half, 256), BF16),
        pltpu.VMEM((2, 4, half, 256), BF16),
        pltpu.VMEM((3, half, 256), BF16),
        pltpu.VMEM((3, half, 256), BF16),
    ]


SCATTER_REFS = 7


def sum_everywhere(links, slots, axis):
    size = lax.axis_size(axis)
    own = slots.at[lax.axis_index(axis)]
    copies = [links.start(own, own, axis, s) for s in range(1, size)]
    yield
    for copy in copies:
        copy.wait_recv()
    for copy in copies:
        copy.wait_send()


def any_space(count):
    return [pl.BlockSpec(memory_space=pl.ANY)] * count


def vmem(count):
    return [pl.BlockSpec(memory_space=pltpu.VMEM)] * count


def shape(dims, dtype):
    return jax.ShapeDtypeStruct(dims, dtype)


def sems(count):
    return [pltpu.SemaphoreType.DMA((count,)), pltpu.SemaphoreType.DMA((count,))]


def options(number, mib=60):
    return pltpu.CompilerParams(
        collective_id=number, has_side_effects=True, vmem_limit_bytes=mib * 2**20
    )


def spots(q, at, size):
    return pl.ds(pl.multiple_of(q * CHUNK + at, 8), size)


def flat2(ref):
    value = ref[...]
    return value.reshape(value.shape[0] * value.shape[1], value.shape[2])


def column(i, j, low, high, shift):
    row = lax.broadcasted_iota(jnp.int32, (i, j), 0)
    col = lax.broadcasted_iota(jnp.int32, (i, j), 1)
    hit = (col == row + shift) & (row >= low) & (row < high)
    return jnp.where(hit, 1.0, 0.0).astype(BF16)


def gather_small(links, vectors, gates, gate_pack, vector_slots, gate_slots, params, gate_a, gate_x):
    z, core = lax.axis_index("z"), lax.axis_index("core")
    width = gate_pack.shape[0]
    gate_pack[...] = jnp.zeros(gate_pack.shape, BF16)
    gate_pack[:, 0:width] = gates[0][0]
    gate_pack[:, 256 : 256 + width] = gates[1][0]
    half = width // 2
    part = pl.ds(pl.multiple_of(core * half, 16), half)
    here = [
        links.local(vectors, vector_slots.at[z]),
        links.local(gate_pack.at[part], gate_slots.at[z, part]),
    ]
    sent = []
    for step in (1, 3, 2):
        sent.append(links.start(vectors, vector_slots.at[z], "z", step))
        sent.append(links.start(gate_pack.at[part], gate_slots.at[z, part], "z", step))
    yield
    for copy in here:
        copy.wait()
    for copy in sent:
        copy.wait_recv()
    block = gate_slots.at[:, part]
    last = links.start(block, block, "core", 1)
    found = vector_slots[0] + vector_slots[1] + vector_slots[2] + vector_slots[3]
    params[8:16, :] = jnp.zeros_like(found)
    params[0:8, :] = found
    minus = -found[7:8, :]
    params[8:9, :] = jnp.maximum(minus, 0.0) + jnp.log1p(jnp.exp(-jnp.abs(minus)))
    params[9:10, :] = jax.nn.sigmoid(minus)
    yield
    last.wait_recv()
    channels = gate_a.shape[1]
    for place in range(RING):
        rows = pl.ds(place * width, width)
        packed = gate_slots[place]
        size = packed.shape[1]
        pick = column(size, channels, 0, width, place * width)
        gate_a[rows, :] = dot_nn(packed, pick).astype(BF16)
        pick = column(size, channels, 256, 256 + width, place * width - 256)
        gate_x[rows, :] = dot_nn(packed, pick).astype(BF16)
    for copy in sent + [last]:
        copy.wait_send()


def fill_lead(buf, halo, tiles):
    count = tiles * 8
    for q in range(RING):
        for i in range(tiles):
            at = buf.shape[1] - count + i * 8
            tile = buf[q, pl.ds(at, 8), :]
            before = halo[i * 8 + 7 : i * 8 + 8, :] if q == 0 else buf[q - 1, pl.ds(at + 7, 1), :]
            buf[q, pl.ds(i * 8, 8), :] = jnp.concatenate([before, tile[:7, :]], axis=0)


def fill_tail(buf, halo, tiles):
    for q in range(RING):
        for i in range(tiles):
            tile = buf[q, pl.ds(i * 8, 8), :]
            after = halo[i * 8 : i * 8 + 1, :] if q == RING - 1 else buf[q + 1, pl.ds(i * 8, 1), :]
            buf[q, pl.ds(CHUNK + i * 8, 8), :] = jnp.concatenate([tile[1:, :], after], axis=0)


def conv_taps(branch, masks, params, conv, low):
    for q in range(RING):

        def taps(here, carry):
            at = here.start
            mask = masks[q, here, :]
            total = params[4:5, :] + params[0:1, :] * branch[q, pl.ds(pl.multiple_of(at + LEAD, 8), 32), :]
            for k in range(1, 4):
                moved = branch[q, pl.ds(pl.multiple_of(at + LEAD - 8 * k, 8), 32), :]
                total = total + params[k : k + 1, :] * (moved * mask[:, k : k + 1])
            conv[spots(q, at, 32), :] = total
            low[spots(q, at, 32), :] = total.astype(BF16)
            return carry

        strips(CHUNK, taps, size=32)


def gate_values(masks, params, conv, rate, admit, decay, scaling, local):
    for q in range(RING):

        def point(here, carry):
            spot = spots(q, here.start, 32)
            restart = masks[q, here, 0:1] > 0.5
            rated = jax.nn.sigmoid(rate[spot, :] + params[5:6, :])
            admitted = jax.nn.sigmoid(admit[spot, :] + params[6:7, :])
            log_decay = -8.0 * rated * params[8:9, :]
            scaled = jnp.where(restart, 1.0, jnp.sqrt(one_minus_exp(2.0 * log_decay)))
            rate[spot, :] = rated
            admit[spot, :] = admitted
            decay[spot, :] = jnp.where(restart, 0.0, jnp.exp(log_decay))
            scaling[spot, :] = scaled
            local[spot, :] = scaled * admitted * conv[spot, :]
            return carry

        strips(CHUNK, point, size=32)


def scan_start(channels):
    return (jnp.zeros((8, channels), F32), jnp.ones((8, channels), F32)) * RING


def scan_forward(decay, local, product):
    def step(j, carry):
        kept = []
        for q in range(RING):
            here = spots(q, j * 8, 8)
            rated = decay[here, :]
            state = rated * carry[2 * q] + local[here, :]
            prod = rated * carry[2 * q + 1]
            local[here, :] = state
            product[here, :] = prod
            kept += [state, prod]
        return tuple(kept)

    return lax.fori_loop(0, STEPS, step, scan_start(local.shape[1]))


def scan_backward(decay, local, product):
    def step(i, carry):
        kept = []
        for q in range(RING):
            here = spots(q, (STEPS - 1 - i) * 8, 8)
            rated = decay[here, :]
            total = local[here, :] + carry[2 * q]
            local[here, :] = total
            product[here, :] = carry[2 * q + 1]
            kept += [rated * total, rated * carry[2 * q + 1]]
        return tuple(kept)

    return lax.fori_loop(0, STEPS, step, scan_start(local.shape[1]))


def join_segments(ends, heads, totals, order):
    channels = totals.shape[2]
    prod, state = jnp.ones((1, channels), F32), jnp.zeros((1, channels), F32)
    for q in order(RING):
        for s in order(8):
            heads[0, q, s : s + 1, :] = prod
            heads[1, q, s : s + 1, :] = state
            rated = ends[2 * q + 1][s : s + 1, :]
            state = rated * state + ends[2 * q][s : s + 1, :]
            prod = rated * prod
    totals[0, 0:1, :] = prod
    totals[0, 1:2, :] = state


def share_totals(links, totals, way):
    return [links.start(totals.at[0], totals.at[step], "z", way * step) for step in range(1, RING)]


def entering_state(copies, totals, way):
    z = lax.axis_index("z")
    for copy in copies:
        copy.wait()
    entering = jnp.zeros((1, totals.shape[2]), F32)
    for step in range(RING - 1, 0, -1):
        later = totals[step, 0:1, :] * entering + totals[step, 1:2, :]
        valid = z - step >= 0 if way > 0 else z + step < RING
        entering = jnp.where(valid, later, entering)
    return entering


def spread_head(heads, q, entering):
    tile = heads[0, q] * entering + heads[1, q]
    return jnp.concatenate([tile] * 4, axis=0)


def follow(plan, actions):
    for name in plan:
        actions[name]()


class A(enum.IntEnum):
    SMALL, WB, WG, WO, W1, W2, W3, NORM, ROWS, COTS, BRANCH, GELU, EDGE, CONV, GATES, POINT, SCAN, FIX, SUMS, RENORM, MLP, TURN = range(22)


def kernel_a(
    x_raw, cot_raw, gain_rec_in, gain_mlp_in, vectors, gate_a_in, gate_x_in, masks, *more,
):
    weights, more = more[:6], more[6:]
    kernel_a_body(
        x_raw, cot_raw, gain_rec_in, gain_mlp_in, weights, vectors, (gate_a_in, gate_x_in), masks, *more
    )


def kernel_a_body(
    x_raw, cot_raw, gain_rec_in, gain_mlp_in, weights, vectors, gates_in, masks,
    mixed_out, x_out, seq_normed, seq_mlp, seq_grad, wb_out, wg_out, out_out, gate_out, up_out, down_out,
    branch_out, conv_out, rate_out, admit_out, decay_out, scaling_out, states_out, gelu_out, gated_out,
    params_out, gate_a_out, gate_x_out,
    mixed, x_in, cot, cot_held, gain_rec, gain_mlp, gate_pack, wide, turned_wide,
    seq, w_branch, w_gelu, w_out, branch, gelu_pre, conv, low, rate, admit, decay, scaling, local, product,
    states, gated, params, gate_a, gate_x, vector_slots, gate_slots, halo, totals, heads, part, far, near, normed,
    send, recv,
):
    links = Links(send, recv)
    y = lax.axis_index("y")
    count = x_in.shape[0]
    width = vectors.shape[1] // RING
    load_wide = [links.local(weights[3 + i], wide.at[i]) for i in range(3)]
    load_cot = links.local(cot_raw, cot_held)
    place_rows(x_raw, x_in)
    spread_gain(gain_rec_in, gain_rec)
    spread_gain(gain_mlp_in, gain_mlp)
    greet()
    saves, kept = [], {}

    def save(*pairs):
        for source, target in pairs:
            saves.append(links.local(source, target))

    def norm():
        def body(here, carry):
            values = x_in[here, :].astype(F32)
            seq[y, here, :] = (values * inverse_rms(values) * gain_rec[...]).astype(BF16)
            return carry

        strips(count, body)

    def turn():
        same = column(256, 256, 0, 256, 0)
        for i in range(3):
            load_wide[i].wait()
            turned_wide[i] = dot_tn(wide[i], same).astype(BF16)

    def cots():
        load_cot.wait()
        place_rows(cot_held, cot)
        own_cot = links.local(cot, seq_grad.at[y])
        save((x_in, x_out))
        yield
        own_cot.wait()
        yield from gather_rows(links, seq_grad)

    def to_branch():
        result = dot_nt(flat2(seq), flat2(w_branch))
        for q in range(RING):
            branch[q, LEAD:, :] = result[q * CHUNK : (q + 1) * CHUNK, :]
        kept["edge"] = links.start(branch.at[RING - 1, pl.ds(CHUNK, LEAD)], halo, "z", 1)

    def to_gelu():
        gelu_pre[...] = dot_nt(flat2(seq), flat2(w_gelu))

    def edge():
        kept["edge"].wait()
        fill_lead(branch, halo, 3)

    def conv_all():
        conv_taps(branch, masks, params, conv, low)

    def gates():
        rate[...] = dot_nn(low[...], gate_a[...])
        admit[...] = dot_nn(low[...], gate_x[...])

    def point_all():
        gate_values(masks, params, conv, rate, admit, decay, scaling, local)

    def scan():
        ends = scan_forward(decay, local, product)
        join_segments(ends, heads, totals, range)
        kept["totals"] = share_totals(links, totals, 1)

    def fix_all():
        entering = entering_state(kept["totals"], totals, 1)
        for q in range(RING):
            head = spread_head(heads, q, entering)

            def fix(here, carry):
                spot = spots(q, here.start, 32)
                state = local[spot, :] + product[spot, :] * head
                states[q, pl.ds(pl.multiple_of(here.start + 8, 8), 32), :] = state
                gated[spot, :] = (state * gelu_parts(gelu_pre[spot, :])[0]).astype(BF16)
                return carry

            strips(CHUNK, fix, size=32)
        halo[0:8, :] = jnp.broadcast_to(entering, (8, entering.shape[1]))
        fill_lead(states, halo, 1)
        save(
            (seq, seq_normed), (w_branch, wb_out), (w_gelu, wg_out), (params, params_out),
            (gate_a, gate_a_out), (gate_x, gate_x_out), (branch, branch_out), (gelu_pre, gelu_out),
            (conv, conv_out), (rate, rate_out), (admit, admit_out), (decay, decay_out), (scaling, scaling_out),
            (states, states_out), (gated, gated_out),
        )

    def produce(q):
        spot = pl.ds(pl.multiple_of(q * CHUNK, CHUNK), CHUNK)
        part[q] = dot_nn(gated[spot, :], flat2(w_out)).astype(BF16)

    def renorm_all():
        def renorm(here, carry):
            values = x_in[here, :].astype(F32) + mixed[here, :]
            mixed[here, :] = values
            normed[here, :] = (values * inverse_rms(values) * gain_mlp[...]).astype(BF16)
            return carry

        strips(count, renorm)
        links.local(normed, seq_mlp.at[y]).wait()
        save((w_out, out_out), (mixed, mixed_out))

    tasks = {
        A.SMALL: gather_small(links, vectors, gates_in, gate_pack, vector_slots, gate_slots, params, gate_a, gate_x),
        A.ROWS: gather_rows(links, seq),
        A.COTS: cots(),
        A.SUMS: scatter_rows(links, produce, part, far, near, mixed),
        A.MLP: gather_rows(links, seq_mlp),
    }
    fulls = (w_branch, w_gelu, w_out, gate_out, up_out, down_out)
    for i, name in enumerate((A.WB, A.WG, A.WO, A.W1, A.W2, A.W3)):
        own = weights[i] if i < 3 else turned_wide.at[i - 3]
        tasks[name] = gather_weight(links, own, fulls[i])
    tasks = {name: Task(stages) for name, stages in tasks.items()}
    actions = {
        A.NORM: norm, A.BRANCH: to_branch, A.GELU: to_gelu, A.EDGE: edge, A.CONV: conv_all, A.GATES: gates,
        A.POINT: point_all, A.SCAN: scan, A.FIX: fix_all, A.RENORM: renorm_all, A.TURN: turn,
    }
    actions.update({name: task.step for name, task in tasks.items()})
    follow(PLAN_A, actions)
    for task in tasks.values():
        task.finish()
    for copy in saves:
        copy.wait()


class B(enum.IntEnum):
    TILE, SUMS, OUTS, DOWNS, GATES, UPS, BACK, MIXED, OUTSUM = range(9)


def kernel_b(
    seq_mlp, seq_grad, w_gate, w_up, w_down, mixed_in, gain_in,
    g_mixed_out, seq_mixed, output, up_part, gate_grad, down_grad, gain_out,
    mixed, gain, g_mixed, mlp, grads, gate, up, down, pre_gate, pre_up, pre_hidden, hidden, g_gate, g_up,
    part, outs, total, low, far, near, far_out, near_out, *rest,
):
    send, recv = rest[-2:]
    links = Links(send, recv)
    y = lax.axis_index("y")
    count, model = mixed.shape
    width = gate.shape[1]
    pairs = ((w_gate, gate), (w_up, up), (w_down, down))
    loads = [[None] * 3 for _ in range(RING)]

    def load(n, *which):
        for i in which:
            loads[n][i] = links.local(pairs[i][0].at[n], pairs[i][1].at[n])

    load_mlp = links.local(seq_mlp, mlp)
    load(0, 0, 1)
    spread_gain(gain_in, gain)
    greet()
    load_grads = links.local(seq_grad, grads)
    load(0, 2)
    kept = {}
    ours = pl.ds(pl.multiple_of(lax.axis_index("core") * 1024, 1024), 1024)

    size = pre_gate.shape[2]
    count_tiles = RING * width // size

    def wait_for(t, which):
        for n in range(t * size // width, ((t + 1) * size - 1) // width + 1):
            if loads[n][which] is not None:
                loads[n][which].wait()
                loads[n][which] = None

    def tile_rows(ref, t):
        pieces, at = [], t * size
        while at < (t + 1) * size:
            n, row = at // width, at % width
            take = min(width - row, (t + 1) * size - at)
            pieces.append(ref[n, row : row + take, :])
            at += take
        return pieces[0] if len(pieces) == 1 else jnp.concatenate(pieces, axis=0)

    def point(t, first, last):
        lanes, slot = pl.ds(t * size, size), t % 2
        for i in range(first, last):
            here = pl.ds(i * 32, 32)
            gates, ups, backs = pre_gate[slot, here, :], pre_up[slot, here, :], pre_hidden[slot, here, :]
            value, tang = gelu_parts(gates)
            hidden[here, lanes] = (value * ups).astype(BF16)
            g_gate[here, lanes] = (backs * ups * gelu_slope(gates, tang)).astype(BF16)
            g_up[here, lanes] = (backs * value).astype(BF16)

    def tiles():
        load_mlp.wait()
        for t in range(count_tiles + 1):
            steps = ((pre_gate, mlp, gate), (pre_up, mlp, up), (pre_hidden, grads, down))
            for which, (pre, left, right) in enumerate(steps):
                if t < count_tiles:
                    wait_for(t, which)
                    if t == 0 and which == 0:
                        load(1, 0, 1, 2)
                    if t == 0 and which == 2:
                        load_grads.wait()
                        kept["mixed"] = links.local(mixed_in, mixed)
                    if which == 2 and t in (0, 1):
                        load(t + 2, 0, 1, 2)
                    pre[t % 2] = dot_nt(flat2(left), tile_rows(right, t))
                if t > 0:
                    point(t - 1, (0, 5, 10)[which], (5, 10, 16)[which])
            yield

    def produce(q):
        spot = pl.ds(pl.multiple_of(q * CHUNK, CHUNK), CHUNK)
        result = dot_nn(g_gate[spot, :], flat2(gate)) + dot_nn(g_up[spot, :], flat2(up))
        part[q] = result.astype(BF16)

    def weight_grad(left, right, out):
        def make(n):
            out[n] = dot_tn(left[:, n * width : (n + 1) * width], flat2(right)).astype(BF16)
            return n < RING - 1

        return make

    def out_parts():
        for q in range(RING):
            outs[q] = dot_nn(hidden[q * CHUNK : (q + 1) * CHUNK, :], flat2(down)).astype(BF16)

    def back_all():
        kept["mixed"].wait()

        def back(here, carry):
            values = mixed[here, :]
            backs = total[here, :]
            scale = inverse_rms(values)
            held = grads[y, here, :].astype(F32) + norm_back(backs, values, scale, gain[...])
            g_mixed[here, :] = held
            low[here, :] = held.astype(BF16)
            new = backs * values * scale
            return carry + new[:8, :] + new[8:, :]

        acc = strips(count, back, jnp.zeros((8, model), F32))
        gain_out[...] = jnp.broadcast_to(jnp.sum(acc, axis=0, keepdims=True), (8, model))
        kept["save"] = links.local(g_mixed, g_mixed_out)
        links.local(low, seq_mixed.at[y]).wait()

    def out_sums():
        yield from scatter_rows(links, lambda q: None, outs, far_out, near_out, total)

        def last(here, carry):
            total[here, :] = mixed[here, :] + total[here, :]
            return carry

        strips(count, last)
        restore_low(total, output)

    def ups():
        yield from share_core(links, up, rest[2 * SCATTER_REFS], weight_grad(g_up, mlp, up))
        copy = links.local(up.at[:, :, ours], up_part)
        yield
        copy.wait()

    tasks = {
        B.TILE: tiles(),
        B.SUMS: scatter_rows(links, produce, part, far, near, total),
        B.DOWNS: scatter_weight(
            links, down, weight_grad(hidden, grads, down), *rest[:SCATTER_REFS], down_grad
        ),
        B.GATES: scatter_weight(
            links, gate, weight_grad(g_gate, mlp, gate), *rest[SCATTER_REFS : 2 * SCATTER_REFS], gate_grad
        ),
        B.UPS: ups(),
        B.MIXED: gather_rows(links, seq_mixed),
        B.OUTSUM: out_sums(),
    }
    tasks = {name: Task(stages) for name, stages in tasks.items()}
    actions = {
        B.OUTS: out_parts, B.BACK: back_all,
    }
    actions.update({name: task.step for name, task in tasks.items()})
    follow(PLAN_B, actions)
    for task in tasks.values():
        task.finish()
    kept["save"].wait()


class C(enum.IntEnum):
    UPS, GATED, POINT, SCAN, OUTW, GELUW, FIX, GATES, SQUARES, CONV, SUMS, BRANCHW, PACK, SMALLS, GAINS, FINISH = range(16)


def kernel_c(
    seq_mixed, seq_normed, wb_in, wg_in, w_out, branch_in, conv_in, rate_in, admit_in, decay_in, scaling_in,
    states_in, gelu_in, gated_in, up_part, params_in, gate_a_in, gate_x_in, masks_in, g_mixed_in, x_saved,
    gain_in, gain_part,
    g_inputs, branch_grad, gelu_grad, out_grad, up_grad, small_out, gain_out,
    params, gate_a, gate_x, masks, g_mixed, x_in, gain,
    seq, normed, w_branch, w_gelu, w_o, branch, conv, rate, admit, decay, scaling, states, gelu_pre, gated,
    local, product, g_gelu, rate_low, admit_low, low, g_conv, halo, totals, heads,
    squares, pack, pack_mate, pack_z, pack_x, small_rows, gain_slots, gain_acc, gain_sum,
    up, branch_part, gelu_part, total, far, near, *rest,
):
    send, recv = rest[-2:]
    links = Links(send, recv)
    count, model = g_mixed.shape
    width = out_grad.shape[0]
    channels = RING * width
    z, x, core = lax.axis_index("z"), lax.axis_index("x"), lax.axis_index("core")
    part, g_branch = seq, low
    loads, kept = {}, {}
    batches = [
        ((seq_mixed, seq), (w_out, w_o), (up_part, up)),
        ((gelu_in, gelu_pre), (states_in, states), (decay_in, decay)),
        (
            (masks_in, masks), (params_in, params), (conv_in, conv), (rate_in, rate), (admit_in, admit),
            (scaling_in, scaling), (gated_in, gated), (seq_normed, normed), (gate_a_in, gate_a), (gate_x_in, gate_x),
        ),
        (
            (branch_in, branch), (wb_in, w_branch), (wg_in, w_gelu), (x_saved, x_in), (g_mixed_in, g_mixed),
        ),
    ]

    def load_next():
        for source, target in batches.pop(0):
            loads[id(target)] = links.local(source, target)

    load_next()
    spread_gain(gain_in, gain)
    greet()
    load_next()

    def need(*targets):
        for target in targets:
            copy = loads.pop(id(target), None)
            if copy is not None:
                copy.wait()

    def ups():
        need(up)
        yield from scatter_chips(links, up, 0, *rest[3 * SCATTER_REFS : 4 * SCATTER_REFS - 1], up_grad)

    def to_gated():
        need(seq, w_o)
        load_next()
        product[...] = dot_nt(flat2(seq), flat2(w_o))

    def point_all():
        need(gelu_pre, states)
        for q in range(RING):

            def point(here, carry):
                spot = spots(q, here.start, 32)
                held = product[spot, :]
                pre = gelu_pre[spot, :]
                value, tang = gelu_parts(pre)
                state = states[q, pl.ds(pl.multiple_of(here.start + 8, 8), 32), :]
                g_gelu[spot, :] = (held * state * gelu_slope(pre, tang)).astype(BF16)
                local[spot, :] = held * value
                return carry

            strips(CHUNK, point, size=32)

    def scan():
        need(decay)
        load_next()
        ends = scan_backward(decay, local, product)
        join_segments(ends, heads, totals, lambda n: range(n - 1, -1, -1))
        kept["totals"] = share_totals(links, totals, -1)

    def weight_grad(left, right, out):
        def make(n):
            if n > 0:
                return False
            need(left, right)
            for first, size in ((0, 256), (256, 256), (512, 128)):
                result = dot_tn(left[:, first : first + size], flat2(right)).astype(BF16)
                at = first
                while at < first + size:
                    place, row = at // width, at % width
                    take = min(width - row, first + size - at)
                    out[place, row : row + take, :] = result[at - first : at - first + take, :]
                    at += take
            return False

        return make

    zero = jnp.zeros((8, channels), F32)

    def eights(value):
        return value[0:8, :] + value[8:16, :] + value[16:24, :] + value[24:32, :]

    def fix_all():
        need(conv, rate, admit, scaling, masks, params)
        entering = entering_state(kept["totals"], totals, -1)
        sums = (zero, zero, zero)
        for q in range(RING):
            head = spread_head(heads, q, entering)

            def fix(here, carry):
                spot = spots(q, here.start, 32)
                running = masks[q, here, 0:1] < 0.5
                before = states[q, here, :]
                carried = local[spot, :] + product[spot, :] * head
                rated, admitted, held = rate[spot, :], admit[spot, :], conv[spot, :]
                spread, scaled = decay[spot, :], scaling[spot, :]
                g_log = jnp.where(
                    running, carried * spread * (before - admitted * held * spread / scaled), 0.0
                )
                g_rate = g_log * (-8.0 * params[8:9, :]) * rated * (1.0 - rated)
                driven = carried * scaled * admitted
                g_admit = driven * held * (1.0 - admitted)
                rate_low[spot, :] = g_rate.astype(BF16)
                admit_low[spot, :] = g_admit.astype(BF16)
                low[spot, :] = held.astype(BF16)
                g_conv[q, here, :] = driven
                return carry[0] + eights(g_rate), carry[1] + eights(g_admit), carry[2] + eights(g_log * rated)

            sums = strips(CHUNK, fix, sums, size=32)
        kept["sums"] = sums

    def gates():
        need(gate_a, gate_x)
        back = dot_nt(rate_low[...], gate_a[...]) + dot_nt(admit_low[...], gate_x[...])
        for q in range(RING):
            g_conv[q, 0:CHUNK, :] = g_conv[q, 0:CHUNK, :] + back[q * CHUNK : (q + 1) * CHUNK, :]
        kept["edge"] = links.start(g_conv.at[0, pl.ds(0, LEAD)], halo, "z", -1)

    def gate_squares():
        squares[0] = dot_tn(low[...], rate_low[...]).astype(BF16)
        squares[1] = dot_tn(low[...], admit_low[...]).astype(BF16)

    def conv_all():
        need(branch)
        kept["edge"].wait()
        fill_tail(g_conv, halo, 3)
        taps = (zero,) * 5
        for q in range(RING):

            def conv_back(here, carry):
                at = here.start
                own = g_conv[q, here, :]
                total_here = params[0:1, :] * own
                new = [carry[0] + eights(own * branch[q, pl.ds(pl.multiple_of(at + LEAD, 8), 32), :])]
                for k in range(1, 4):
                    later = pl.ds(pl.multiple_of(at + 8 * k, 8), 32)
                    total_here = total_here + params[k : k + 1, :] * (
                        g_conv[q, later, :] * masks[q, later, k : k + 1]
                    )
                    moved = branch[q, pl.ds(pl.multiple_of(at + LEAD - 8 * k, 8), 32), :]
                    new.append(carry[k] + eights(own * masks[q, here, k : k + 1] * moved))
                new.append(carry[4] + eights(own))
                g_branch[spots(q, at, 32), :] = total_here.astype(BF16)
                return tuple(new)

            taps = strips(CHUNK, conv_back, taps, size=32)
        kept["taps"] = taps
        gain_acc[...] = jnp.zeros((8, model), F32)

    def produce(q):
        need(w_branch, w_gelu, normed)
        spot = pl.ds(pl.multiple_of(q * CHUNK, CHUNK), CHUNK)
        result = dot_nn(g_branch[spot, :], flat2(w_branch)) + dot_nn(g_gelu[spot, :], flat2(w_gelu))
        part[q] = result.astype(BF16)

        def gather_gain(here, carry):
            new = part[q, here, :].astype(F32) * normed[q, here, :].astype(F32)
            gain_acc[...] = gain_acc[...] + new[:8, :] + new[8:, :]
            return carry

        strips(CHUNK, gather_gain)

    def pack_all():
        for i, value in enumerate(kept["taps"] + kept["sums"]):
            row = jnp.sum(value, axis=0, keepdims=True)
            small_rows[i : i + 1, :] = row * 8.0 * params[9:10, :] if i == 7 else row
        small_rows[8:16, :] = jnp.zeros((8, channels), F32)
        size = pack.shape[2]
        for place in range(RING):
            pick = column(channels, size, place * width, (place + 1) * width, -place * width)
            rows_here = pl.ds(place * width, width)
            pack[place, 0:width, :] = dot_nn(squares[0, rows_here, :], pick).astype(BF16)
            pack[place, width : 2 * width, :] = dot_nn(squares[1, rows_here, :], pick).astype(BF16)
            pack[place, 2 * width : 2 * width + 16, :] = dot_nn(small_rows[...].astype(BF16), pick).astype(BF16)
            pack[place, 2 * width + 16 :, :] = jnp.zeros((pack.shape[1] - 2 * width - 16, size), BF16)

    def smalls():
        half = pack.shape[1] // 2
        ours = pl.ds(pl.multiple_of(core * half, 16), half)
        theirs = pl.ds(pl.multiple_of((1 - core) * half, 16), half)
        across = links.start(pack.at[:, theirs], pack_mate, "core", 1)
        yield
        across.wait_recv()
        for place in range(RING):
            held = pack.at[place, ours]
            add_rows(held, [held, pack_mate.at[place]])
        sent = [
            links.start(pack.at[turned(z, step), ours], pack_z.at[i], "z", step)
            for i, step in enumerate((1, 3, 2))
        ]
        yield
        for copy in sent:
            copy.wait_recv()
        add_rows(pack_x.at[x], [pack.at[z, ours]] + [pack_z.at[i] for i in range(3)])
        yield from sum_everywhere(links, pack_x, "x")
        add_rows(small_out.at[ours], [pack_x.at[i] for i in range(RING)])
        held = small_out.at[ours]
        final = links.start(held, held, "core", 1)
        yield
        final.wait()
        for copy in [across] + sent:
            copy.wait_send()

    def gains():
        rec = jnp.sum(gain_acc[...], axis=0, keepdims=True) / gain[...]
        other = gain_part[0:1, :]
        for i in range(4):
            for part in range(2):
                block = 2 * i + part
                at = ((block % 2) * 4 + block // 2) * 256
                lanes = pl.ds(part * 256, 256)
                gain_sum[i : i + 1, lanes] = rec[:, at : at + 256]
                gain_sum[4 + i : 5 + i, lanes] = other[:, at : at + 256]
        for n, axis in enumerate(("y", "z", "x", "core")):
            slots = gain_slots.at[n, pl.ds(0, lax.axis_size(axis))]
            slots[lax.axis_index(axis)] = gain_sum[...]
            yield from sum_everywhere(links, slots, axis)
            found = slots[0]
            for i in range(1, lax.axis_size(axis)):
                found = found + slots[i]
            gain_sum[...] = found
        for i in range(8):
            for part in range(4):
                at = i * 4 + part
                gain_out[at : at + 1, :] = gain_sum[i : i + 1, part * 128 : (part + 1) * 128]

    def finish_all():
        need(x_in, g_mixed)

        def finish(here, carry):
            values = x_in[here, :].astype(F32)
            total[here, :] = g_mixed[here, :] + norm_back(
                total[here, :], values, inverse_rms(values), gain[...]
            )
            return carry

        strips(count, finish)
        restore_wide(total, g_inputs)

    first, second, third = (rest[i * SCATTER_REFS : (i + 1) * SCATTER_REFS] for i in range(3))
    tasks = {
        C.UPS: ups(),
        C.OUTW: scatter_weight(links, w_o, weight_grad(gated, seq, w_o), *first, out_grad),
        C.GELUW: scatter_weight(links, gelu_part, weight_grad(g_gelu, normed, gelu_part), *second, gelu_grad),
        C.BRANCHW: scatter_weight(links, branch_part, weight_grad(g_branch, normed, branch_part), *third, branch_grad),
        C.SUMS: scatter_rows(links, produce, part, far, near, total),
        C.SMALLS: smalls(),
        C.GAINS: gains(),
    }
    tasks = {name: Task(stages) for name, stages in tasks.items()}
    actions = {
        C.GATED: to_gated, C.POINT: point_all, C.SCAN: scan, C.FIX: fix_all, C.GATES: gates,
        C.SQUARES: gate_squares, C.CONV: conv_all, C.PACK: pack_all, C.FINISH: finish_all,
    }
    actions.update({name: task.step for name, task in tasks.items()})
    follow(PLAN_C, actions)
    for task in tasks.values():
        task.finish()


def kernel_d(
    output_in, inputs_in, branch_in, gelu_in, out_in, packed, gains, gate_in, up_in, down_in,
    output, g_inputs, branch, gelu, out, gain_rec, gain_mlp, gate, up, down,
    gate_a, gate_x, taps, conv_bias, bias_a, bias_x, decay, sems,
):
    copies = []
    pairs = ((inputs_in, g_inputs), (output_in, output), (branch_in, branch), (gelu_in, gelu), (out_in, out))
    for i, (source, target) in enumerate(pairs):
        copies.append(pltpu.make_async_copy(source, target, sems.at[i]))
        copies[-1].start()
    for source, target in ((gate_in, gate), (up_in, up), (down_in, down)):
        target[...] = source[...].T
    gain_rec[...] = gains[0:16, :]
    gain_mlp[...] = gains[16:32, :]
    width = gate_a.shape[1]
    gate_a[0] = packed[0:width, 0:width].astype(F32)
    gate_x[0] = packed[width : 2 * width, 0:width].astype(F32)
    vectors = packed[2 * width : 2 * width + 16, 0:width].astype(F32)
    taps[...] = vectors[0:4, :]
    for i, target in enumerate((conv_bias, bias_a, bias_x, decay)):
        target[...] = vectors[4 + i : 5 + i, :]
    for copy in copies:
        copy.wait()


PLAN_A = (
    A.WB, A.NORM, A.WO, A.WG, A.ROWS, A.TURN, A.WB, A.SMALL, A.ROWS, A.COTS, A.COTS, A.WB, A.WG, A.WB, A.WO, A.ROWS, A.SMALL, A.WB, A.BRANCH, A.WG, A.W1, A.EDGE, A.SMALL, A.WO, A.W3, A.CONV, A.GATES, A.POINT, A.WG, A.SCAN, A.COTS, A.W2, A.WO, A.WG, A.WO, A.W3, A.GELU, A.FIX, A.W2, A.SUMS, A.SUMS, A.W1, A.SUMS, A.SUMS, A.SUMS, A.W2, A.COTS, A.RENORM, A.W3, A.MLP, A.MLP, A.W1, A.W3, A.W2, A.W1, A.W1, A.W2, A.MLP, A.W3,
)
PLAN_B = (
    B.TILE, B.TILE, B.TILE, B.TILE, B.TILE, B.TILE, B.TILE, B.SUMS, B.OUTS, B.OUTSUM, B.OUTSUM, B.DOWNS, B.OUTSUM, B.DOWNS, B.DOWNS, B.DOWNS, B.DOWNS, B.SUMS, B.SUMS, B.DOWNS, B.GATES, B.GATES, B.SUMS, B.GATES, B.GATES, B.GATES, B.OUTSUM, B.UPS, B.SUMS, B.BACK, B.GATES, B.MIXED, B.UPS, B.OUTSUM, B.UPS, B.UPS, B.MIXED, B.DOWNS, B.GATES, B.DOWNS, B.UPS, B.MIXED, B.GATES, B.UPS,
)
PLAN_C = (
    C.UPS, C.GATED, C.POINT, C.SCAN, C.UPS, C.GELUW, C.OUTW, C.FIX, C.GATES, C.SQUARES, C.OUTW, C.GELUW, C.UPS, C.CONV, C.BRANCHW, C.OUTW, C.PACK, C.SMALLS, C.SUMS, C.BRANCHW, C.SMALLS, C.GELUW, C.SUMS, C.BRANCHW, C.SUMS, C.GAINS, C.SUMS, C.SMALLS, C.GAINS, C.GELUW, C.OUTW, C.SMALLS, C.UPS, C.GAINS, C.BRANCHW, C.SUMS, C.GELUW, C.OUTW, C.GAINS, C.FINISH, C.GAINS, C.SMALLS, C.BRANCHW,
)


def call_a(x_in, cot, gain_rec, gain_mlp, vectors, gate_a, gate_x, masks, *weights):
    count, model = x_in.shape
    width, hidden = weights[0].shape[0], weights[3].shape[1]
    channels = RING * width
    rows = RING * CHUNK
    wide = shape((rows, channels), F32)
    seq = shape((RING, count, model), BF16)
    square = shape((channels, channels), BF16)
    big = shape((RING, hidden, model), BF16)
    lead = (RING, CHUNK + LEAD, channels)
    held = (RING, CHUNK + 8, channels)
    flat = pltpu.VMEM((rows, channels), F32)
    weight = shape((RING, width, model), BF16)
    return pl.pallas_call(
        kernel_a,
        out_shape=[
            shape((count, model), F32), shape((count, model), BF16), seq, seq, seq,
            weight, weight, weight, big, big, big,
            shape(lead, F32), wide, wide, wide, wide, wide, shape(held, F32), wide,
            shape((rows, channels), BF16), shape((16, channels), F32), square, square,
        ],
        in_specs=vmem(1) + any_space(1) + vmem(2) + vmem(4) + any_space(6),
        out_specs=any_space(23),
        scratch_shapes=[
            pltpu.VMEM((count, model), F32),
            pltpu.VMEM((count, model), BF16),
            pltpu.VMEM((count, model), BF16),
            pltpu.VMEM((count, model), BF16),
            pltpu.VMEM((1, model), F32),
            pltpu.VMEM((1, model), F32),
            pltpu.VMEM((width, 512), BF16),
            pltpu.VMEM((3, 256, hidden), BF16),
            pltpu.VMEM((3, hidden, 256), BF16),
            pltpu.VMEM((RING, count, model), BF16),
            pltpu.VMEM((RING, width, model), BF16),
            pltpu.VMEM((RING, width, model), BF16),
            pltpu.VMEM((RING, width, model), BF16),
            pltpu.VMEM(lead, F32),
            flat, flat,
            pltpu.VMEM((rows, channels), BF16),
            flat, flat, flat, flat, flat, flat,
            pltpu.VMEM(held, F32),
            pltpu.VMEM((rows, channels), BF16),
            pltpu.VMEM((16, channels), F32),
            pltpu.VMEM((channels, channels), BF16),
            pltpu.VMEM((channels, channels), BF16),
            pltpu.VMEM((RING, 8, channels), F32),
            pltpu.VMEM((RING, width, 512), BF16),
            pltpu.VMEM((LEAD, channels), F32),
            pltpu.VMEM((RING, 8, channels), F32),
            pltpu.VMEM((2, RING, 8, channels), F32),
            pltpu.VMEM((RING, count, model), BF16),
        ]
        + ROW_SCRATCH
        + [pltpu.VMEM((count, model), BF16)]
        + sems(200),
        compiler_params=options(1),
    )(x_in, cot, gain_rec, gain_mlp, vectors, gate_a, gate_x, masks, *weights)


def call_b(seq_mlp, seq_grad, w_gate, w_up, w_down, mixed, gain):
    count, model = mixed.shape
    hidden = w_gate.shape[1]
    rows = RING * CHUNK
    seq = shape((RING, count, model), BF16)
    big = pltpu.VMEM((RING, hidden, model), BF16)
    final = shape((hidden, 256), F32)
    wide = pltpu.VMEM((rows, RING * hidden), BF16)
    pre = pltpu.VMEM((2, rows, 256), F32)
    rows_held = pltpu.VMEM((RING, count, model), BF16)
    return pl.pallas_call(
        kernel_b,
        out_shape=[
            shape((count, model), F32),
            seq,
            shape((count, model), BF16),
            shape((RING, hidden, 1024), BF16),
            final,
            final,
            shape((8, model), F32),
        ],
        in_specs=any_space(6) + vmem(1),
        out_specs=any_space(2) + vmem(1) + any_space(1) + vmem(3),
        scratch_shapes=[
            pltpu.VMEM((count, model), F32),
            pltpu.VMEM((1, model), F32),
            pltpu.VMEM((count, model), F32),
            rows_held, rows_held, big, big, big, pre, pre, pre, wide, wide, wide, rows_held, rows_held,
            pltpu.VMEM((count, model), F32),
            pltpu.VMEM((count, model), BF16),
        ]
        + ROW_SCRATCH * 2
        + scatter_scratch(hidden) * 2
        + scatter_scratch(hidden)[:1]
        + sems(128),
        compiler_params=options(2, 63),
    )(seq_mlp, seq_grad, w_gate, w_up, w_down, mixed, gain)


def call_c(*args):
    w_branch, up_part, g_mixed = args[2], args[14], args[19]
    count, model = g_mixed.shape
    width, hidden = w_branch.shape[1], up_part.shape[1]
    channels = RING * width
    rows = RING * CHUNK
    pack = (RING, 2 * width + 32, 256)
    flat = pltpu.VMEM((rows, channels), F32)
    thin = pltpu.VMEM((rows, channels), BF16)
    rows_held = pltpu.VMEM((RING, count, model), BF16)
    lead = pltpu.VMEM((RING, CHUNK + LEAD, channels), F32)
    weight = pltpu.VMEM((RING, width, model), BF16)
    half = pack[1] // 2
    grad = shape((width, 256), F32)
    return pl.pallas_call(
        kernel_c,
        out_shape=[
            shape((count, 1, model), F32),
            grad,
            grad,
            grad,
            shape((hidden, 256), F32),
            shape(pack[1:], BF16),
            shape((32, 128), F32),
        ],
        in_specs=any_space(21) + vmem(2),
        out_specs=vmem(7),
        scratch_shapes=[
            pltpu.VMEM((16, channels), F32),
            pltpu.VMEM((channels, channels), BF16),
            pltpu.VMEM((channels, channels), BF16),
            pltpu.VMEM(args[18].shape, F32),
            pltpu.VMEM((count, model), F32),
            pltpu.VMEM((count, model), BF16),
            pltpu.VMEM((1, model), F32),
            rows_held, rows_held, weight, weight, weight,
            lead, flat, flat, flat, flat, flat,
            pltpu.VMEM((RING, CHUNK + 8, channels), F32),
            flat, thin,
            flat, flat, thin, thin, thin, thin, lead,
            pltpu.VMEM((LEAD, channels), F32),
            pltpu.VMEM((RING, 8, channels), F32),
            pltpu.VMEM((2, RING, 8, channels), F32),
            pltpu.VMEM((2, channels, channels), BF16),
            pltpu.VMEM(pack, BF16),
            pltpu.VMEM((RING, half, 256), BF16),
            pltpu.VMEM((3, half, 256), BF16),
            pltpu.VMEM((RING, half, 256), BF16),
            pltpu.VMEM((16, channels), F32),
            pltpu.VMEM((4, RING, 8, model // 4), F32),
            pltpu.VMEM((8, model), F32),
            pltpu.VMEM((8, model // 4), F32),
            pltpu.VMEM((RING, hidden, 1024), BF16),
            weight, weight,
            pltpu.VMEM((count, model), F32),
        ]
        + ROW_SCRATCH
        + scatter_scratch(width) * 3
        + scatter_scratch(hidden)[1:]
        + sems(160),
        compiler_params=options(3, 63),
    )(*args)


def call_d(output, g_inputs, grad_branch, grad_gelu, grad_out, packed, gains, grad_gate, grad_up, grad_down):
    width = grad_branch.shape[0]
    hidden = grad_gate.shape[0]
    thin = shape((width, 256), F32)
    wide = shape((256, hidden), F32)
    gain = shape((16, 128), F32)
    square = shape((1, width, width), F32)
    row = shape((1, width), F32)
    return pl.pallas_call(
        kernel_d,
        out_shape=[
            shape(output.shape, BF16), shape(g_inputs.shape, F32), thin, thin, thin, gain, gain,
            wide, wide, wide, square, square, shape((4, width), F32), row, row, row, row,
        ],
        in_specs=vmem(10),
        out_specs=any_space(5) + vmem(12),
        scratch_shapes=[pltpu.SemaphoreType.DMA((5,))],
        compiler_params=pltpu.CompilerParams(vmem_limit_bytes=63 * 2**20),
    )(output, g_inputs, grad_branch, grad_gelu, grad_out, packed, gains, grad_gate, grad_up, grad_down)


def position_masks(resets, z):
    rows = RING * CHUNK
    flags = jnp.pad(resets.reshape(-1).astype(F32), (8, 24), constant_values=1.0)
    window = lax.dynamic_slice(flags, (z * rows,), (rows + 32,))
    keep = 1.0 - window
    first = keep[8:]
    second = first * keep[7:-1]
    third = second * keep[6:-2]
    columns = jnp.stack([window[8:], first, second, third] + [jnp.zeros_like(first)] * 4, axis=1)

    def steps(start):
        held = columns[start : start + rows].reshape(RING, 8, STEPS, 8)
        return held.transpose(0, 2, 1, 3)

    both = jnp.concatenate([steps(0), steps(STEPS)[:, :3]], axis=1)
    return both.reshape(RING, CHUNK + LEAD, 8)


def on_device(
    inputs,
    resets,
    gain_rec,
    w_branch,
    w_gelu,
    conv_weight,
    conv_bias,
    gate_a_weight,
    gate_a_bias,
    gate_x_weight,
    gate_x_bias,
    decay_param,
    w_out,
    gain_mlp,
    w_gate,
    w_up,
    w_down,
    cotangent,
):
    count, _, model = inputs.shape
    z = lax.axis_index("z")
    width = w_branch.shape[1]
    masks = position_masks(resets, z)
    vectors = jnp.concatenate(
        [conv_weight, jnp.stack([conv_bias, gate_a_bias, gate_x_bias, decay_param])], axis=0
    )
    vectors = lax.dynamic_update_slice(jnp.zeros((8, RING * width), F32), vectors, (0, z * width))
    weights = [w.T for w in (w_branch, w_gelu, w_out)] + [w_gate, w_up, w_down]
    gain_rec, gain_mlp = gain_rec.reshape(-1, 128), gain_mlp.reshape(-1, 128)
    (
        mixed, x_placed, seq_normed, seq_mlp, seq_grad,
        w_b_all, w_g_all, w_out_all, w_gate_all, w_up_all, w_down_all,
        branch, conv, rate, admit, decay, scaling, states, gelu_pre, gated, params, gate_a, gate_x,
    ) = call_a(
        inputs.reshape(count, model), cotangent.reshape(count, model), gain_rec, gain_mlp, vectors,
        gate_a_weight, gate_x_weight, masks, *weights,
    )
    g_mixed, seq_mixed, output, up_part, grad_gate, grad_down, gain_part = call_b(
        seq_mlp, seq_grad, w_gate_all, w_up_all, w_down_all, mixed, gain_mlp
    )
    g_inputs, grad_branch, grad_gelu, grad_out, grad_up, packed, gains = call_c(
        seq_mixed, seq_normed, w_b_all, w_g_all, w_out_all, branch, conv, rate, admit, decay, scaling,
        states, gelu_pre, gated, up_part, params, gate_a, gate_x, masks, g_mixed, x_placed, gain_rec, gain_part,
    )
    (
        output, g_inputs, grad_branch, grad_gelu, grad_out, gain_rec, gain_mlp, grad_gate, grad_up, grad_down,
        gate_a, gate_x, taps, *rows,
    ) = call_d(output, g_inputs, grad_branch, grad_gelu, grad_out, packed, gains, grad_gate, grad_up, grad_down)
    conv_bias, bias_a, bias_x, decay = (row.reshape(-1) for row in rows)
    return (
        output.reshape(count, 1, model),
        g_inputs,
        gain_rec.reshape(-1),
        grad_branch.T,
        grad_gelu.T,
        taps,
        conv_bias,
        gate_a,
        bias_a,
        gate_x,
        bias_x,
        decay,
        grad_out.T,
        gain_mlp.reshape(-1),
        grad_gate,
        grad_up,
        grad_down,
    )


def solution(mesh):
    sizes = {"blk": mesh.shape["blk"], "tok": mesh.shape["tok"]}
    grid = Mesh(mesh.devices.reshape(RING, sizes["blk"] // RING, sizes["tok"] // 2, 2), AXES)
    blk, tok = ("z", "y"), ("x", "core")
    in_specs = (
        P(blk, tok, None),
        P(None, tok),
        P(),
        P(tok, blk),
        P(tok, blk),
        P(None, blk),
        P(blk),
        P(blk, None, None),
        P(blk),
        P(blk, None, None),
        P(blk),
        P(blk),
        P(tok, blk),
        P(),
        P(tok, blk),
        P(tok, blk),
        P(tok, blk),
        P(blk, tok, None),
    )
    out_specs = (
        P(blk, tok, None),
        P(blk, tok, None),
        P(),
        P(tok, blk),
        P(tok, blk),
        P(None, blk),
        P(blk),
        P(blk, None, None),
        P(blk),
        P(blk, None, None),
        P(blk),
        P(blk),
        P(tok, blk),
        P(),
        P(tok, blk),
        P(tok, blk),
        P(tok, blk),
    )
    return jax.shard_map(
        on_device, mesh=grid, in_specs=in_specs, out_specs=out_specs, check_vma=False
    )
```
